32 devices in a mesh: grp: 8 (over z, x), row: 4 (over y, core).
Axes of the slice: x: 2, y: 2, z: 4, core: 2. Of those that a mesh axis runs over, the one named last changes fastest.
Arguments:
- item_owner: int32 [32, 1024, 1], P(('grp', 'row')), may hold values from 0 to 3; in each aligned block of 1024 rows (0 to 1023, 1024 to 2047, ..., all dimensions but the last counted through in order) at most 512 rows name the same one
- item_row: int32 [32, 1024], P(('grp', 'row')), may hold values from 0 to 50047
- seg: int32 [32, 1024], P(('grp', 'row')), may hold values from 0 to 7, never falling along the last dimension, each value on 1 to 512 neighbouring positions
- query_slot: int32 [32, 256], P(('grp', 'row')), may hold values from 0 to 1023, as said below
- tgt_owner: int32 [32, 256, 1], P(('grp', 'row')), may hold values from 0 to 3; in each aligned block of 256 rows (0 to 255, 256 to 511, ..., all dimensions but the last counted through in order) at most 128 rows name the same one
- tgt_row: int32 [32, 256], P(('grp', 'row')), may hold values from 0 to 50047
- freq_idx: int32 [32, 256], P(('grp', 'row')), may hold values from 0 to 1023
- valid: int32 [32, 256], P(('grp', 'row')), may hold values from 0 to 1
- logfreq: bfloat16 [1024], replicated, may hold values from -3 to 0
- table_w: float32 [200192, 256], P(('row', 'grp')), may hold values from -6 to 6
- table_m: float32 [200192, 256], P(('row', 'grp')), may hold values from -0.00048828125 to 0.00048828125
- table_a: float32 [200192, 256], P(('row', 'grp')), may hold values from -6 to 6
- attn_w: float32 [256, 1024], P(('grp', 'row')), may hold values from -0.375 to 0.375
- attn_m: float32 [256, 1024], P(('grp', 'row')), may hold values from -0.0390625 to 0.0390625
- attn_a: float32 [256, 1024], P(('grp', 'row')), may hold values from -0.375 to 0.375
- ffn_w: float32 [256, 2048], P(('grp', 'row')), may hold values from -0.375 to 0.375
- ffn_m: float32 [256, 2048], P(('grp', 'row')), may hold values from -0.0390625 to 0.0390625
- ffn_a: float32 [256, 2048], P(('grp', 'row')), may hold values from -0.375 to 0.375
- pos_w: float32 [256, 512], P(('grp', 'row')), may hold values from -6 to 6
- pos_m: float32 [256, 512], P(('grp', 'row')), may hold values from -0.0390625 to 0.0390625
- pos_a: float32 [256, 512], P(('grp', 'row')), may hold values from -6 to 6
- small_w: float32 [256, 11], P(('grp', 'row'))
- small_m: float32 [256, 11], P(('grp', 'row')), may hold values from -0.0390625 to 0.0390625
- small_a: float32 [256, 11], P(('grp', 'row'))
Outputs:
- loss: float32 [], replicated
- table_w_new: float32 [200192, 256], P(('row', 'grp'))
- table_m_new: float32 [200192, 256], P(('row', 'grp'))
- table_a_new: float32 [200192, 256], P(('row', 'grp'))
- table_copy: bfloat16 [200192, 256], P(('row', 'grp'))
- attn_w_new: float32 [256, 1024], P(('grp', 'row'))
- attn_m_new: float32 [256, 1024], P(('grp', 'row'))
- attn_a_new: float32 [256, 1024], P(('grp', 'row'))
- attn_copy: bfloat16 [256, 1024], P(('grp', 'row'))
- ffn_w_new: float32 [256, 2048], P(('grp', 'row'))
- ffn_m_new: float32 [256, 2048], P(('grp', 'row'))
- ffn_a_new: float32 [256, 2048], P(('grp', 'row'))
- ffn_copy: bfloat16 [256, 2048], P(('grp', 'row'))
- pos_w_new: float32 [256, 512], P(('grp', 'row'))
- pos_m_new: float32 [256, 512], P(('grp', 'row'))
- pos_a_new: float32 [256, 512], P(('grp', 'row'))
- pos_copy: bfloat16 [256, 512], P(('grp', 'row'))
- small_w_new: float32 [256, 11], P(('grp', 'row'))
- small_m_new: float32 [256, 11], P(('grp', 'row'))
- small_a_new: float32 [256, 11], P(('grp', 'row'))
- small_copy: bfloat16 [256, 11], P(('grp', 'row'))
The draws below stay inside these ranges and needn't reach their ends.
Inputs may be any that keep to these rules, and one draw needn't show every extreme that they name: `item_owner`: in each packed row no table shard is named by more than 512 slots, and in some rows one shard by exactly 512. `seg`: history numbers of a packed row start at 0 and never fall; a history has 1 to 512 slots. `query_slot`: the 256 slots of a packed row are distinct and rising. `tgt_owner`: in each packed row no table shard is named by more than 128 targets, and in some rows one shard by exactly 128.
All inputs are finite; a program needn't handle non-finite values.
Results may differ from the reference program's by a relative error of at most 0.0085.
The reference program's roundings to bfloat16 on the way count: a program that leaves them out, or rounds other values in their place, can miss the bound.
Values may be sent and summed in bfloat16 or wider, within the bound.
No kernel may reach another device: no remote copies, remote signals or barrier semaphores. Data moves between devices by JAX's collectives and lax.ppermute only.
A program may use at most 256 MiB of HBM per device.

```python
import math
import jax
import jax.numpy as jnp
import numpy as np
from jax import lax

D = 256
HEADS = 8
HEAD = 32
FF = 1024
VOCAB = 200192
MAXLEN = 512
SLOTS = 1024
SEGS = 8
NFREQ = 1024
QRY = 256
OWNERS = 4
NROWS = 32
VS = 50048
QTOTAL = 8192
CAP_S = 512
CAP_Q = 128
NS = 11


def draw_query_slot(key, part):

    def one_row(row_key):
        return jnp.sort(jax.random.permutation(row_key, SLOTS)[:QRY]).astype(jnp.int32)
    return jax.vmap(one_row)(jax.random.split(key, NROWS))


def draw_valid(key, part):
    blocks = jnp.arange(NROWS, dtype=jnp.int32)[:, None]
    thresh = 250 + 500 * blocks // max(NROWS - 1, 1)
    drawn = jax.random.randint(key, (NROWS, QRY), 0, 1000)
    return (drawn < thresh).astype(jnp.int32)


def small_entries(key):
    column = jnp.arange(NS, dtype=jnp.int32)[None, :] * jnp.ones((D, 1), jnp.int32)
    gains = jax.random.uniform(jax.random.fold_in(key, 1), (D, NS), jnp.float32, 0.7, 1.3)
    shifts = 0.5 * jax.random.normal(jax.random.fold_in(key, 2), (D, NS), jnp.float32)
    is_gain = (column == 0) | (column == 2) | (column == 4)
    return jnp.where(is_gain, gains, shifts)


def draw_small_w(key, part):
    return small_entries(jax.random.fold_in(key, 11))


def draw_small_a(key, part):
    return small_entries(jax.random.fold_in(key, 12))


def set_ends(result, own_key, smallest, top_value):
    extent = result.shape
    spot = [jax.random.randint(jax.random.fold_in(own_key, axis), (), 0, extent[axis]) for axis in range(len(extent))]
    result = result.at[tuple(spot)].set(smallest)
    longest = extent.index(max(extent))
    spot[longest] = (spot[longest] + 1) % extent[longest]
    return result.at[tuple(spot)].set(top_value)


def levels(rng, dims, shards, smallest, high):
    def one(position, shards_of):
        heights = jax.random.uniform(jax.random.fold_in(jax.random.fold_in(rng, 6), position), (shards_of,), jnp.float32, smallest / len(shards), high / len(shards))
        return jnp.repeat(jnp.exp(heights), dims[position] // shards_of).reshape((-1,) + (1,) * (len(dims) - position - 1))

    factor_of = one(*shards[0])
    for cut in shards[1:]:
        factor_of = factor_of * one(*cut)
    return factor_of


def split_up(count, total, bound, skew):
    portions = [(1 << 20) // math.isqrt(grade ** skew) + 1 for grade in range(2, count + 1)]
    rest, holding = total - bound - (count - 1), [1] * (count - 1)
    while rest > 0:
        free = [i for i in range(count - 1) if holding[i] < bound]
        whole, left = sum([portions[i] for i in free]), rest
        for i in free:
            more = min(bound - holding[i], max(1, left * portions[i] // whole), rest)
            holding[i] = holding[i] + more
            rest = rest - more
    return np.array([bound] + holding)


def uneven(own_key, count, total, reach, lean):
    if count == 2:
        one = jax.random.randint(own_key, (), max(1, total - reach), min(reach, total - 1) + 1)
        return jnp.stack([one, total - one])
    lengths = jnp.asarray(split_up(count, total, reach, lean), jnp.int32)
    couples = (count - 1) // 2
    source_of, receiver = lengths[1:1 + 2 * couples:2], lengths[2:2 + 2 * couples:2]
    slack = jnp.minimum(source_of - 1, reach - receiver)
    moved = jax.random.randint(jax.random.fold_in(own_key, 1), (couples,), 0, 1 << 20) % (slack + 1)
    lengths = lengths.at[1:1 + 2 * couples:2].set(source_of - moved).at[2:2 + 2 * couples:2].set(receiver + moved)
    return lengths[jax.random.permutation(jax.random.fold_in(own_key, 2), count)]


def assign_block(key, own, number, rows, number_of, top, bound, skew):
    ranking = jax.random.permutation(key, number_of)
    crowded, ordinary = portions_of(number_of, rows * top, bound, skew, True), portions_of(number_of, rows * top, bound, skew, False)
    places = jnp.arange(number_of)

    def named(lengths, rotation):
        used = int((lengths > 0).sum())
        fixed = max(1, used // 4)
        moved = fixed + (places - fixed + rotation * (used - fixed)) % max(1, number_of - fixed)
        return jnp.zeros((number_of,), jnp.int32).at[ranking[jnp.where(places < fixed, places, moved)]].set(jnp.asarray(lengths, jnp.int32))

    lengths = jnp.where(number % 4 == 0, named(crowded, number // 4), named(ordinary, number - number // 4 - 1))
    mixed = jax.random.permutation(jax.random.fold_in(own, 3), number_of)
    giver, receiver = mixed[0:number_of // 2 * 2:2], mixed[1:number_of // 2 * 2:2]
    room = jnp.minimum(lengths[giver] - 1, bound - lengths[receiver]) // 2
    room = jnp.where((giver == ranking[0]) | (receiver == ranking[0]) | (lengths[receiver] == 0), 0, jnp.maximum(room, 0))
    moved = jax.random.randint(jax.random.fold_in(own, 4), (number_of // 2,), 0, 1 << 20) % (room + 1)
    lengths = lengths.at[giver].add(-moved).at[receiver].add(moved)
    items = jnp.searchsorted(jnp.cumsum(lengths), jnp.arange(rows * top), side="right").astype(jnp.int32)
    grid = items.reshape(top, rows).T
    grid = grid[jax.random.permutation(jax.random.fold_in(own, 1), rows)]
    rotation = jax.random.randint(jax.random.fold_in(own, 2), (rows, 1), 0, top)
    return jnp.take_along_axis(grid, (jnp.arange(top)[None, :] + rotation) % top, axis=1)


def portions_of(number_of, total, most, lean, full):
    portions = [(1 << 20) // math.isqrt(rank ** lean) + 1 for rank in range(1, number_of + 1)]
    largest = most if full else min(most, max(-(-total // number_of), total * portions[0] // sum(portions)))
    least = 1 if total - largest >= number_of - 1 else 0
    given, rest = [largest] + [least] * (number_of - 1), total - largest - least * (number_of - 1)
    while rest > 0:
        candidates = [i for i in range(1, number_of) if given[i] < largest] or [i for i in range(1, number_of) if given[i] < most]
        pool, left = sum([portions[i] for i in candidates]), rest
        for i in candidates:
            more = min(most - given[i], max(1, left * portions[i] // pool), rest)
            given[i] = given[i] + more
            rest = rest - more
    return np.array(given)


def centred(rng, extent, width, limit, cuts=(), kind=jnp.bfloat16):
    result = width * jax.random.normal(rng, extent, jnp.float32)
    if cuts:
        result = result * levels(rng, extent, cuts, -0.22, 0.18)
    return jnp.clip(result, -limit, limit).astype(kind)


def setup_inputs(seed: int = 0) -> dict:
    key_of = jax.random.split(jax.random.key(seed), 25)
    item_owner_keys = jax.random.split(jax.random.fold_in(key_of[0], 1), NROWS * SLOTS // SLOTS)
    item_owner_turns = jax.random.permutation(jax.random.fold_in(key_of[0], 3), NROWS * SLOTS // SLOTS)
    item_owner = jax.vmap(lambda own, number: assign_block(jax.random.fold_in(key_of[0], 2), own, number, SLOTS, OWNERS, 1, CAP_S, 2))(item_owner_keys, item_owner_turns).reshape((NROWS, SLOTS, 1))
    item_row = set_ends(jax.random.randint(key_of[1], (NROWS, SLOTS), 0, VS), jax.random.fold_in(key_of[1], 1), 0, VS - 1).astype(jnp.int32)
    seg = jax.vmap(lambda own: jnp.searchsorted(jnp.cumsum(uneven(own, SEGS, SLOTS, MAXLEN, 2)), jnp.arange(SLOTS), side="right"))(jax.random.split(key_of[2], NROWS)).reshape((NROWS, SLOTS)).astype(jnp.int32)
    query_slot = draw_query_slot(jax.random.fold_in(key_of[24], 71), 0)
    tgt_owner_keys = jax.random.split(jax.random.fold_in(key_of[4], 1), NROWS * QRY // QRY)
    tgt_owner_turns = jax.random.permutation(jax.random.fold_in(key_of[4], 3), NROWS * QRY // QRY)
    tgt_owner = jax.vmap(lambda own, number: assign_block(jax.random.fold_in(key_of[4], 2), own, number, QRY, OWNERS, 1, CAP_Q, 2))(tgt_owner_keys, tgt_owner_turns).reshape((NROWS, QRY, 1))
    tgt_row = set_ends(jax.random.randint(key_of[5], (NROWS, QRY), 0, VS), jax.random.fold_in(key_of[5], 1), 0, VS - 1).astype(jnp.int32)
    freq_idx = set_ends(jax.random.randint(key_of[6], (NROWS, QRY), 0, NFREQ), jax.random.fold_in(key_of[6], 1), 0, NFREQ - 1).astype(jnp.int32)
    valid = draw_valid(jax.random.fold_in(key_of[24], 71), 0)
    logfreq = jnp.clip(jax.random.uniform(key_of[8], (NFREQ,), jnp.float32, -3.0, 0.0), -3.0, 0.0).astype(jnp.bfloat16)
    table_w = centred(key_of[9], (VOCAB, D), 1.0, 6.0, ((0, 32),), jnp.float32)
    table_m = centred(key_of[10], (VOCAB, D), (0.25 * QTOTAL ** -1), 0.00048828125, ((0, 32),), jnp.float32)
    table_a = centred(key_of[11], (VOCAB, D), 1.0, 6.0, ((0, 32),), jnp.float32)
    attn_w = centred(key_of[12], (D, 4 * D), D ** -0.5, 0.375, ((0, 32),), jnp.float32)
    attn_m = centred(key_of[13], (D, 4 * D), (0.25 * QTOTAL ** -0.5), 0.0390625, ((0, 32),), jnp.float32)
    attn_a = centred(key_of[14], (D, 4 * D), D ** -0.5, 0.375, ((0, 32),), jnp.float32)
    ffn_w = centred(key_of[15], (D, 2 * FF), D ** -0.5, 0.375, ((0, 32),), jnp.float32)
    ffn_m = centred(key_of[16], (D, 2 * FF), (0.25 * QTOTAL ** -0.5), 0.0390625, ((0, 32),), jnp.float32)
    ffn_a = centred(key_of[17], (D, 2 * FF), D ** -0.5, 0.375, ((0, 32),), jnp.float32)
    pos_w = centred(key_of[18], (D, MAXLEN), 0.5, 6.0, ((0, 32),), jnp.float32)
    pos_m = centred(key_of[19], (D, MAXLEN), (0.25 * QTOTAL ** -0.5), 0.0390625, ((0, 32),), jnp.float32)
    pos_a = centred(key_of[20], (D, MAXLEN), 0.5, 6.0, ((0, 32),), jnp.float32)
    small_w = draw_small_w(jax.random.fold_in(key_of[24], 71), 0)
    small_m = centred(key_of[22], (D, NS), (0.25 * QTOTAL ** -0.5), 0.0390625, ((0, 32),), jnp.float32)
    small_a = draw_small_a(jax.random.fold_in(key_of[24], 71), 0)
    return dict(item_owner=item_owner, item_row=item_row, seg=seg, query_slot=query_slot, tgt_owner=tgt_owner, tgt_row=tgt_row, freq_idx=freq_idx, valid=valid, logfreq=logfreq, table_w=table_w, table_m=table_m, table_a=table_a, attn_w=attn_w, attn_m=attn_m, attn_a=attn_a, ffn_w=ffn_w, ffn_m=ffn_m, ffn_a=ffn_a, pos_w=pos_w, pos_m=pos_m, pos_a=pos_a, small_w=small_w, small_m=small_m, small_a=small_a)


@jax.custom_vjp
def low(v):
    return lax.optimization_barrier(v.astype(jnp.bfloat16)).astype(jnp.float32)

@jax.custom_vjp
def low_back(v):
    return v

def low_keep(v):
    return (low(v), None)

def low_pass(kept, grad):
    return (grad,)

def back_keep(v):
    return (v, None)

def back_low(kept, grad):
    return (low(grad),)
low.defvjp(low_keep, low_pass)
low_back.defvjp(back_keep, back_low)
norm_eps = 1e-05
score_scale = 0.125
logit_scale = 0.125
momentum_rate = 0.5
average_rate = 0.5
highest = lax.Precision.HIGHEST

def matmul(left, right):
    return jnp.dot(left, right, precision=highest, preferred_element_type=jnp.float32)

def normed(values, gain, shift):
    centre = values - lax.optimization_barrier(jnp.mean(values, axis=-1, keepdims=True))
    spread = lax.optimization_barrier(jnp.mean(centre * centre, axis=-1, keepdims=True))
    return centre * lax.rsqrt(spread + norm_eps) * gain + shift

def positions(seg_row):
    slot_index = jnp.arange(seg_row.shape[0], dtype=jnp.int32)
    before = lax.optimization_barrier(jnp.sum((seg_row[None, :] < seg_row[:, None]).astype(jnp.int32), axis=1))
    return (slot_index - before, slot_index)

def row_forward(weights, row_items, seg_row, row_slots):
    table, attn, ffn, pos, small = weights
    places, slot_index = positions(seg_row)
    first = table[row_items] + pos.T[places]
    normed_a = low(normed(first, small[:, 0], small[:, 1]))
    joined = low(low_back(matmul(normed_a, attn[:, :3 * D])))
    heads_q = joined[:, :D].reshape(SLOTS, HEADS, HEAD)
    heads_k = joined[:, D:2 * D].reshape(SLOTS, HEADS, HEAD)
    heads_v = joined[:, 2 * D:].reshape(SLOTS, HEADS, HEAD)
    scores = low_back(jnp.einsum('qhd,khd->hqk', heads_q, heads_k, precision=highest) * score_scale)
    allowed = (seg_row[:, None] == seg_row[None, :]) & (slot_index[:, None] >= slot_index[None, :])
    scores = jnp.where(allowed[None], scores, -1e+30)
    probs = low(jax.nn.softmax(scores, axis=-1))
    mixed = jnp.einsum('hqk,khd->qhd', probs, heads_v, precision=highest).reshape(SLOTS, D)
    mixed = low(low_back(mixed))
    second = first + low_back(matmul(mixed, attn[:, 3 * D:]))
    normed_b = low(normed(second, small[:, 2], small[:, 3]))
    hidden = low_back(matmul(normed_b, ffn[:, :FF]) + small[:, 7:].T.reshape(FF))
    active = low(jax.nn.relu(hidden))
    third = second + low_back(matmul(active, ffn[:, FF:].T) + small[:, 6])
    return low(normed(third, small[:, 4], small[:, 5])[row_slots])

def total_loss(table, attn, ffn, pos, small, item_ids, seg, query_slot, target_ids, corr, weight):
    table_low = low(table)
    weights = (table_low, low(attn), low(ffn), low(pos), low(small))

    def one_row(packed):
        return row_forward(weights, packed[0], packed[1], packed[2])
    queries = lax.map(jax.checkpoint(one_row), (item_ids, seg, query_slot))
    targets = table_low[target_ids.reshape(-1)]
    starts = jnp.arange(NROWS, dtype=jnp.int32) * QRY

    def one_block(packed):
        rows_h, rows_w, start = packed
        logits = low_back(matmul(rows_h, targets.T) * logit_scale) - corr[None, :]
        row_top = lax.optimization_barrier(jnp.max(logits, axis=1, keepdims=True))
        log_total = row_top[:, 0] + jnp.log(lax.optimization_barrier(jnp.sum(jnp.exp(logits - row_top), axis=1)))
        own_cols = (start + jnp.arange(QRY, dtype=jnp.int32))[:, None]
        own = jnp.take_along_axis(logits, own_cols, axis=1)[:, 0]
        return jnp.sum(rows_w * (log_total - own))
    return jnp.sum(lax.map(jax.checkpoint(one_block), (queries, weight, starts)))

def advance(weight, moment, average, grad, rate):
    moment_new = momentum_rate * moment + grad
    weight_new = weight - rate * (grad + momentum_rate * moment_new)
    average_new = average_rate * average + (1.0 - average_rate) * weight_new
    return (weight_new, moment_new, average_new, weight_new.astype(jnp.bfloat16))

def reference(item_owner, item_row, seg, query_slot, tgt_owner, tgt_row, freq_idx, valid, logfreq, table_w, table_m, table_a, attn_w, attn_m, attn_a, ffn_w, ffn_m, ffn_a, pos_w, pos_m, pos_a, small_w, small_m, small_a):
    item_ids = (item_owner[:, :, 0] * VS + item_row).astype(jnp.int32)
    target_ids = (tgt_owner[:, :, 0] * VS + tgt_row).astype(jnp.int32)
    valid_total = jnp.maximum(jnp.sum(valid).astype(jnp.float32), 1.0)
    weight = valid.astype(jnp.float32) / valid_total
    corr = logfreq.astype(jnp.float32)[freq_idx.reshape(-1)]

    def loss_of(table, attn, ffn, pos, small):
        return total_loss(table, attn, ffn, pos, small, item_ids, seg, query_slot, target_ids, corr, weight)
    loss, back = jax.vjp(loss_of, table_w, attn_w, ffn_w, pos_w, small_w)
    grads = back(jnp.ones_like(loss))
    rate_table = 4.0 * QTOTAL
    rate_dense = 0.25 * math.sqrt(QTOTAL)
    rate_place = 2.0 * math.sqrt(QTOTAL)
    table_out = advance(table_w, table_m, table_a, grads[0], rate_table)
    attn_out = advance(attn_w, attn_m, attn_a, grads[1], rate_dense)
    ffn_out = advance(ffn_w, ffn_m, ffn_a, grads[2], rate_dense)
    pos_out = advance(pos_w, pos_m, pos_a, grads[3], rate_place)
    small_out = advance(small_w, small_m, small_a, grads[4], rate_dense)
    return (loss, table_out[0], table_out[1], table_out[2], table_out[3], attn_out[0], attn_out[1], attn_out[2], attn_out[3], ffn_out[0], ffn_out[1], ffn_out[2], ffn_out[3], pos_out[0], pos_out[1], pos_out[2], pos_out[3], small_out[0], small_out[1], small_out[2], small_out[3])
```

```python
import functools
import math

import jax
import jax.numpy as jnp
from jax import lax
from jax.experimental import pallas as pl
from jax.experimental.pallas import tpu as pltpu
from jax.sharding import PartitionSpec as P

D = 256
HEADS = 8
HEAD = 32
FF = 1024
QKV = 3 * D
ATTN = 4 * D
DOWN = ATTN + FF
TABLES = ATTN + 2 * FF
NSMALL = 11
SMALL = 128
META = 16

norm_eps = 1e-05
score_scale = 0.125
logit_scale = 0.125
momentum_rate = 0.5
average_rate = 0.5
negative = -1e30
bf16 = jnp.bfloat16
f32 = jnp.float32
i32 = jnp.int32


def iota(shape, dim, dtype=i32):
    return lax.broadcasted_iota(i32, shape, dim).astype(dtype)


def hot(condition):
    return jnp.where(condition, 1.0, 0.0).astype(bf16)


def dot(left, right):
    return lax.dot_general(left, right, (((1,), (0,)), ((), ())), preferred_element_type=f32)


def dot_cols(left, right):
    return lax.dot_general(left, right, (((1,), (1,)), ((), ())), preferred_element_type=f32)


def split(value):
    high = value.astype(bf16)
    rest = value - high.astype(f32)
    middle = rest.astype(bf16)
    low = (rest - middle.astype(f32)).astype(bf16)
    return (high, middle, low)


def run(body, outs, args, smem=(), scratch=(), flops=0, moved=0, vmem=56):
    return pl.pallas_call(
        body,
        out_shape=[jax.ShapeDtypeStruct(shape, dtype) for shape, dtype in outs],
        in_specs=[
            pl.BlockSpec(memory_space=pltpu.SMEM if i in smem else pltpu.VMEM)
            for i in range(len(args))
        ],
        out_specs=[pl.BlockSpec(memory_space=pltpu.VMEM) for unused in outs],
        scratch_shapes=list(scratch),
        compiler_params=pltpu.CompilerParams(vmem_limit_bytes=vmem << 20),
        cost_estimate=pl.CostEstimate(flops=flops, bytes_accessed=moved, transcendentals=0),
    )(*args)


def route_kernel(cap, dest_ref, local_ref, valid_ref, wanted_ref, place_ref, column_ref, rank_ref):
    devices, width = wanted_ref.shape
    asks = dest_ref.shape[1]
    dest = dest_ref[...]
    local = local_ref[...]
    named = jnp.where(iota((devices, asks), 0) == dest, 1.0, 0.0)
    earlier = hot(iota((asks, asks), 0) < iota((asks, asks), 1))
    before = dot(named.astype(bf16), earlier)
    rank = jnp.sum(named * before, axis=0, keepdims=True)
    count = jnp.sum(named, axis=1, keepdims=True)
    spot = iota((width, asks), 0, f32)
    at_spot = hot((spot == rank) & (spot < cap))
    high = (local >> 6).astype(f32)
    low = (local & 63).astype(f32)
    ids = dot_cols((named * high).astype(bf16), at_spot) * 64.0 + dot_cols(
        (named * low).astype(bf16), at_spot
    )
    lane = iota((devices, width), 1, f32)
    most = jnp.max(count, axis=0, keepdims=True)
    flags = jnp.sum(valid_ref[...].astype(f32), axis=1, keepdims=True)
    ids = jnp.where(lane < jnp.minimum(count, cap), ids, -1.0)
    ids = jnp.where(lane == cap, count, ids)
    ids = jnp.where(lane == cap + 1, most, ids)
    ids = jnp.where(lane == cap + 2, flags, ids)
    wanted_ref[...] = ids.astype(i32)
    place = jnp.where(rank < cap, dest.astype(f32) * cap + rank, -1.0)
    place_ref[...] = place.astype(i32)
    rank_ref[...] = rank.astype(i32)
    column_ref[...] = jnp.broadcast_to(place, (128, asks)).T[:, :1].astype(i32)


def lookup_kernel(cap, asked_ref, table_ref, rows_ref, held):
    devices = asked_ref.shape[0]
    step = 512

    def clear(i, carry):
        held[pl.ds(pl.multiple_of(i * step, step), step), :] = jnp.zeros((step, D), f32)
        return carry

    lax.fori_loop(0, held.shape[0] // step, clear, 0)

    def one_device(n, carry):
        count = jnp.minimum(asked_ref[n, cap], cap)

        def eight(k, carry):
            for j in range(8):
                row = jnp.maximum(asked_ref[n, k * 8 + j], 0)
                held[pl.ds(n * cap + k * 8 + j, 1), :] = table_ref[pl.ds(row, 1), :]
            return carry

        lax.fori_loop(0, (count + 7) // 8, eight, 0)
        return carry

    lax.fori_loop(0, devices, one_device, 0)

    def low(i, carry):
        part = pl.ds(pl.multiple_of(i * step, step), step)
        rows_ref[part, :] = held[part, :].astype(bf16)
        return carry

    lax.fori_loop(0, held.shape[0] // step, low, 0)


def extract_kernel(found_ref, column_ref, freq_ref, logfreq_ref, item_ref, target_ref):
    slots = item_ref.shape[0]
    queries = freq_ref.shape[1]
    block = 256
    total = found_ref.shape[0]

    def rows_of(begin):
        place = column_ref[pl.ds(begin, block), :]
        return dot(hot(place == iota((block, total), 1)), found_ref[...]).astype(bf16)

    def items(i, carry):
        begin = pl.multiple_of(i * block, block)
        item_ref[pl.ds(begin, block), :] = rows_of(begin)
        return carry

    lax.fori_loop(0, slots // block, items, 0)
    target_ref[:queries, :] = rows_of(slots)
    entries = logfreq_ref.shape[1]
    corr = dot(logfreq_ref[...], hot(iota((entries, queries), 0) == freq_ref[...]))
    target_ref[queries:, :] = jnp.broadcast_to(corr, (META, queries)).astype(bf16)


def centred(values):
    centre = values - jnp.mean(values, axis=-1, keepdims=True)
    spread = jnp.mean(centre * centre, axis=-1, keepdims=True)
    scale = lax.rsqrt(spread + norm_eps)
    return (centre * scale, scale)


def norm_back(grad, unit, scale, gain):
    inner = grad * gain
    grad_in = scale * (
        inner
        - jnp.mean(inner, axis=-1, keepdims=True)
        - unit * jnp.mean(inner * unit, axis=-1, keepdims=True)
    )
    return (
        grad_in,
        jnp.sum(grad * unit, axis=0, keepdims=True),
        jnp.sum(grad, axis=0, keepdims=True),
    )


def places_of(seg):
    slots = seg.shape[0]
    lane = iota((slots, 128), 1)
    below = jnp.sum(jnp.where(seg < lane, 1.0, 0.0), axis=0, keepdims=True)
    start = jnp.sum(jnp.where(seg == lane, below, 0.0), axis=1, keepdims=True)
    return iota((slots, 1), 0) - start.astype(i32)


def small_rows(dense_ref, begin):
    return dense_ref[:, begin:].astype(f32).T


def mask_bias(seg, slots_q):
    shape = (seg.shape[0], slots_q.shape[1])
    slot = iota(shape, 0)
    wide = seg.astype(f32)
    seg_q = jnp.sum(jnp.where(slot == slots_q, wide, 0.0), axis=0, keepdims=True)
    return jnp.where((wide == seg_q) & (slot <= slots_q), 0.0, negative)


def forward_kernel(
    item_ref,
    seg_ref,
    slot_row_ref,
    slot_col_ref,
    dense_ref,
    query_ref,
    first_ref,
    normed_ref,
    kv_ref,
    q_ref,
    mixed_ref,
    lse_ref,
    second_ref,
    normed_b_ref,
    active_ref,
    third_ref,
    bias_ref,
    value_t_ref,
    mixed_t_ref,
):
    slots = item_ref.shape[0]
    queries = slot_row_ref.shape[1]
    small_at = dense_ref.shape[1] - SMALL
    pos = dense_ref[:, TABLES:small_at]
    rows = small_rows(dense_ref, small_at)
    seg = seg_ref[...]
    pos_hot = hot(places_of(seg) == iota((slots, small_at - TABLES), 1))
    first = item_ref[...].astype(f32) + dot_cols(pos_hot, pos)
    first_ref[...] = first
    unit, unused = centred(first)
    normed = (unit * rows[0:1] + rows[1:2]).astype(bf16)
    normed_ref[...] = normed
    kv_ref[...] = dot(normed, dense_ref[:, D:QKV]).astype(bf16)
    choose = hot(slot_col_ref[...] == iota((queries, slots), 1))
    normed_q = dot(choose, normed).astype(bf16)
    q_ref[...] = dot(normed_q, dense_ref[:, :D]).astype(bf16)
    first_q = dot(choose, item_ref[...]) + dot_cols(dot(choose, pos_hot).astype(bf16), pos)
    bias_ref[...] = mask_bias(seg, slot_row_ref[...])
    value_t_ref[...] = kv_ref[:, D:].T

    def one_head(h, carry):
        own = iota((1, D), 1) // HEAD == h
        q_own = jnp.where(own, q_ref[...].astype(f32) * score_scale, 0.0).astype(bf16)
        scores = dot_cols(kv_ref[:, :D], q_own) + bias_ref[...]
        top = jnp.max(scores, axis=0, keepdims=True)
        weight = jnp.exp(scores - top)
        total = jnp.sum(weight, axis=0, keepdims=True)
        lse_ref[pl.ds(h, 1), :] = top + jnp.log(total)
        part = pl.ds(pl.multiple_of(h * HEAD, HEAD), HEAD)
        mixed_t_ref[part, :] = dot(value_t_ref[part, :], (weight * (1.0 / total)).astype(bf16))
        return carry

    lax.fori_loop(0, HEADS, one_head, 0)
    mixed = mixed_t_ref[...].T.astype(bf16)
    mixed_ref[...] = mixed
    second = first_q + dot(mixed, dense_ref[:, QKV:ATTN])
    second_ref[...] = second
    unit, unused = centred(second)
    normed_b = (unit * rows[2:3] + rows[3:4]).astype(bf16)
    normed_b_ref[...] = normed_b
    up_bias = jnp.concatenate([rows[7 + k : 8 + k] for k in range(FF // D)], axis=1)
    hidden = dot(normed_b, dense_ref[:, ATTN:DOWN]) + up_bias
    active = jnp.maximum(hidden, 0.0).astype(bf16)
    active_ref[...] = active
    third = second + dot_cols(active, dense_ref[:, DOWN:TABLES]) + rows[6:7]
    third_ref[...] = third
    unit, unused = centred(third)
    query_ref[...] = (unit * rows[4:5] + rows[5:6]).astype(bf16)


def totals_kernel(query_ref, target_ref, out_ref, target_t_ref, corr_ref):
    owners, height, unused = out_ref.shape
    queries = query_ref.shape[0] // owners
    grps = target_ref.shape[0]
    corr_rows = jnp.concatenate(
        [target_ref[g, queries : queries + 1, :].astype(f32) for g in range(grps)]
        + [jnp.zeros((128 - grps, queries), f32)],
        axis=0,
    )
    corr_ref[...] = corr_rows.T

    for g in range(grps):
        target_t_ref[:, g * queries : (g + 1) * queries] = target_ref[g, :queries, :].T

    def one_owner(r, carry):
        begin = pl.multiple_of(r * queries, queries)
        query = (query_ref[pl.ds(begin, queries), :].astype(f32) * logit_scale).astype(bf16)
        logits = [
            dot_cols(target_ref[g, :queries, :], query) - corr_ref[:, g : g + 1]
            for g in range(grps)
        ]
        top = functools.reduce(jnp.maximum, [jnp.max(x, axis=0, keepdims=True) for x in logits])
        total = jnp.zeros((1, queries), f32)
        mixed = jnp.zeros((D, queries), f32)
        for g in range(grps):
            weight = jnp.exp(logits[g] - top)
            total = total + jnp.sum(weight, axis=0, keepdims=True)
            mixed = mixed + dot(
                target_t_ref[:, g * queries : (g + 1) * queries], weight.astype(bf16)
            )
        out_ref[r, :D, :] = mixed.astype(bf16)
        pieces = split(top) + split(total)
        fill = jnp.zeros((META - len(pieces), queries), f32)
        out_ref[r, D:, :] = jnp.concatenate(
            [x.astype(f32) for x in pieces] + [fill], axis=0
        ).astype(bf16)
        return carry

    lax.fori_loop(0, owners, one_owner, 0)


def backward_kernel(
    parts_ref,
    target_ref,
    valid_ref,
    total_ref,
    seg_ref,
    slot_row_ref,
    slot_col_ref,
    dense_ref,
    query_ref,
    first_ref,
    normed_ref,
    kv_ref,
    q_ref,
    mixed_ref,
    lse_ref,
    second_ref,
    normed_b_ref,
    active_ref,
    third_ref,
    grad_first_ref,
    grads_ref,
    sums_ref,
    bias_ref,
    key_t_ref,
    grad_q_t_ref,
    grad_o_ref,
    probs_ref,
    grad_s_ref,
    stack_ref,
    p_ref,
    dp_ref,
):
    owners = parts_ref.shape[0]
    queries = slot_row_ref.shape[1]
    slots = seg_ref.shape[0]
    small_at = dense_ref.shape[1] - SMALL
    rows = small_rows(dense_ref, small_at)
    seg = seg_ref[...]

    tops, totals = [], []
    for r in range(owners):
        tail = parts_ref[r, D:, :].astype(f32)
        tops.append(tail[0:1] + tail[1:2] + tail[2:3])
        totals.append(tail[3:4] + tail[4:5] + tail[5:6])
    top = functools.reduce(jnp.maximum, tops)
    scales = [jnp.exp(x - top) for x in tops]
    total = sum(x * y for x, y in zip(scales, totals))
    log_total = top + jnp.log(total)
    weight = valid_ref[...].astype(f32) / total_ref[0, 0]
    mean_t = jnp.zeros((D, queries), f32)
    for r in range(owners):
        mean_t = mean_t + parts_ref[r, :D, :].astype(f32) * (scales[r] / total)
    target = target_ref[:queries, :].astype(f32)
    grad_query = ((mean_t - target.T) * (weight * logit_scale)).T
    own = jnp.sum((query_ref[...].astype(f32) * target).T, axis=0, keepdims=True) * logit_scale
    own = own - target_ref[queries : queries + 1, :].astype(f32)
    loss = jnp.sum(weight * (log_total - own), axis=1, keepdims=True)
    sums_ref[...] = jnp.concatenate(
        [log_total, weight, jnp.broadcast_to(loss, (1, queries)), jnp.zeros((5, queries), f32)],
        axis=0,
    )

    unit, scale = centred(third_ref[...])
    grad_third, gain_f, shift_f = norm_back(grad_query, unit, scale, rows[4:5])
    grad_f = grad_third.astype(bf16)
    active = active_ref[...]
    grads_ref[:, DOWN:TABLES] = dot(grad_f.T, active).astype(bf16)
    down_bias = jnp.sum(grad_f.astype(f32), axis=0, keepdims=True)
    grad_active = dot(grad_f, dense_ref[:, DOWN:TABLES])
    grad_hidden = jnp.where(active.astype(f32) > 0.0, grad_active, 0.0).astype(bf16)
    grads_ref[:, ATTN:DOWN] = dot(normed_b_ref[...].T, grad_hidden).astype(bf16)
    up_bias = jnp.sum(grad_hidden.astype(f32), axis=0, keepdims=True)
    grad_b = dot_cols(grad_hidden, dense_ref[:, ATTN:DOWN])
    unit, scale = centred(second_ref[...])
    through, gain_b, shift_b = norm_back(grad_b, unit, scale, rows[2:3])
    grad_second = grad_third + through
    grad_y = grad_second.astype(bf16)
    grads_ref[:, QKV:ATTN] = dot(mixed_ref[...].T, grad_y).astype(bf16)
    grad_o_ref[...] = dot_cols(grad_y, dense_ref[:, QKV:ATTN]).astype(bf16)

    bias_ref[...] = mask_bias(seg, slot_row_ref[...])
    key_t_ref[...] = kv_ref[:, :D].T

    def one_head(h, carry):
        own = iota((1, D), 1) // HEAD == h
        q_own = jnp.where(own, q_ref[...].astype(f32), 0.0)
        stack_ref[0, pl.ds(pl.multiple_of(h * queries, queries), queries), :] = q_own.astype(bf16)
        o_own = jnp.where(own, grad_o_ref[...].astype(f32), 0.0).astype(bf16)
        stack_ref[1, pl.ds(pl.multiple_of(h * queries, queries), queries), :] = o_own
        scores = dot_cols(kv_ref[:, :D], (q_own * score_scale).astype(bf16)) + bias_ref[...]
        probs = jnp.exp(scores - lse_ref[pl.ds(h, 1), :])
        p_ref[...] = probs
        columns = pl.ds(pl.multiple_of(h * queries, queries), queries)
        probs_ref[:, columns] = probs.astype(bf16)
        grad_p = dot_cols(kv_ref[:, D:], o_own)
        dp_ref[...] = grad_p
        inner = jnp.sum(p_ref[...] * grad_p, axis=0, keepdims=True)
        grad_s = (p_ref[...] * (dp_ref[...] - inner)).astype(bf16)
        grad_s_ref[:, columns] = grad_s
        part = pl.ds(pl.multiple_of(h * HEAD, HEAD), HEAD)
        grad_q_t_ref[part, :] = dot(key_t_ref[part, :], grad_s)
        return carry

    lax.fori_loop(0, HEADS, one_head, 0)
    grad_q = (grad_q_t_ref[...].T * score_scale).astype(bf16)
    grad_k = (dot(grad_s_ref[...], stack_ref[0]) * score_scale).astype(bf16)
    grad_v = dot(probs_ref[...], stack_ref[1]).astype(bf16)
    normed = normed_ref[...]
    normed_t = normed.T
    grads_ref[:, D : 2 * D] = dot(normed_t, grad_k).astype(bf16)
    grads_ref[:, 2 * D : QKV] = dot(normed_t, grad_v).astype(bf16)
    spread = hot(iota((slots, queries), 0) == slot_row_ref[...])
    grad_q_all = dot(spread, grad_q).astype(bf16)
    grads_ref[:, :D] = dot(normed_t, grad_q_all).astype(bf16)
    grad_a = (
        dot_cols(grad_q_all, dense_ref[:, :D])
        + dot_cols(grad_k, dense_ref[:, D : 2 * D])
        + dot_cols(grad_v, dense_ref[:, 2 * D : QKV])
    )
    unit, scale = centred(first_ref[...])
    through, gain_a, shift_a = norm_back(grad_a, unit, scale, rows[0:1])
    high, middle, low = split(grad_second)
    grad_first = through + ((dot(spread, high) + dot(spread, middle)) + dot(spread, low))
    grad_first_ref[...] = grad_first.astype(bf16)
    pos_hot = hot(places_of(seg) == iota((slots, small_at - TABLES), 1))
    high, middle, low = split(grad_first)
    grads_ref[:, TABLES:small_at] = (dot(high.T, pos_hot) + dot(middle.T, pos_hot)).astype(bf16)
    columns = jnp.concatenate(
        [gain_a, shift_a, gain_b, shift_b, gain_f, shift_f, down_bias]
        + [up_bias[:, k * D : (k + 1) * D] for k in range(FF // D)]
        + [jnp.zeros((SMALL - NSMALL, D), f32)],
        axis=0,
    )
    grads_ref[:, small_at:] = columns.T.astype(bf16)


def target_grad_kernel(
    owners, where_ref, query_ref, target_ref, sums_ref, out_ref, corr_ref
):
    grps = target_ref.shape[0]
    queries = query_ref.shape[0] // owners
    corr_rows = jnp.concatenate(
        [target_ref[g, queries : queries + 1, :].astype(f32) for g in range(grps)]
        + [jnp.zeros((128 - grps, queries), f32)],
        axis=0,
    )
    corr_ref[...] = corr_rows.T
    same = jnp.where(iota((queries, queries), 0) == iota((queries, queries), 1), 1.0, 0.0)
    own_g, own_r = where_ref[0, 0], where_ref[0, 1]
    loss = functools.reduce(jnp.add, [sums_ref[8 * r + 2 : 8 * r + 3, :] for r in range(owners)])
    pieces = split(loss)
    tail = jnp.concatenate(
        [x.astype(f32) for x in pieces] + [jnp.zeros((META - len(pieces), queries), f32)], axis=0
    ).astype(bf16)
    for g in range(grps):
        target = target_ref[g, :queries, :]
        grad = jnp.zeros((queries, D), f32)
        for r in range(owners):
            query = query_ref[r * queries : (r + 1) * queries, :]
            logits = dot_cols(target, query) * logit_scale - corr_ref[:, g : g + 1]
            hit = jnp.where((own_g == g) & (own_r == r), 1.0, 0.0)
            coeff = sums_ref[8 * r + 1 : 8 * r + 2, :] * (
                jnp.exp(logits - sums_ref[8 * r : 8 * r + 1, :]) - hit * same
            )
            grad = grad + dot(coeff.astype(bf16), query)
        out_ref[g, :queries, :] = grad.astype(bf16)
        out_ref[g, queries:, :] = tail


def send_kernel(grad_first_ref, parts_ref, place_ref, sent_ref, both_ref):
    grps, height, unused = parts_ref.shape
    slots = grad_first_ref.shape[0]
    queries = height - META
    both_ref[:slots, :] = grad_first_ref[...]
    total = parts_ref[0, :queries, :].astype(f32)
    for g in range(1, grps):
        total = total + parts_ref[g, :queries, :].astype(f32)
    both_ref[slots:, :] = (total * logit_scale).astype(bf16)
    block = 256
    asks = both_ref.shape[0]

    def one_block(i, carry):
        begin = pl.multiple_of(i * block, block)
        spread = hot(place_ref[...] - begin == iota((block, asks), 0))
        sent_ref[pl.ds(begin, block), :] = dot(spread, both_ref[...]).astype(bf16)
        return carry

    lax.fori_loop(0, sent_ref.shape[0] // block, one_block, 0)


def advance(weight, moment, average, grad, rate):
    moment_new = momentum_rate * moment + grad
    weight_new = weight - rate * (grad + momentum_rate * moment_new)
    average_new = average_rate * average + (1.0 - average_rate) * weight_new
    return (weight_new, moment_new, average_new, weight_new.astype(bf16))


def update_kernel(
    rate, ids_ref, recv_ref, w_ref, m_ref, a_ref, w_out_ref, m_out_ref, a_out_ref, copy_ref
):
    rows = w_ref.shape[0]
    base = pl.program_id(0) * rows
    spread = hot(ids_ref[...] - base == iota((rows, ids_ref.shape[1]), 0))
    grad = dot(spread, recv_ref[...])
    new = advance(w_ref[...], m_ref[...], a_ref[...], grad, rate)
    w_out_ref[...], m_out_ref[...], a_out_ref[...], copy_ref[...] = new


def update_table(ids, recv, table_w, table_m, table_a, rate):
    rows = 368
    count = table_w.shape[0]
    block = pl.BlockSpec((rows, D), lambda i: (i, 0))
    whole = [pl.BlockSpec(memory_space=pltpu.VMEM)] * 2
    return tuple(
        pl.pallas_call(
            functools.partial(update_kernel, rate),
            grid=(pl.cdiv(count, rows),),
            in_specs=whole + [block] * 3,
            out_specs=[block] * 4,
            out_shape=[jax.ShapeDtypeStruct((count, D), f32)] * 3
            + [jax.ShapeDtypeStruct((count, D), bf16)],
            compiler_params=pltpu.CompilerParams(vmem_limit_bytes=56 << 20),
            cost_estimate=pl.CostEstimate(
                flops=2 * count * recv.shape[0] * D, bytes_accessed=26 * count * D, transcendentals=0
            ),
        )(ids, recv, table_w, table_m, table_a)
    )


def everyone(values):
    return lax.all_to_all(values, ("grp", "row"), split_axis=0, concat_axis=0, tiled=True)


def local(
    item_owner,
    item_row,
    seg,
    query_slot,
    tgt_owner,
    tgt_row,
    freq_idx,
    valid,
    logfreq,
    table_w,
    table_m,
    table_a,
    attn_w,
    attn_m,
    attn_a,
    ffn_w,
    ffn_m,
    ffn_a,
    pos_w,
    pos_m,
    pos_a,
    small_w,
    small_m,
    small_a,
):
    owners = lax.axis_size("row")
    grps = lax.axis_size("grp")
    devices = grps * owners
    local_rows = table_w.shape[0]
    slots = seg.shape[1]
    queries = query_slot.shape[1]
    asks = slots + queries
    total_q = queries * devices
    mean = 2 * asks // devices
    cap = 16 * math.ceil((mean + 3.5 * math.sqrt(mean)) / 16)
    width = 128 * math.ceil((cap + 3) / 128)
    maxlen = pos_w.shape[1]
    own_rows = attn_w.shape[0]
    my_grp, my_row = lax.axis_index("grp"), lax.axis_index("row")

    dense = lax.all_gather(
        jnp.concatenate(
            [
                attn_w.astype(bf16),
                ffn_w.astype(bf16),
                pos_w.astype(bf16),
                jnp.pad(small_w.astype(bf16), ((0, 0), (0, SMALL - NSMALL))),
            ],
            axis=1,
        ),
        ("grp", "row"),
        axis=0,
        tiled=True,
    )

    owner_all = jnp.concatenate(
        [item_owner.reshape(1, slots), tgt_owner.reshape(1, queries)], axis=1
    )
    row_all = jnp.concatenate([item_row, tgt_row], axis=1)
    part = row_all // local_rows
    local_row = row_all - part * local_rows
    dest = part * owners + owner_all
    wanted, place, place_col, rank = run(
        functools.partial(route_kernel, cap),
        [((devices, width), i32), ((1, asks), i32), ((asks, 1), i32), ((1, asks), i32)],
        [dest, local_row, valid],
        flops=2 * devices * asks * asks,
    )
    asked = everyone(wanted)
    most = jnp.max(asked[:, cap + 1])
    rounds = (most + cap - 1) // cap
    valid_total = jnp.maximum(jnp.sum(asked[:, cap + 2]).astype(f32), 1.0).reshape(1, 1)
    (rows_found,) = run(
        functools.partial(lookup_kernel, cap),
        [((devices * cap, D), bf16)],
        [asked, table_w],
        smem=(0,),
        scratch=[pltpu.VMEM((devices * cap, D), f32)],
        moved=8 * local_rows * D,
    )
    found = everyone(rows_found.reshape(devices, cap, D)).reshape(devices * cap, D)
    item_emb, target_emb = run(
        extract_kernel,
        [((slots, D), bf16), ((queries + META, D), bf16)],
        [found, place_col, freq_idx, logfreq.reshape(1, -1)],
        flops=2 * devices * cap * asks * D,
    )

    def wanted_of(k):
        here = rank[0] // cap == k
        spot = jnp.where(here, dest[0] * cap + rank[0] - k * cap, devices * cap)
        ids = jnp.full((devices * cap,), -1, i32).at[spot].set(local_row[0], mode="drop")
        return here, spot, everyone(ids.reshape(devices, cap)).reshape(devices * cap)

    def more_rows(both):
        def one_round(carry):
            k, items, targets = carry
            here, spot, ids = wanted_of(k)
            rows = jnp.where((ids >= 0)[:, None], table_w[jnp.maximum(ids, 0)], 0.0).astype(bf16)
            got = everyone(rows.reshape(devices, cap, D)).reshape(devices * cap, D)
            got = got[jnp.minimum(spot, devices * cap - 1)]
            items = jnp.where(here[:slots, None], got[:slots], items)
            top = jnp.where(here[slots:, None], got[slots:], targets[:queries])
            return (k + 1, items, targets.at[:queries].set(top))

        return lax.while_loop(lambda c: c[0] < rounds, one_round, (jnp.int32(1),) + both)[1:]

    item_emb, target_emb = lax.cond(
        rounds > 1, more_rows, lambda both: both, (item_emb, target_emb)
    )

    targets = lax.all_to_all(
        jnp.broadcast_to(target_emb[None], (grps, queries + META, D)),
        "grp",
        split_axis=0,
        concat_axis=0,
        tiled=True,
    )
    seg_col = seg.reshape(slots, 1)
    slot_col = query_slot.reshape(queries, 1)
    query_own, *kept = run(
        forward_kernel,
        [
            ((queries, D), bf16),
            ((slots, D), f32),
            ((slots, D), bf16),
            ((slots, 2 * D), bf16),
            ((queries, D), bf16),
            ((queries, D), bf16),
            ((HEADS, queries), f32),
            ((queries, D), f32),
            ((queries, D), bf16),
            ((queries, FF), bf16),
            ((queries, D), f32),
        ],
        [item_emb, seg_col, query_slot, slot_col, dense],
        scratch=[
            pltpu.VMEM((slots, queries), f32),
            pltpu.VMEM((D, slots), bf16),
            pltpu.VMEM((D, queries), f32),
        ],
        flops=6 << 30,
    )
    query_all = lax.all_gather(query_own, "row", axis=0, tiled=True)
    (mixed,) = run(
        totals_kernel,
        [((owners, D + META, queries), bf16)],
        [query_all, targets],
        scratch=[pltpu.VMEM((D, grps * queries), bf16), pltpu.VMEM((queries, 128), f32)],
        flops=4 * owners * grps * queries * queries * D,
    )
    mixed = lax.all_to_all(mixed, "row", split_axis=0, concat_axis=0, tiled=True)
    grad_first, grads, sums = run(
        backward_kernel,
        [((slots, D), bf16), ((D, dense.shape[1]), bf16), ((8, queries), f32)],
        [mixed, target_emb, valid, valid_total, seg_col, query_slot, slot_col, dense, query_own]
        + kept,
        smem=(3,),
        scratch=[
            pltpu.VMEM((slots, queries), f32),
            pltpu.VMEM((D, slots), bf16),
            pltpu.VMEM((D, queries), f32),
            pltpu.VMEM((queries, D), bf16),
            pltpu.VMEM((slots, HEADS * queries), bf16),
            pltpu.VMEM((slots, HEADS * queries), bf16),
            pltpu.VMEM((2, HEADS * queries, D), bf16),
            pltpu.VMEM((slots, queries), f32),
            pltpu.VMEM((slots, queries), f32),
        ],
        flops=12 << 30,
    )
    sums_all = lax.all_gather(sums, "row", axis=0, tiled=True)
    (target_parts,) = run(
        functools.partial(target_grad_kernel, owners),
        [((grps, queries + META, D), bf16)],
        [jnp.stack([my_grp, my_row]).astype(i32).reshape(1, 2), query_all, targets, sums_all],
        smem=(0,),
        scratch=[pltpu.VMEM((queries, 128), f32)],
        flops=4 * owners * grps * queries * queries * D,
    )
    target_parts = lax.all_to_all(target_parts, "grp", split_axis=0, concat_axis=0, tiled=True)
    loss = jnp.sum(target_parts[:, queries : queries + 3, 0].astype(f32))

    sent, both = run(
        send_kernel,
        [((devices * cap, D), bf16), ((asks, D), bf16)],
        [grad_first, target_parts, place],
        flops=2 * devices * cap * asks * D,
    )
    received = everyone(sent.reshape(devices, cap, D)).reshape(devices * cap, D)

    held = grads.reshape(grps, owners, own_rows, -1)
    bit = 1
    while bit < owners:
        pairs = held.reshape(grps, held.shape[1] // 2, 2, own_rows, -1)
        mine = (my_row // bit) % 2
        keep = lax.dynamic_index_in_dim(pairs, mine, 2, keepdims=False)
        give = lax.dynamic_index_in_dim(pairs, 1 - mine, 2, keepdims=False)
        got = lax.ppermute(give, "row", [(i, i ^ bit) for i in range(owners)])
        held = (keep.astype(f32) + got.astype(f32)).astype(bf16)
        bit *= 2
    held = lax.all_to_all(
        held.reshape(grps, own_rows, -1), "grp", split_axis=0, concat_axis=0, tiled=True
    )
    grad_own = jnp.sum(held.astype(f32), axis=0)

    rate_table = 4.0 * total_q
    rate_dense = 0.25 * math.sqrt(total_q)
    rate_place = 2.0 * math.sqrt(total_q)
    ids = asked[:, :cap].reshape(1, devices * cap)

    def slow_update(received):
        def add(k, total, ids, rows):
            spot = jnp.where(ids >= 0, ids, local_rows)
            return total.at[spot].add(rows.astype(f32), mode="drop")

        def one_round(carry):
            k, total = carry
            here, spot, more_ids = wanted_of(k)
            rows = jnp.zeros((devices * cap, D), bf16).at[spot].set(both, mode="drop")
            rows = everyone(rows.reshape(devices, cap, D)).reshape(devices * cap, D)
            return (k + 1, add(k, total, more_ids, rows))

        total = add(0, jnp.zeros((local_rows, D), f32), ids[0], received)
        total = lax.while_loop(lambda c: c[0] < rounds, one_round, (jnp.int32(1), total))[1]
        return advance(table_w, table_m, table_a, total, rate_table)

    def fast_update(received):
        return update_table(ids, received, table_w, table_m, table_a, rate_table)

    table_out = lax.cond(rounds > 1, slow_update, fast_update, received)
    place_at = TABLES + maxlen
    return (
        (loss,)
        + table_out
        + advance(attn_w, attn_m, attn_a, grad_own[:, :ATTN], rate_dense)
        + advance(ffn_w, ffn_m, ffn_a, grad_own[:, ATTN:TABLES], rate_dense)
        + advance(pos_w, pos_m, pos_a, grad_own[:, TABLES:place_at], rate_place)
        + advance(
            small_w, small_m, small_a, grad_own[:, place_at : place_at + NSMALL], rate_dense
        )
    )


def solution(mesh):
    rows = P(("grp", "row"), None)
    table = P(("row", "grp"), None)
    ids = P(("grp", "row"), None, None)
    in_specs = (ids, rows, rows, rows, ids, rows, rows, rows, P()) + (table,) * 3 + (rows,) * 12
    out_specs = (P(),) + (table,) * 4 + (rows,) * 16
    return jax.shard_map(local, mesh=mesh, in_specs=in_specs, out_specs=out_specs, check_vma=False)
```

```python
import functools
import math

import jax
import jax.numpy as jnp
from jax import lax
from jax.experimental import pallas as pl
from jax.experimental.pallas import tpu as pltpu
from jax.sharding import PartitionSpec as P

D = 256
HEADS = 8
HEAD = 32
FF = 1024
QKV = 3 * D
ATTN = 4 * D
DOWN = ATTN + FF
TABLES = ATTN + 2 * FF
NSMALL = 11
SMALL = 128
META = 16

norm_eps = 1e-05
score_scale = 0.125
logit_scale = 0.125
momentum_rate = 0.5
average_rate = 0.5
negative = -1e30
bf16 = jnp.bfloat16
f32 = jnp.float32
i32 = jnp.int32


def iota(shape, dim, dtype=i32):
    return lax.broadcasted_iota(i32, shape, dim).astype(dtype)


def hot(condition):
    return jnp.where(condition, 1.0, 0.0).astype(bf16)


def dot(left, right):
    return lax.dot_general(left, right, (((1,), (0,)), ((), ())), preferred_element_type=f32)


def dot_cols(left, right):
    return lax.dot_general(left, right, (((1,), (1,)), ((), ())), preferred_element_type=f32)


def split(value):
    high = value.astype(bf16)
    rest = value - high.astype(f32)
    middle = rest.astype(bf16)
    low = (rest - middle.astype(f32)).astype(bf16)
    return (high, middle, low)


def run(body, outs, args, smem=(), scratch=(), flops=0, moved=0, vmem=56):
    return pl.pallas_call(
        body,
        out_shape=[jax.ShapeDtypeStruct(shape, dtype) for shape, dtype in outs],
        in_specs=[
            pl.BlockSpec(memory_space=pltpu.SMEM if i in smem else pltpu.VMEM)
            for i in range(len(args))
        ],
        out_specs=[pl.BlockSpec(memory_space=pltpu.VMEM) for unused in outs],
        scratch_shapes=list(scratch),
        compiler_params=pltpu.CompilerParams(vmem_limit_bytes=vmem << 20),
        cost_estimate=pl.CostEstimate(flops=flops, bytes_accessed=moved, transcendentals=0),
    )(*args)


def block_of(total, limit):
    return max(b for b in range(16, limit + 1, 16) if total % b == 0)


def by_rows(total, block, body, init=0):
    def step(i, carry):
        return body(pl.ds(pl.multiple_of(i * block, block), block), carry)

    return lax.fori_loop(0, total // block, step, init)


def fold(values, combine):
    parts = values.reshape(values.shape[0] // 8, 8, values.shape[1])
    return functools.reduce(combine, [parts[k] for k in range(parts.shape[0])])


def route_kernel(cap, dest_ref, local_ref, valid_ref, wanted_ref, place_ref, column_ref, rank_ref):
    devices, width = wanted_ref.shape
    asks = dest_ref.shape[1]
    dest = dest_ref[...]
    local = local_ref[...]
    named = jnp.where(iota((devices, asks), 0) == dest, 1.0, 0.0)
    earlier = hot(iota((asks, asks), 0) < iota((asks, asks), 1))
    before = dot(named.astype(bf16), earlier)
    rank = jnp.sum(named * before, axis=0, keepdims=True)
    count = jnp.sum(named, axis=1, keepdims=True)
    spot = iota((width, asks), 0, f32)
    at_spot = hot((spot == rank) & (spot < cap))
    high = (local >> 6).astype(f32)
    low = (local & 63).astype(f32)
    ids = dot_cols((named * high).astype(bf16), at_spot) * 64.0 + dot_cols(
        (named * low).astype(bf16), at_spot
    )
    lane = iota((devices, width), 1, f32)
    most = jnp.max(count, axis=0, keepdims=True)
    flags = jnp.sum(valid_ref[...].astype(f32), axis=1, keepdims=True)
    ids = jnp.where(lane < jnp.minimum(count, cap), ids, -1.0)
    ids = jnp.where(lane == cap, count, ids)
    ids = jnp.where(lane == cap + 1, most, ids)
    ids = jnp.where(lane == cap + 2, flags, ids)
    wanted_ref[...] = ids.astype(i32)
    place = jnp.where(rank < cap, dest.astype(f32) * cap + rank, -1.0)
    place_ref[...] = place.astype(i32)
    rank_ref[...] = rank.astype(i32)
    column_ref[...] = jnp.broadcast_to(place, (128, asks)).T[:, :1].astype(i32)


def lookup_kernel(cap, asked_ref, table_ref, rows_ref, held):
    devices = asked_ref.shape[0]

    def one_device(n, carry):
        count = jnp.minimum(asked_ref[n, cap], cap)

        def sixteen(k, carry):
            rows = [
                table_ref[pl.ds(jnp.maximum(asked_ref[n, k * 16 + j], 0), 1), :] for j in range(16)
            ]
            part = held.at[pl.ds(pl.multiple_of(k * 16, 16), 16)]
            for j in range(16):
                part[j : j + 1, :] = rows[j]
            return carry

        lax.fori_loop(0, (count + 15) // 16, sixteen, 0)
        live = iota((cap, 1), 0) < count
        rows_ref[pl.ds(pl.multiple_of(n * cap, 16), cap), :] = jnp.where(
            live, held[...], 0.0
        ).astype(bf16)
        return carry

    lax.fori_loop(0, devices, one_device, 0)


def extract_kernel(found_ref, column_ref, freq_ref, logfreq_ref, item_ref, target_ref):
    slots = item_ref.shape[0]
    queries = freq_ref.shape[1]
    block = 256
    total = found_ref.shape[0]

    def rows_of(begin):
        place = column_ref[pl.ds(begin, block), :]
        return dot(hot(place == iota((block, total), 1)), found_ref[...]).astype(bf16)

    def items(i, carry):
        begin = pl.multiple_of(i * block, block)
        item_ref[pl.ds(begin, block), :] = rows_of(begin)
        return carry

    lax.fori_loop(0, slots // block, items, 0)
    rows = rows_of(slots)
    entries = logfreq_ref.shape[1]
    corr = dot(logfreq_ref[...], hot(iota((entries, queries), 0) == freq_ref[...]))
    tail = jnp.broadcast_to(corr, (META, queries)).astype(bf16)
    for g in range(target_ref.shape[0]):
        target_ref[g, :queries, :] = rows
        target_ref[g, queries:, :] = tail


def centred(values):
    centre = values - jnp.mean(values, axis=-1, keepdims=True)
    spread = jnp.mean(centre * centre, axis=-1, keepdims=True)
    scale = lax.rsqrt(spread + norm_eps)
    return (centre * scale, scale)


def norm_back(grad, unit, scale, gain):
    inner = grad * gain
    return scale * (
        inner
        - jnp.mean(inner, axis=-1, keepdims=True)
        - unit * jnp.mean(inner * unit, axis=-1, keepdims=True)
    )


def total_of(values):
    return jnp.sum(values, axis=0, keepdims=True)


def places_of(seg):
    slots = seg.shape[0]
    lane = iota((slots, 128), 1)
    below = jnp.sum(jnp.where(seg < lane, 1.0, 0.0), axis=0, keepdims=True)
    start = jnp.sum(jnp.where(seg == lane, below, 0.0), axis=1, keepdims=True)
    return iota((slots, 1), 0) - start.astype(i32)


def small_rows(dense_ref, begin):
    return dense_ref[:, begin:].astype(f32).T


def mask_bias(seg, slots_q):
    shape = (seg.shape[0], slots_q.shape[1])
    slot = iota(shape, 0)
    wide = seg.astype(f32)
    seg_q = jnp.sum(jnp.where(slot == slots_q, wide, 0.0), axis=0, keepdims=True)
    return jnp.where((wide == seg_q) & (slot <= slots_q), 0.0, negative)


def prepare_kernel(
    seg_ref,
    slot_row_ref,
    slot_col_ref,
    dense_ref,
    pos_ref,
    pos_hot_t_ref,
    pos_q_ref,
    bias_ref,
    choose_ref,
):
    slots = seg_ref.shape[0]
    queries = slot_row_ref.shape[1]
    maxlen = pos_hot_t_ref.shape[0]
    pos = dense_ref[:, TABLES : TABLES + maxlen]
    seg = seg_ref[...]
    places = places_of(seg)
    pos_hot = hot(places == iota((slots, maxlen), 1))
    places_row = jnp.broadcast_to(places.astype(f32), (slots, 128)).T[:1]
    pos_hot_t_ref[...] = hot(places_row == iota((maxlen, slots), 0, f32))
    pos_ref[...] = dot_cols(pos_hot, pos)
    choose = hot(slot_col_ref[...] == iota((queries, slots), 1))
    choose_ref[...] = choose
    pos_q_ref[...] = dot(choose, pos_ref[...].astype(bf16))
    bias_ref[...] = mask_bias(seg, slot_row_ref[...])


def forward_kernel(
    item_ref,
    pos_ref,
    pos_q_ref,
    bias_ref,
    choose_ref,
    dense_ref,
    query_ref,
    first_ref,
    normed_ref,
    kv_ref,
    q_ref,
    mixed_ref,
    lse_ref,
    second_ref,
    normed_b_ref,
    active_ref,
    third_ref,
    value_t_ref,
    mixed_t_ref,
):
    small_at = dense_ref.shape[1] - SMALL
    rows = small_rows(dense_ref, small_at)
    first = item_ref[...].astype(f32) + pos_ref[...]
    first_ref[...] = first
    unit, unused = centred(first)
    normed_ref[...] = (unit * rows[0:1] + rows[1:2]).astype(bf16)
    normed = normed_ref[...]
    kv_ref[...] = dot(normed, dense_ref[:, D:QKV]).astype(bf16)
    choose = choose_ref[...]
    normed_q = dot(choose, normed).astype(bf16)
    q_ref[...] = dot(normed_q, dense_ref[:, :D]).astype(bf16)
    first_q = dot(choose, item_ref[...]) + pos_q_ref[...]
    value_t_ref[...] = kv_ref[:, D:].T

    def one_head(h, carry):
        own = iota((1, D), 1) // HEAD == h
        q_own = jnp.where(own, q_ref[...].astype(f32) * score_scale, 0.0).astype(bf16)
        scores = dot_cols(kv_ref[:, :D], q_own) + bias_ref[...]
        top = jnp.max(scores, axis=0, keepdims=True)
        weight = jnp.exp(scores - top)
        total = jnp.sum(weight, axis=0, keepdims=True)
        lse_ref[pl.ds(h, 1), :] = top + jnp.log(total)
        part = pl.ds(pl.multiple_of(h * HEAD, HEAD), HEAD)
        mixed_t_ref[part, :] = dot(value_t_ref[part, :], (weight * (1.0 / total)).astype(bf16))
        return carry

    lax.fori_loop(0, HEADS, one_head, 0)
    mixed = mixed_t_ref[...].T.astype(bf16)
    mixed_ref[...] = mixed
    second = first_q + dot(mixed, dense_ref[:, QKV:ATTN])
    second_ref[...] = second
    unit, unused = centred(second)
    normed_b = (unit * rows[2:3] + rows[3:4]).astype(bf16)
    normed_b_ref[...] = normed_b
    up_bias = jnp.concatenate([rows[7 + k : 8 + k] for k in range(FF // D)], axis=1)
    hidden = dot(normed_b, dense_ref[:, ATTN:DOWN]) + up_bias
    active = jnp.maximum(hidden, 0.0).astype(bf16)
    active_ref[...] = active
    third = second + dot_cols(active, dense_ref[:, DOWN:TABLES]) + rows[6:7]
    third_ref[...] = third
    unit, unused = centred(third)
    query_ref[...] = (unit * rows[4:5] + rows[5:6]).astype(bf16)


def columns_of(target_ref, queries):
    grps = target_ref.shape[0]
    return jnp.concatenate(
        [target_ref[g, queries : queries + 1, :].astype(f32) for g in range(grps)]
        + [jnp.zeros((128 - grps, queries), f32)],
        axis=0,
    ).T


def totals_kernel(
    query_ref,
    target_ref,
    own_ref,
    mine_ref,
    valid_ref,
    out_ref,
    target_t_ref,
    corr_ref,
):
    owners, height, unused = out_ref.shape
    queries = query_ref.shape[0] // owners
    grps = target_ref.shape[0]
    corr_ref[...] = columns_of(target_ref, queries)

    for g in range(grps):
        target_t_ref[:, g * queries : (g + 1) * queries] = target_ref[g, :queries, :].T

    tops, totals = [], []
    for r in range(owners):
        columns = slice(r * queries, (r + 1) * queries)
        query = (query_ref[columns, :].astype(f32) * logit_scale).astype(bf16)
        logits = [
            dot_cols(target_ref[g, :queries, :], query) - corr_ref[:, g : g + 1]
            for g in range(grps)
        ]
        top = functools.reduce(jnp.maximum, [jnp.max(x, axis=0, keepdims=True) for x in logits])
        total = jnp.zeros((1, queries), f32)
        mixed = jnp.zeros((D, queries), f32)
        for g in range(grps):
            weight = jnp.exp(logits[g] - top)
            total = total + jnp.sum(weight, axis=0, keepdims=True)
            mixed = mixed + dot(
                target_t_ref[:, g * queries : (g + 1) * queries], weight.astype(bf16)
            )
        out_ref[r, :D, :] = mixed.astype(bf16)
        tops.append(top)
        totals.append(total)

    product = own_ref[...].astype(f32) * mine_ref[:queries, :].astype(f32)
    own = jnp.sum(product.T, axis=0, keepdims=True) * logit_scale
    own = own - mine_ref[queries : queries + 1, :].astype(f32)
    pieces = [p for x in tops + totals + [own, valid_ref[...].astype(f32)] for p in split(x)]
    fill = jnp.zeros((height - D - len(pieces), queries), f32)
    tail = jnp.concatenate([x.astype(f32) for x in pieces] + [fill], axis=0).astype(bf16)
    for r in range(owners):
        out_ref[r, D:, :] = tail


def piece(tail, k):
    return tail[3 * k : 3 * k + 1] + tail[3 * k + 1 : 3 * k + 2] + tail[3 * k + 2 : 3 * k + 3]


def backward_dense_kernel(
    parts_ref,
    sums_ref,
    target_ref,
    valid_ref,
    total_ref,
    dense_ref,
    mixed_ref,
    second_ref,
    normed_b_ref,
    active_ref,
    third_ref,
    grads_ref,
    proj_ref,
    grad_second_ref,
    grad_o_ref,
    columns_ref,
):
    owners = parts_ref.shape[0]
    queries = valid_ref.shape[1]
    small_at = dense_ref.shape[1] - SMALL
    rows = small_rows(dense_ref, small_at)
    sums = sums_ref[...]
    tops = [sums[2 * r : 2 * r + 1] for r in range(owners)]
    totals = [sums[2 * r + 1 : 2 * r + 2] for r in range(owners)]
    top = functools.reduce(jnp.maximum, tops)
    scales = [jnp.exp(x - top) for x in tops]
    total = sum(x * y for x, y in zip(scales, totals))
    weight = valid_ref[...].astype(f32) / total_ref[0, 0]
    mean_t = jnp.zeros((D, queries), f32)
    for r in range(owners):
        mean_t = mean_t + parts_ref[r, :D, :].astype(f32) * (scales[r] / total)
    target = target_ref[0, :queries, :].astype(f32)
    grad_query = ((mean_t - target.T) * (weight * logit_scale)).T

    unit, scale = centred(third_ref[...])
    grad_third = norm_back(grad_query, unit, scale, rows[4:5])
    gain_f, shift_f = total_of(grad_query * unit), total_of(grad_query)
    grad_f = grad_third.astype(bf16)
    active = active_ref[...]
    grads_ref[:, FF:] = dot(grad_f.T, active).astype(bf16)
    down_bias = total_of(grad_f.astype(f32))
    grad_active = dot(grad_f, dense_ref[:, DOWN:TABLES])
    grad_hidden = jnp.where(active.astype(f32) > 0.0, grad_active, 0.0).astype(bf16)
    grads_ref[:, :FF] = dot(normed_b_ref[...].T, grad_hidden).astype(bf16)
    up_bias = total_of(grad_hidden.astype(f32))
    grad_b = dot_cols(grad_hidden, dense_ref[:, ATTN:DOWN])
    unit, scale = centred(second_ref[...])
    grad_second = grad_third + norm_back(grad_b, unit, scale, rows[2:3])
    gain_b, shift_b = total_of(grad_b * unit), total_of(grad_b)
    grad_second_ref[...] = grad_second
    grad_y = grad_second.astype(bf16)
    proj_ref[...] = dot(mixed_ref[...].T, grad_y).astype(bf16)
    grad_o_ref[...] = dot_cols(grad_y, dense_ref[:, QKV:ATTN]).astype(bf16)
    columns = [gain_b, shift_b, gain_f, shift_f, down_bias]
    columns += [up_bias[:, k * D : (k + 1) * D] for k in range(FF // D)]
    columns_ref[...] = jnp.concatenate(
        columns + [jnp.zeros((META - len(columns), D), f32)], axis=0
    )


def backward_kernel(
    proj_ref,
    grad_second_ref,
    grad_o_ref,
    columns_ref,
    slot_row_ref,
    dense_ref,
    bias_ref,
    pos_hot_t_ref,
    first_ref,
    normed_t_ref,
    key_t_ref,
    kv_ref,
    q_ref,
    lse_ref,
    grad_first_ref,
    grads_ref,
    grad_q_t_ref,
    probs_ref,
    grad_s_ref,
    stack_ref,
    p_ref,
    dp_ref,
    joined_ref,
    grad_a_ref,
    base_ref,
    halves_ref,
):
    slots, queries = bias_ref.shape
    maxlen = pos_hot_t_ref.shape[0]
    small_at = dense_ref.shape[1] - SMALL
    rows = small_rows(dense_ref, small_at)

    def one_head(h, carry):
        own = iota((1, D), 1) // HEAD == h
        q_own = jnp.where(own, q_ref[...].astype(f32), 0.0)
        stack_ref[0, pl.ds(pl.multiple_of(h * queries, queries), queries), :] = q_own.astype(bf16)
        o_own = jnp.where(own, grad_o_ref[...].astype(f32), 0.0).astype(bf16)
        stack_ref[1, pl.ds(pl.multiple_of(h * queries, queries), queries), :] = o_own
        columns = pl.ds(pl.multiple_of(h * queries, queries), queries)
        scores = dot_cols(kv_ref[:, :D], (q_own * score_scale).astype(bf16)) + bias_ref[...]
        probs = jnp.exp(scores - lse_ref[pl.ds(h, 1), :])
        p_ref[...] = probs
        probs_ref[:, columns] = probs.astype(bf16)
        grad_p = dot_cols(kv_ref[:, D:], o_own)
        dp_ref[...] = grad_p
        inner = jnp.sum(p_ref[...] * grad_p, axis=0, keepdims=True)
        grad_s_ref[:, columns] = (p_ref[...] * (dp_ref[...] - inner)).astype(bf16)
        part = pl.ds(pl.multiple_of(h * HEAD, HEAD), HEAD)
        grad_q_t_ref[part, :] = dot(key_t_ref[part, :], grad_s_ref[:, columns])
        return carry

    lax.fori_loop(0, HEADS, one_head, 0)
    grad_q = (grad_q_t_ref[...].T * score_scale).astype(bf16)
    spread = hot(iota((slots, queries), 0) == slot_row_ref[...])
    joined_ref[:, :D] = dot(spread, grad_q).astype(bf16)
    joined_ref[:, D : 2 * D] = (dot(grad_s_ref[...], stack_ref[0]) * score_scale).astype(bf16)
    joined_ref[:, 2 * D :] = dot(probs_ref[...], stack_ref[1]).astype(bf16)
    grads_ref[:, :QKV] = dot(normed_t_ref[...], joined_ref[...]).astype(bf16)
    grads_ref[:, QKV:ATTN] = proj_ref[...]
    grad_a_ref[...] = dot_cols(joined_ref[...], dense_ref[:, :QKV])
    high, middle, unused = split(grad_second_ref[...])
    base_ref[...] = dot(spread, high) + dot(spread, middle)

    grad_a = grad_a_ref[...]
    unit, scale = centred(first_ref[...])
    grad_first = base_ref[...] + norm_back(grad_a, unit, scale, rows[0:1])
    grad_first_ref[...] = grad_first.astype(bf16)
    high, middle, unused = split(grad_first)
    halves_ref[:, :D] = high
    halves_ref[:, D:] = middle
    gain_a, shift_a = total_of(grad_a * unit), total_of(grad_a)
    both = dot(pos_hot_t_ref[...], halves_ref[...])
    grads_ref[:, ATTN : ATTN + maxlen] = (both[:, :D] + both[:, D:]).T.astype(bf16)
    columns = jnp.concatenate(
        [gain_a, shift_a, columns_ref[: NSMALL - 2]]
        + [jnp.zeros((SMALL - NSMALL, D), f32)],
        axis=0,
    )
    grads_ref[:, ATTN + maxlen :] = columns.T.astype(bf16)


def target_grad_kernel(
    owners,
    where_ref,
    total_ref,
    query_ref,
    target_ref,
    parts_ref,
    out_ref,
    sums_ref,
    corr_ref,
):
    grps = target_ref.shape[0]
    queries = query_ref.shape[0] // owners
    corr_ref[...] = columns_of(target_ref, queries)
    same = jnp.where(iota((queries, queries), 0) == iota((queries, queries), 1), 1.0, 0.0)
    own_g, own_r = where_ref[0, 0], where_ref[0, 1]
    tails = [parts_ref[r, D:, :].astype(f32) for r in range(owners)]
    log_totals, weights = [], []
    loss = jnp.zeros((1, queries), f32)
    sums_ref[...] = jnp.zeros(sums_ref.shape, f32)
    for r in range(owners):
        tops = [piece(tail, r) for tail in tails]
        totals = [piece(tail, owners + r) for tail in tails]
        top = functools.reduce(jnp.maximum, tops)
        total = functools.reduce(
            jnp.add, [totals[k] * jnp.exp(tops[k] - top) for k in range(owners)]
        )
        log_totals.append(top + jnp.log(total))
        weights.append(piece(tails[r], 2 * owners + 1) / total_ref[0, 0])
        loss = loss + weights[r] * (log_totals[r] - piece(tails[r], 2 * owners))
        mine = own_r == r
        for k in range(owners):
            sums_ref[2 * k : 2 * k + 1, :] += jnp.where(mine, tops[k], 0.0)
            sums_ref[2 * k + 1 : 2 * k + 2, :] += jnp.where(mine, totals[k], 0.0)
    loss = jnp.sum(loss, axis=1, keepdims=True)
    pieces = split(jnp.broadcast_to(loss, (1, queries)))
    tail = jnp.concatenate(
        [x.astype(f32) for x in pieces] + [jnp.zeros((META - len(pieces), queries), f32)], axis=0
    ).astype(bf16)
    for g in range(grps):
        target = target_ref[g, :queries, :]
        grad = jnp.zeros((queries, D), f32)
        for r in range(owners):
            query = query_ref[r * queries : (r + 1) * queries, :]
            logits = dot_cols(target, query) * logit_scale - corr_ref[:, g : g + 1]
            hit = jnp.where((own_g == g) & (own_r == r), 1.0, 0.0)
            coeff = weights[r] * (jnp.exp(logits - log_totals[r]) - hit * same)
            grad = grad + dot(coeff.astype(bf16), query)
        out_ref[g, :queries, :] = grad.astype(bf16)
        out_ref[g, queries:, :] = tail


def turn_kernel(normed_ref, kv_ref, normed_t_ref, key_t_ref):
    normed_t_ref[...] = normed_ref[...].T
    key_t_ref[...] = kv_ref[:, :D].T


def send_kernel(grad_first_ref, parts_ref, place_ref, sent_ref, both_ref):
    grps, height, unused = parts_ref.shape
    slots = grad_first_ref.shape[0]
    queries = height - META
    both_ref[:slots, :] = grad_first_ref[...]
    total = parts_ref[0, :queries, :].astype(f32)
    for g in range(1, grps):
        total = total + parts_ref[g, :queries, :].astype(f32)
    both_ref[slots:, :] = (total * logit_scale).astype(bf16)
    asks = both_ref.shape[0]
    block = block_of(sent_ref.shape[0], 2048)

    def one_block(i, carry):
        begin = pl.multiple_of(i * block, block)
        spread = hot(place_ref[...] - begin == iota((block, asks), 0))
        sent_ref[pl.ds(begin, block), :] = dot(spread, both_ref[...]).astype(bf16)
        return carry

    lax.fori_loop(0, sent_ref.shape[0] // block, one_block, 0)


def advance(weight, moment, average, grad, rate):
    moment_new = momentum_rate * moment + grad
    weight_new = weight - rate * (grad + momentum_rate * moment_new)
    average_new = average_rate * average + (1.0 - average_rate) * weight_new
    return (weight_new, moment_new, average_new, weight_new.astype(bf16))


def update_kernel(
    rate,
    rounds_ref,
    ids_ref,
    recv_ref,
    extra_ref,
    w_ref,
    m_ref,
    a_ref,
    w_out_ref,
    m_out_ref,
    a_out_ref,
    copy_ref,
):
    rows = w_ref.shape[0]
    base = pl.program_id(0) * rows
    spread = hot(ids_ref[...] - base == iota((rows, ids_ref.shape[1]), 0))
    grad = dot(spread, recv_ref[...])
    grad = grad + jnp.where(rounds_ref[0] > 1, extra_ref[...], 0.0)
    new = advance(w_ref[...], m_ref[...], a_ref[...], grad, rate)
    w_out_ref[...], m_out_ref[...], a_out_ref[...], copy_ref[...] = new


def update_table(rounds, ids, recv, extra, table_w, table_m, table_a, rate):
    rows = 800
    count = table_w.shape[0]
    block = pl.BlockSpec((rows, D), lambda i, rounds: (i, 0))
    spare = pl.BlockSpec((rows, D), lambda i, rounds: (jnp.where(rounds[0] > 1, i, 0), 0))
    whole = [pl.BlockSpec(memory_space=pltpu.VMEM)] * 2
    return tuple(
        pl.pallas_call(
            functools.partial(update_kernel, rate),
            grid_spec=pltpu.PrefetchScalarGridSpec(
                num_scalar_prefetch=1,
                grid=(pl.cdiv(count, rows),),
                in_specs=whole + [spare] + [block] * 3,
                out_specs=[block] * 4,
            ),
            out_shape=[jax.ShapeDtypeStruct((count, D), f32)] * 3
            + [jax.ShapeDtypeStruct((count, D), bf16)],
            compiler_params=pltpu.CompilerParams(vmem_limit_bytes=40 << 20),
            cost_estimate=pl.CostEstimate(
                flops=2 * count * recv.shape[0] * D, bytes_accessed=26 * count * D, transcendentals=0
            ),
        )(rounds.reshape(1), ids, recv, extra, table_w, table_m, table_a)
    )


def blank_kernel(seed_ref, out_ref):
    del seed_ref, out_ref


def everyone(values):
    return lax.all_to_all(values, ("grp", "row"), split_axis=0, concat_axis=0, tiled=True)


def swap(values, axis, bit):
    pairs = [(i, i ^ bit) for i in range(lax.axis_size(axis))]
    return lax.ppermute(values, axis, pairs)


def bits_of(size):
    return [1 << k for k in range(size.bit_length() - 1)]


def after(values, *others):
    return lax.optimization_barrier((values,) + others)[0]


def spread_row(values, bit):
    got = swap(values, "row", bit)
    mine = (lax.axis_index("row") // bit) % 2 == 0
    return jnp.stack([jnp.where(mine, values, got), jnp.where(mine, got, values)], axis=-3)


def sum_row(values, owners):
    for bit in bits_of(owners):
        grps, count, rows, width = values.shape
        pairs = values.reshape(grps, count // 2, 2, rows, width)
        mine = (lax.axis_index("row") // bit) % 2
        keep = lax.dynamic_index_in_dim(pairs, mine, 2, keepdims=False)
        give = lax.dynamic_index_in_dim(pairs, 1 - mine, 2, keepdims=False)
        values = (keep.astype(f32) + swap(give, "row", bit).astype(f32)).astype(bf16)
    return values.reshape(grps, rows, width)


def local(
    item_owner,
    item_row,
    seg,
    query_slot,
    tgt_owner,
    tgt_row,
    freq_idx,
    valid,
    logfreq,
    table_w,
    table_m,
    table_a,
    attn_w,
    attn_m,
    attn_a,
    ffn_w,
    ffn_m,
    ffn_a,
    pos_w,
    pos_m,
    pos_a,
    small_w,
    small_m,
    small_a,
):
    owners = lax.axis_size("row")
    grps = lax.axis_size("grp")
    devices = grps * owners
    local_rows = table_w.shape[0]
    slots = seg.shape[1]
    queries = query_slot.shape[1]
    asks = slots + queries
    total_q = queries * devices
    mean = 2 * asks // devices
    cap = 16 * math.ceil((mean + 3.5 * math.sqrt(mean)) / 16)
    width = 128 * math.ceil((cap + 3) / 128)
    maxlen = pos_w.shape[1]
    own_rows = attn_w.shape[0]
    my_grp, my_row = lax.axis_index("grp"), lax.axis_index("row")

    dense_own = jnp.concatenate(
        [
            attn_w.astype(bf16),
            ffn_w.astype(bf16),
            pos_w.astype(bf16),
            jnp.pad(small_w.astype(bf16), ((0, 0), (0, SMALL - NSMALL))),
        ],
        axis=1,
    )
    owner_all = jnp.concatenate(
        [item_owner.reshape(1, slots), tgt_owner.reshape(1, queries)], axis=1
    )
    row_all = jnp.concatenate([item_row, tgt_row], axis=1)
    part = row_all // local_rows
    local_row = row_all - part * local_rows
    dest = part * owners + owner_all
    wanted, place, place_col, rank = run(
        functools.partial(route_kernel, cap),
        [((devices, width), i32), ((1, asks), i32), ((asks, 1), i32), ((1, asks), i32)],
        [dest, local_row, valid],
        flops=2 * devices * asks * asks,
    )
    asked = everyone(wanted)
    dense = lax.all_to_all(
        jnp.broadcast_to(after(dense_own, asked)[None], (grps, own_rows, dense_own.shape[1])),
        "grp",
        split_axis=0,
        concat_axis=0,
        tiled=True,
    )
    most = jnp.max(asked[:, cap + 1])
    rounds = (most + cap - 1) // cap
    valid_total = jnp.maximum(jnp.sum(asked[:, cap + 2]).astype(f32), 1.0).reshape(1, 1)
    (rows_found,) = run(
        functools.partial(lookup_kernel, cap),
        [((devices * cap, D), bf16)],
        [asked, table_w],
        smem=(0,),
        scratch=[pltpu.VMEM((cap, D), f32)],
        moved=8 * local_rows * D,
        vmem=24,
    )
    dense = after(dense, rows_found)
    for bit in reversed(bits_of(owners)):
        dense = spread_row(dense, bit)
    dense = dense.reshape(D, -1)
    found = everyone(rows_found.reshape(devices, cap, D)).reshape(devices * cap, D)
    seg_col = seg.reshape(slots, 1)
    slot_col = query_slot.reshape(queries, 1)
    pos_part, pos_hot_t, pos_q, bias, choose = run(
        prepare_kernel,
        [
            ((slots, D), f32),
            ((maxlen, slots), bf16),
            ((queries, D), f32),
            ((slots, queries), f32),
            ((queries, slots), bf16),
        ],
        [seg_col, query_slot, slot_col, dense],
        flops=1 << 30,
    )
    found = after(found, pos_part)
    item_emb, target_emb = run(
        extract_kernel,
        [((slots, D), bf16), ((grps, queries + META, D), bf16)],
        [found, place_col, freq_idx, logfreq.reshape(1, -1)],
        flops=2 * devices * cap * asks * D,
    )

    def wanted_of(k):
        here = rank[0] // cap == k
        spot = jnp.where(here, dest[0] * cap + rank[0] - k * cap, devices * cap)
        ids = jnp.full((devices * cap,), -1, i32).at[spot].set(local_row[0], mode="drop")
        return here, spot, everyone(ids.reshape(devices, cap)).reshape(devices * cap)

    def more_rows(carry):
        k, items, targets = carry
        here, spot, ids = wanted_of(k)
        rows = jnp.where((ids >= 0)[:, None], table_w[jnp.maximum(ids, 0)], 0.0).astype(bf16)
        got = everyone(rows.reshape(devices, cap, D)).reshape(devices * cap, D)
        got = got[jnp.minimum(spot, devices * cap - 1)]
        items = jnp.where(here[:slots, None], got[:slots], items)
        top = jnp.where(here[None, slots:, None], got[None, slots:], targets[:, :queries])
        return (k + 1, items, targets.at[:, :queries].set(top))

    unused, item_emb, target_emb = lax.while_loop(
        lambda carry: carry[0] < rounds, more_rows, (jnp.int32(1), item_emb, target_emb)
    )
    targets = lax.all_to_all(target_emb, "grp", split_axis=0, concat_axis=0, tiled=True)
    query_own, first, normed, kv, q_own, mixed_o, lse, second, normed_b, active, third = run(
        forward_kernel,
        [
            ((queries, D), bf16),
            ((slots, D), f32),
            ((slots, D), bf16),
            ((slots, 2 * D), bf16),
            ((queries, D), bf16),
            ((queries, D), bf16),
            ((HEADS, queries), f32),
            ((queries, D), f32),
            ((queries, D), bf16),
            ((queries, FF), bf16),
            ((queries, D), f32),
        ],
        [item_emb, pos_part, pos_q, bias, choose, dense],
        scratch=[
            pltpu.VMEM((D, slots), bf16),
            pltpu.VMEM((D, queries), f32),
        ],
        flops=6 << 30,
    )
    query_all = lax.all_gather(query_own, "row", axis=0, tiled=True)
    tall = 16 * math.ceil((6 * owners + 6) / 16)
    (mixed,) = run(
        totals_kernel,
        [((owners, D + tall, queries), bf16)],
        [query_all, targets, query_own, target_emb[0], valid],
        scratch=[
            pltpu.VMEM((D, grps * queries), bf16),
            pltpu.VMEM((queries, 128), f32),
        ],
        flops=4 * owners * grps * queries * queries * D,
    )
    mixed = lax.all_to_all(mixed, "row", split_axis=0, concat_axis=0, tiled=True)
    target_parts, sums = run(
        functools.partial(target_grad_kernel, owners),
        [((grps, queries + META, D), bf16), ((2 * owners, queries), f32)],
        [
            jnp.stack([my_grp, my_row]).astype(i32).reshape(1, 2),
            valid_total,
            query_all,
            targets,
            mixed,
        ],
        smem=(0, 1),
        scratch=[pltpu.VMEM((queries, 128), f32)],
        flops=4 * owners * grps * queries * queries * D,
    )
    target_parts = lax.all_to_all(target_parts, "grp", split_axis=0, concat_axis=0, tiled=True)
    normed_t, key_t = run(turn_kernel, [((D, slots), bf16)] * 2, [normed, kv], moved=4 << 20)
    grads_ffn, grads_proj, grad_second, grad_o, columns = run(
        backward_dense_kernel,
        [
            ((D, 2 * FF), bf16),
            ((D, D), bf16),
            ((queries, D), f32),
            ((queries, D), bf16),
            ((META, D), f32),
        ],
        [mixed, sums, target_emb, valid, valid_total, dense, mixed_o, second, normed_b]
        + [active, third],
        smem=(4,),
        flops=1 << 30,
    )
    grads_ffn = sum_row(grads_ffn.reshape(grps, owners, own_rows, -1), owners)
    grad_first, grads = run(
        backward_kernel,
        [((slots, D), bf16), ((D, ATTN + maxlen + SMALL), bf16)],
        [grads_proj, grad_second, grad_o, columns, query_slot, dense, bias, pos_hot_t, first]
        + [normed_t, key_t, kv, q_own, lse],
        scratch=[
            pltpu.VMEM((D, queries), f32),
            pltpu.VMEM((slots, HEADS * queries), bf16),
            pltpu.VMEM((slots, HEADS * queries), bf16),
            pltpu.VMEM((2, HEADS * queries, D), bf16),
            pltpu.VMEM((slots, queries), f32),
            pltpu.VMEM((slots, queries), f32),
            pltpu.VMEM((slots, QKV), bf16),
            pltpu.VMEM((slots, D), f32),
            pltpu.VMEM((slots, D), f32),
            pltpu.VMEM((slots, 2 * D), bf16),
        ],
        flops=10 << 30,
    )
    loss = jnp.sum(target_parts[:, queries : queries + 3, 0].astype(f32))

    sent, both = run(
        send_kernel,
        [((devices * cap, D), bf16), ((asks, D), bf16)],
        [grad_first, target_parts, place],
        flops=2 * devices * cap * asks * D,
    )
    received = everyone(sent.reshape(devices, cap, D)).reshape(devices * cap, D)
    grads = sum_row(grads.reshape(grps, owners, own_rows, -1), owners)
    grad_own = jnp.concatenate([grads_ffn, grads], axis=-1)
    grad_own, received = lax.optimization_barrier((grad_own, received))
    grad_own = lax.all_to_all(grad_own, "grp", split_axis=0, concat_axis=0, tiled=True)
    grad_own = jnp.sum(grad_own.astype(f32), axis=0)

    rate_table = 4.0 * total_q
    rate_dense = 0.25 * math.sqrt(total_q)
    rate_place = 2.0 * math.sqrt(total_q)
    ids = asked[:, :cap].reshape(1, devices * cap)

    blank = pl.pallas_call(
        blank_kernel,
        out_shape=jax.ShapeDtypeStruct((local_rows, D), f32),
        in_specs=[pl.BlockSpec(memory_space=pl.ANY)],
        out_specs=pl.BlockSpec(memory_space=pl.ANY),
    )(wanted)

    def more_grads(carry):
        k, total = carry
        here, spot, more_ids = wanted_of(k)
        rows = jnp.zeros((devices * cap, D), bf16).at[spot].set(both, mode="drop")
        rows = everyone(rows.reshape(devices, cap, D)).reshape(devices * cap, D)
        spot = jnp.where(more_ids >= 0, more_ids, local_rows)
        total = jnp.where(k > 1, total, 0.0)
        return (k + 1, total.at[spot].add(rows.astype(f32), mode="drop"))

    unused, extra = lax.while_loop(
        lambda carry: carry[0] < rounds,
        more_grads,
        (jnp.int32(1), blank),
    )
    table_out = update_table(rounds, ids, received, extra, table_w, table_m, table_a, rate_table)
    attn_at, place_at = 2 * FF, 2 * FF + ATTN
    small_at = place_at + maxlen
    return (
        (loss,)
        + table_out
        + advance(attn_w, attn_m, attn_a, grad_own[:, attn_at:place_at], rate_dense)
        + advance(ffn_w, ffn_m, ffn_a, grad_own[:, :attn_at], rate_dense)
        + advance(pos_w, pos_m, pos_a, grad_own[:, place_at:small_at], rate_place)
        + advance(small_w, small_m, small_a, grad_own[:, small_at : small_at + NSMALL], rate_dense)
    )


def solution(mesh):
    rows = P(("grp", "row"), None)
    table = P(("row", "grp"), None)
    ids = P(("grp", "row"), None, None)
    in_specs = (ids, rows, rows, rows, ids, rows, rows, rows, P()) + (table,) * 3 + (rows,) * 12
    out_specs = (P(),) + (table,) * 4 + (rows,) * 16
    return jax.shard_map(local, mesh=mesh, in_specs=in_specs, out_specs=out_specs, check_vma=False)
```

```python
import functools
import math

import jax
import jax.numpy as jnp
from jax import lax
from jax.experimental import pallas as pl
from jax.experimental.pallas import tpu as pltpu
from jax.sharding import PartitionSpec as P

D = 256
HEADS = 8
HEAD = 32
FF = 1024
QKV = 3 * D
ATTN = 4 * D
DOWN = ATTN + FF
TABLES = ATTN + 2 * FF
NSMALL = 11
SMALL = 128
META = 16
CHUNK = 512

norm_eps = 1e-05
score_scale = 0.125
logit_scale = 0.125
momentum_rate = 0.5
average_rate = 0.5
negative = -1e30
bf16 = jnp.bfloat16
f32 = jnp.float32
i32 = jnp.int32


def iota(shape, dim, dtype=i32):
    return lax.broadcasted_iota(i32, shape, dim).astype(dtype)


def hot(condition):
    return jnp.where(condition, 1.0, 0.0).astype(bf16)


def dot(left, right):
    return lax.dot_general(left, right, (((1,), (0,)), ((), ())), preferred_element_type=f32)


def dot_cols(left, right):
    return lax.dot_general(left, right, (((1,), (1,)), ((), ())), preferred_element_type=f32)


def split(value):
    high = value.astype(bf16)
    rest = value - high.astype(f32)
    middle = rest.astype(bf16)
    low = (rest - middle.astype(f32)).astype(bf16)
    return (high, middle, low)


def run(body, outs, args, smem=(), scratch=(), flops=0, moved=0, vmem=56):
    return pl.pallas_call(
        body,
        out_shape=[jax.ShapeDtypeStruct(shape, dtype) for shape, dtype in outs],
        in_specs=[
            pl.BlockSpec(memory_space=pltpu.SMEM if i in smem else pltpu.VMEM)
            for i in range(len(args))
        ],
        out_specs=[pl.BlockSpec(memory_space=pltpu.VMEM) for unused in outs],
        scratch_shapes=list(scratch),
        compiler_params=pltpu.CompilerParams(vmem_limit_bytes=vmem << 20),
        cost_estimate=pl.CostEstimate(flops=flops, bytes_accessed=moved, transcendentals=0),
    )(*args)


def block_of(total, limit):
    return max(b for b in range(16, limit + 1, 16) if total % b == 0)


def by_rows(total, block, body, init=0):
    def step(i, carry):
        return body(pl.ds(pl.multiple_of(i * block, block), block), carry)

    return lax.fori_loop(0, total // block, step, init)


def fold(values, combine):
    parts = values.reshape(values.shape[0] // 8, 8, values.shape[1])
    return functools.reduce(combine, [parts[k] for k in range(parts.shape[0])])


def column_of(row):
    return jnp.broadcast_to(row, (128, row.shape[1])).T[:, :1]


def route_kernel(
    cap,
    local_rows,
    grps,
    item_owner_ref,
    item_row_ref,
    tgt_owner_ref,
    tgt_row_ref,
    valid_ref,
    wanted_ref,
    place_ref,
    column_ref,
    rank_ref,
    dest_ref,
    local_ref,
):
    devices, width = wanted_ref.shape
    asks = dest_ref.shape[1]
    owner = jnp.concatenate([item_owner_ref[...], tgt_owner_ref[...]], axis=1).astype(f32)
    row = jnp.concatenate([item_row_ref[...], tgt_row_ref[...]], axis=1).astype(f32)
    part = jnp.zeros((1, asks), f32)
    for g in range(1, grps):
        part = part + jnp.where(row >= g * local_rows, 1.0, 0.0)
    dest = part * (devices // grps) + owner
    local = row - part * local_rows
    dest_ref[...] = dest.astype(i32)
    local_ref[...] = local.astype(i32)
    named = jnp.where(iota((devices, asks), 0, f32) == dest, 1.0, 0.0)
    count = jnp.sum(named, axis=1, keepdims=True)
    count_row = jnp.broadcast_to(count, (devices, 128)).T[:1, :]
    below = jnp.where(iota((devices, devices), 1) < iota((devices, devices), 0), 1.0, 0.0)
    before = jnp.sum(below * count_row, axis=1, keepdims=True)
    room = jnp.sum(named * jnp.maximum(cap - count, 0.0), axis=0, keepdims=True)
    item = (dest * local_rows + local).astype(i32)
    key = item * 2048 + iota((1, asks), 1)
    key_col = column_of(dest * local_rows + local).astype(i32) * 2048 + iota((asks, 1), 0)
    rank = jnp.sum(jnp.where(key_col < key, 1.0, 0.0), axis=0, keepdims=True)
    rank = rank - jnp.sum(named * before, axis=0, keepdims=True)
    lead = jnp.floor(local * (cap / local_rows)) - rank + dest * 4096.0
    lead = jnp.where(key_col <= key, column_of(lead), 0.0)
    lead = jnp.max(lead, axis=0, keepdims=True) - dest * 4096.0
    slot = rank + jnp.minimum(lead, room)
    spot = iota((width, asks), 0, f32)
    at_spot = hot((spot == slot) & (rank < cap))
    high = jnp.floor((local + 1.0) * (1.0 / 64.0))
    low = local + 1.0 - high * 64.0
    ids = dot_cols((named * high).astype(bf16), at_spot) * 64.0 + dot_cols(
        (named * low).astype(bf16), at_spot
    )
    lane = iota((devices, width), 1, f32)
    most = jnp.max(count, axis=0, keepdims=True)
    flags = jnp.sum(valid_ref[...].astype(f32), axis=1, keepdims=True)
    ids = ids - 1.0
    ids = jnp.where(lane == cap, count, ids)
    ids = jnp.where(lane == cap + 1, most, ids)
    ids = jnp.where(lane == cap + 2, flags, ids)
    wanted_ref[...] = ids.astype(i32)
    place = jnp.where(rank < cap, dest * cap + slot, -1.0)
    place_ref[...] = place.astype(i32)
    rank_ref[...] = rank.astype(i32)
    column_ref[...] = column_of(place).astype(i32)


def low_kernel(attn_ref, ffn_ref, pos_ref, small_ref, out_ref):
    small_at = out_ref.shape[2] - SMALL
    rows = attn_ref.shape[0]
    tail = jnp.concatenate([small_ref[...], jnp.zeros((rows, SMALL - NSMALL), f32)], axis=1)
    for g in range(out_ref.shape[0]):
        out_ref[g, :, :ATTN] = attn_ref[...].astype(bf16)
        out_ref[g, :, ATTN:TABLES] = ffn_ref[...].astype(bf16)
        out_ref[g, :, TABLES:small_at] = pos_ref[...].astype(bf16)
        out_ref[g, :, small_at:] = tail.astype(bf16)


def lower_table_kernel(table_ref, low_ref, token_ref, held_ref, sems):
    count = table_ref.shape[0]
    edges = [count * k // 32 * 8 for k in range(4)] + [count]
    copies = []
    for k in range(4):
        part = pl.ds(edges[k], edges[k + 1] - edges[k])
        copies.append(pltpu.make_async_copy(table_ref.at[part], held_ref.at[part], sems.at[k]))
        copies[k].start()
    for k in range(4):
        copies[k].wait()
        part = slice(edges[k], edges[k + 1])
        low_ref[part, :] = held_ref[part, :].astype(bf16)
    spare = low_ref.shape[0] - count
    if spare:
        low_ref[count:, :] = jnp.zeros((spare, D), bf16)
    token_ref[...] = jnp.zeros(token_ref.shape, f32)


def lower_table(table):
    count = table.shape[0]
    return pl.pallas_call(
        lower_table_kernel,
        out_shape=[
            pltpu.VMEM((CHUNK * math.ceil(count / CHUNK), D), bf16),
            jax.ShapeDtypeStruct((8, 128), f32),
        ],
        in_specs=[pl.BlockSpec(memory_space=pl.ANY)],
        out_specs=[pl.BlockSpec(memory_space=pltpu.VMEM)] * 2,
        scratch_shapes=[pltpu.VMEM((count, D), f32), pltpu.SemaphoreType.DMA((4,))],
        compiler_params=pltpu.CompilerParams(vmem_limit_bytes=16 << 20),
        cost_estimate=pl.CostEstimate(flops=0, bytes_accessed=6 * count * D, transcendentals=0),
    )(pltpu.with_memory_space_constraint(table, pltpu.HBM))


def lookup_kernel(cap, local_rows, asked_ref, token_ref, low_ref, rows_ref, ids_ref, total_ref):
    del token_ref
    devices, width = asked_ref.shape
    chunk = CHUNK
    turned = asked_ref[...].astype(f32).T
    slot = iota((16, devices), 0)
    for j in range(cap // 16):
        part = turned[16 * j : 16 * (j + 1), :]
        for n in range(devices):
            ids_ref[16 * n : 16 * (n + 1), :] = jnp.broadcast_to(part[:, n : n + 1], (16, 128))
        first = jnp.min(jnp.where(part >= 0.0, part, float(local_rows))).astype(i32)
        last = jnp.max(part).astype(i32)
        total_ref[...] = jnp.zeros(total_ref.shape, f32)

        def one_chunk(c, carry):
            begin = pl.multiple_of(c * chunk, chunk)
            ids = ids_ref[...] - (c * chunk).astype(f32)
            near = jnp.concatenate(
                [hot(ids == iota((1, 128), 1, f32) + 128.0 * k) for k in range(chunk // 128)],
                axis=1,
            )
            total_ref[...] += dot(near, low_ref[pl.ds(begin, chunk), :])
            return carry

        lax.fori_loop(first // chunk, last // chunk + 1, one_chunk, 0)
        for n in range(devices):
            rows_ref[n, 16 * j : 16 * (j + 1), :] = total_ref[16 * n : 16 * (n + 1), :].astype(bf16)


def rows_of(found_ref, place):
    total = found_ref.shape[0]
    return dot(hot(place == iota((place.shape[0], total), 1)), found_ref[...])


def extract_targets_kernel(found_ref, column_ref, corr_ref, target_ref):
    queries = corr_ref.shape[1]
    rows = rows_of(found_ref, column_ref[column_ref.shape[0] - queries :, :])
    for g in range(target_ref.shape[0]):
        target_ref[g, :queries, :] = rows.astype(bf16)
        target_ref[g, queries:, :] = corr_ref[...]


def extract_items_kernel(found_ref, column_ref, patch_ref, item_ref):
    def items(part, carry):
        place = column_ref[part, :]
        rows = rows_of(found_ref, place)
        item_ref[part, :] = jnp.where(place < 0, patch_ref[part, :].astype(f32), rows).astype(bf16)
        return carry

    by_rows(item_ref.shape[0], 256, items)


def centred(values):
    centre = values - jnp.mean(values, axis=-1, keepdims=True)
    spread = jnp.mean(centre * centre, axis=-1, keepdims=True)
    scale = lax.rsqrt(spread + norm_eps)
    return (centre * scale, scale)


def norm_back(grad, unit, scale, gain):
    inner = grad * gain
    return scale * (
        inner
        - jnp.mean(inner, axis=-1, keepdims=True)
        - unit * jnp.mean(inner * unit, axis=-1, keepdims=True)
    )


def total_of(values):
    return jnp.sum(values, axis=0, keepdims=True)


def places_of(seg):
    slots = seg.shape[0]
    lane = iota((slots, 128), 1)
    below = jnp.sum(jnp.where(seg < lane, 1.0, 0.0), axis=0, keepdims=True)
    start = jnp.sum(jnp.where(seg == lane, below, 0.0), axis=1, keepdims=True)
    return iota((slots, 1), 0) - start.astype(i32)


def small_rows(dense_ref, begin):
    return dense_ref[:, begin:].astype(f32).T


def mask_bias(seg, slots_q):
    shape = (seg.shape[0], slots_q.shape[1])
    slot = iota(shape, 0)
    wide = seg.astype(f32)
    seg_q = jnp.sum(jnp.where(slot == slots_q, wide, 0.0), axis=0, keepdims=True)
    return jnp.where((wide == seg_q) & (slot <= slots_q), 0.0, negative)


def prepare_kernel(
    seg_ref,
    slot_row_ref,
    slot_col_ref,
    dense_ref,
    freq_ref,
    logfreq_ref,
    pos_ref,
    pos_hot_t_ref,
    pos_q_ref,
    bias_ref,
    choose_ref,
    corr_ref,
):
    slots = seg_ref.shape[0]
    queries = slot_row_ref.shape[1]
    maxlen = pos_hot_t_ref.shape[0]
    pos = dense_ref[:, TABLES : TABLES + maxlen]
    seg = seg_ref[...]
    places = places_of(seg)
    pos_hot = hot(places == iota((slots, maxlen), 1))
    places_row = jnp.broadcast_to(places.astype(f32), (slots, 128)).T[:1]
    pos_hot_t_ref[...] = hot(places_row == iota((maxlen, slots), 0, f32))
    pos_ref[...] = dot_cols(pos_hot, pos)
    choose = hot(slot_col_ref[...] == iota((queries, slots), 1))
    choose_ref[...] = choose
    pos_q_ref[...] = dot(choose, pos_ref[...].astype(bf16))
    bias_ref[...] = mask_bias(seg, slot_row_ref[...])
    entries = logfreq_ref.shape[1]
    corr = dot(logfreq_ref[...], hot(iota((entries, queries), 0) == freq_ref[...]))
    corr_ref[...] = jnp.broadcast_to(corr, (META, queries)).astype(bf16)


def forward_kernel(
    item_ref,
    pos_ref,
    pos_q_ref,
    bias_ref,
    choose_ref,
    dense_ref,
    query_ref,
    first_ref,
    normed_ref,
    kv_ref,
    q_ref,
    mixed_ref,
    lse_ref,
    second_ref,
    normed_b_ref,
    active_ref,
    third_ref,
    value_t_ref,
    mixed_t_ref,
):
    small_at = dense_ref.shape[1] - SMALL
    rows = small_rows(dense_ref, small_at)
    first = item_ref[...].astype(f32) + pos_ref[...]
    first_ref[...] = first
    unit, unused = centred(first)
    normed_ref[...] = (unit * rows[0:1] + rows[1:2]).astype(bf16)
    normed = normed_ref[...]
    kv_ref[...] = dot(normed, dense_ref[:, D:QKV]).astype(bf16)
    choose = choose_ref[...]
    normed_q = dot(choose, normed).astype(bf16)
    q_ref[...] = dot(normed_q, dense_ref[:, :D]).astype(bf16)
    first_q = dot(choose, item_ref[...]) + pos_q_ref[...]
    value_t_ref[...] = kv_ref[:, D:].T

    def one_head(h, carry):
        own = iota((1, D), 1) // HEAD == h
        q_own = jnp.where(own, q_ref[...].astype(f32) * score_scale, 0.0).astype(bf16)
        scores = dot_cols(kv_ref[:, :D], q_own) + bias_ref[...]
        top = jnp.max(scores, axis=0, keepdims=True)
        weight = jnp.exp(scores - top)
        total = jnp.sum(weight, axis=0, keepdims=True)
        lse_ref[pl.ds(h, 1), :] = top + jnp.log(total)
        part = pl.ds(pl.multiple_of(h * HEAD, HEAD), HEAD)
        mixed_t_ref[part, :] = dot(value_t_ref[part, :], (weight * (1.0 / total)).astype(bf16))
        return carry

    lax.fori_loop(0, HEADS, one_head, 0)
    mixed = mixed_t_ref[...].T.astype(bf16)
    mixed_ref[...] = mixed
    second = first_q + dot(mixed, dense_ref[:, QKV:ATTN])
    second_ref[...] = second
    unit, unused = centred(second)
    normed_b = (unit * rows[2:3] + rows[3:4]).astype(bf16)
    normed_b_ref[...] = normed_b
    up_bias = jnp.concatenate([rows[7 + k : 8 + k] for k in range(FF // D)], axis=1)
    hidden = dot(normed_b, dense_ref[:, ATTN:DOWN]) + up_bias
    active = jnp.maximum(hidden, 0.0).astype(bf16)
    active_ref[...] = active
    third = second + dot_cols(active, dense_ref[:, DOWN:TABLES]) + rows[6:7]
    third_ref[...] = third
    unit, unused = centred(third)
    query_ref[...] = (unit * rows[4:5] + rows[5:6]).astype(bf16)


def columns_of(target_ref, queries):
    grps = target_ref.shape[0]
    return jnp.concatenate(
        [target_ref[g, queries : queries + 1, :].astype(f32) for g in range(grps)]
        + [jnp.zeros((128 - grps, queries), f32)],
        axis=0,
    ).T


def totals_kernel(
    query_ref,
    target_ref,
    own_ref,
    mine_ref,
    valid_ref,
    out_ref,
    target_t_ref,
    corr_ref,
):
    owners, height, unused = out_ref.shape
    queries = query_ref.shape[0] // owners
    grps = target_ref.shape[0]
    corr_ref[...] = columns_of(target_ref, queries)

    for g in range(grps):
        target_t_ref[:, g * queries : (g + 1) * queries] = target_ref[g, :queries, :].T

    tops, totals = [], []
    for r in range(owners):
        columns = slice(r * queries, (r + 1) * queries)
        query = (query_ref[columns, :].astype(f32) * logit_scale).astype(bf16)
        logits = [
            dot_cols(target_ref[g, :queries, :], query) - corr_ref[:, g : g + 1]
            for g in range(grps)
        ]
        top = functools.reduce(jnp.maximum, [jnp.max(x, axis=0, keepdims=True) for x in logits])
        total = jnp.zeros((1, queries), f32)
        mixed = jnp.zeros((D, queries), f32)
        for g in range(grps):
            weight = jnp.exp(logits[g] - top)
            total = total + jnp.sum(weight, axis=0, keepdims=True)
            mixed = mixed + dot(
                target_t_ref[:, g * queries : (g + 1) * queries], weight.astype(bf16)
            )
        out_ref[r, :D, :] = mixed.astype(bf16)
        tops.append(top)
        totals.append(total)

    product = own_ref[...].astype(f32) * mine_ref[:queries, :].astype(f32)
    own = jnp.sum(product.T, axis=0, keepdims=True) * logit_scale
    own = own - mine_ref[queries : queries + 1, :].astype(f32)
    pieces = [p for x in tops + totals + [own, valid_ref[...].astype(f32)] for p in split(x)]
    fill = jnp.zeros((height - D - len(pieces), queries), f32)
    tail = jnp.concatenate([x.astype(f32) for x in pieces] + [fill], axis=0).astype(bf16)
    for r in range(owners):
        out_ref[r, D:, :] = tail


def piece(tail, k):
    return tail[3 * k : 3 * k + 1] + tail[3 * k + 1 : 3 * k + 2] + tail[3 * k + 2 : 3 * k + 3]


def backward_dense_kernel(
    parts_ref,
    sums_ref,
    target_ref,
    valid_ref,
    total_ref,
    dense_ref,
    mixed_ref,
    second_ref,
    normed_b_ref,
    active_ref,
    third_ref,
    grads_ref,
    proj_ref,
    grad_second_ref,
    grad_o_ref,
    columns_ref,
):
    owners = parts_ref.shape[0]
    queries = valid_ref.shape[1]
    small_at = dense_ref.shape[1] - SMALL
    rows = small_rows(dense_ref, small_at)
    sums = sums_ref[...]
    tops = [sums[2 * r : 2 * r + 1] for r in range(owners)]
    totals = [sums[2 * r + 1 : 2 * r + 2] for r in range(owners)]
    top = functools.reduce(jnp.maximum, tops)
    scales = [jnp.exp(x - top) for x in tops]
    total = sum(x * y for x, y in zip(scales, totals))
    weight = valid_ref[...].astype(f32) / total_ref[0, 0]
    mean_t = jnp.zeros((D, queries), f32)
    for r in range(owners):
        mean_t = mean_t + parts_ref[r, :D, :].astype(f32) * (scales[r] / total)
    target = target_ref[0, :queries, :].astype(f32)
    grad_query = ((mean_t - target.T) * (weight * logit_scale)).T

    unit, scale = centred(third_ref[...])
    grad_third = norm_back(grad_query, unit, scale, rows[4:5])
    gain_f, shift_f = total_of(grad_query * unit), total_of(grad_query)
    grad_f = grad_third.astype(bf16)
    active = active_ref[...]
    grads_ref[:, FF:] = dot(grad_f.T, active).astype(bf16)
    down_bias = total_of(grad_f.astype(f32))
    grad_active = dot(grad_f, dense_ref[:, DOWN:TABLES])
    grad_hidden = jnp.where(active.astype(f32) > 0.0, grad_active, 0.0).astype(bf16)
    grads_ref[:, :FF] = dot(normed_b_ref[...].T, grad_hidden).astype(bf16)
    up_bias = total_of(grad_hidden.astype(f32))
    grad_b = dot_cols(grad_hidden, dense_ref[:, ATTN:DOWN])
    unit, scale = centred(second_ref[...])
    grad_second = grad_third + norm_back(grad_b, unit, scale, rows[2:3])
    gain_b, shift_b = total_of(grad_b * unit), total_of(grad_b)
    grad_second_ref[...] = grad_second
    grad_y = grad_second.astype(bf16)
    proj_ref[...] = dot(mixed_ref[...].T, grad_y).astype(bf16)
    grad_o_ref[...] = dot_cols(grad_y, dense_ref[:, QKV:ATTN]).astype(bf16)
    columns = [gain_b, shift_b, gain_f, shift_f, down_bias]
    columns += [up_bias[:, k * D : (k + 1) * D] for k in range(FF // D)]
    columns_ref[...] = jnp.concatenate(
        columns + [jnp.zeros((META - len(columns), D), f32)], axis=0
    )


def backward_kernel(
    proj_ref,
    grad_second_ref,
    grad_o_ref,
    columns_ref,
    slot_row_ref,
    dense_ref,
    bias_ref,
    pos_hot_t_ref,
    first_ref,
    normed_t_ref,
    key_t_ref,
    kv_ref,
    q_ref,
    lse_ref,
    grad_first_ref,
    grads_ref,
    grad_q_t_ref,
    probs_ref,
    grad_s_ref,
    stack_ref,
    p_ref,
    dp_ref,
    joined_ref,
    grad_a_ref,
    base_ref,
    halves_ref,
):
    slots, queries = bias_ref.shape
    maxlen = pos_hot_t_ref.shape[0]
    small_at = dense_ref.shape[1] - SMALL
    rows = small_rows(dense_ref, small_at)

    def one_head(h, carry):
        own = iota((1, D), 1) // HEAD == h
        q_own = jnp.where(own, q_ref[...].astype(f32), 0.0)
        stack_ref[0, pl.ds(pl.multiple_of(h * queries, queries), queries), :] = q_own.astype(bf16)
        o_own = jnp.where(own, grad_o_ref[...].astype(f32), 0.0).astype(bf16)
        stack_ref[1, pl.ds(pl.multiple_of(h * queries, queries), queries), :] = o_own
        columns = pl.ds(pl.multiple_of(h * queries, queries), queries)
        scores = dot_cols(kv_ref[:, :D], (q_own * score_scale).astype(bf16)) + bias_ref[...]
        probs = jnp.exp(scores - lse_ref[pl.ds(h, 1), :])
        p_ref[...] = probs
        probs_ref[:, columns] = probs.astype(bf16)
        grad_p = dot_cols(kv_ref[:, D:], o_own)
        dp_ref[...] = grad_p
        inner = jnp.sum(p_ref[...] * grad_p, axis=0, keepdims=True)
        grad_s_ref[:, columns] = (p_ref[...] * (dp_ref[...] - inner)).astype(bf16)
        part = pl.ds(pl.multiple_of(h * HEAD, HEAD), HEAD)
        grad_q_t_ref[part, :] = dot(key_t_ref[part, :], grad_s_ref[:, columns])
        return carry

    lax.fori_loop(0, HEADS, one_head, 0)
    grad_q = (grad_q_t_ref[...].T * score_scale).astype(bf16)
    spread = hot(iota((slots, queries), 0) == slot_row_ref[...])
    joined_ref[:, :D] = dot(spread, grad_q).astype(bf16)
    joined_ref[:, D : 2 * D] = (dot(grad_s_ref[...], stack_ref[0]) * score_scale).astype(bf16)
    joined_ref[:, 2 * D :] = dot(probs_ref[...], stack_ref[1]).astype(bf16)
    grads_ref[:, :QKV] = dot(normed_t_ref[...], joined_ref[...]).astype(bf16)
    grads_ref[:, QKV:ATTN] = proj_ref[...]
    grad_a_ref[...] = dot_cols(joined_ref[...], dense_ref[:, :QKV])
    high, middle, unused = split(grad_second_ref[...])
    base_ref[...] = dot(spread, high) + dot(spread, middle)

    grad_a = grad_a_ref[...]
    unit, scale = centred(first_ref[...])
    grad_first = base_ref[...] + norm_back(grad_a, unit, scale, rows[0:1])
    grad_first_ref[...] = grad_first.astype(bf16)
    high, middle, unused = split(grad_first)
    halves_ref[:, :D] = high
    halves_ref[:, D:] = middle
    gain_a, shift_a = total_of(grad_a * unit), total_of(grad_a)
    both = dot(pos_hot_t_ref[...], halves_ref[...])
    grads_ref[:, ATTN : ATTN + maxlen] = (both[:, :D] + both[:, D:]).T.astype(bf16)
    columns = jnp.concatenate(
        [gain_a, shift_a, columns_ref[: NSMALL - 2]]
        + [jnp.zeros((SMALL - NSMALL, D), f32)],
        axis=0,
    )
    grads_ref[:, ATTN + maxlen :] = columns.T.astype(bf16)


def target_grad_kernel(
    owners,
    where_ref,
    total_ref,
    query_ref,
    target_ref,
    parts_ref,
    out_ref,
    sums_ref,
    corr_ref,
):
    grps = target_ref.shape[0]
    queries = query_ref.shape[0] // owners
    corr_ref[...] = columns_of(target_ref, queries)
    same = jnp.where(iota((queries, queries), 0) == iota((queries, queries), 1), 1.0, 0.0)
    own_g, own_r = where_ref[0, 0], where_ref[0, 1]
    tails = [parts_ref[r, D:, :].astype(f32) for r in range(owners)]
    log_totals, weights = [], []
    loss = jnp.zeros((1, queries), f32)
    sums_ref[...] = jnp.zeros(sums_ref.shape, f32)
    for r in range(owners):
        tops = [piece(tail, r) for tail in tails]
        totals = [piece(tail, owners + r) for tail in tails]
        top = functools.reduce(jnp.maximum, tops)
        total = functools.reduce(
            jnp.add, [totals[k] * jnp.exp(tops[k] - top) for k in range(owners)]
        )
        log_totals.append(top + jnp.log(total))
        weights.append(piece(tails[r], 2 * owners + 1) / total_ref[0, 0])
        loss = loss + weights[r] * (log_totals[r] - piece(tails[r], 2 * owners))
        mine = own_r == r
        for k in range(owners):
            sums_ref[2 * k : 2 * k + 1, :] += jnp.where(mine, tops[k], 0.0)
            sums_ref[2 * k + 1 : 2 * k + 2, :] += jnp.where(mine, totals[k], 0.0)
    loss = jnp.sum(loss, axis=1, keepdims=True)
    pieces = split(jnp.broadcast_to(loss, (1, queries)))
    tail = jnp.concatenate(
        [x.astype(f32) for x in pieces] + [jnp.zeros((META - len(pieces), queries), f32)], axis=0
    ).astype(bf16)
    for g in range(grps):
        target = target_ref[g, :queries, :]
        grad = jnp.zeros((queries, D), f32)
        for r in range(owners):
            query = query_ref[r * queries : (r + 1) * queries, :]
            logits = dot_cols(target, query) * logit_scale - corr_ref[:, g : g + 1]
            hit = jnp.where((own_g == g) & (own_r == r), 1.0, 0.0)
            coeff = weights[r] * (jnp.exp(logits - log_totals[r]) - hit * same)
            grad = grad + dot(coeff.astype(bf16), query)
        out_ref[g, :queries, :] = grad.astype(bf16)
        out_ref[g, queries:, :] = tail


def turn_kernel(normed_ref, kv_ref, normed_t_ref, key_t_ref):
    normed_t_ref[...] = normed_ref[...].T
    key_t_ref[...] = kv_ref[:, :D].T


def send_kernel(grad_first_ref, parts_ref, place_ref, sent_ref, both_ref, loss_ref):
    grps, height, unused = parts_ref.shape
    slots = grad_first_ref.shape[0]
    queries = height - META
    both_ref[:slots, :] = grad_first_ref[...]
    total = parts_ref[0, :queries, :].astype(f32)
    for g in range(1, grps):
        total = total + parts_ref[g, :queries, :].astype(f32)
    both_ref[slots:, :] = (total * logit_scale).astype(bf16)
    loss = parts_ref[0, queries : queries + 8, :].astype(f32)
    for g in range(1, grps):
        loss = loss + parts_ref[g, queries : queries + 8, :].astype(f32)
    loss_ref[...] = jnp.sum(loss[:, :1], axis=0, keepdims=True)
    asks = both_ref.shape[0]
    block = block_of(sent_ref.shape[0], 2048)

    def one_block(i, carry):
        begin = pl.multiple_of(i * block, block)
        spread = hot(place_ref[...] - begin == iota((block, asks), 0))
        sent_ref[pl.ds(begin, block), :] = dot(spread, both_ref[...]).astype(bf16)
        return carry

    lax.fori_loop(0, sent_ref.shape[0] // block, one_block, 0)


def advance(weight, moment, average, grad, rate):
    moment_new = momentum_rate * moment + grad
    weight_new = weight - rate * (grad + momentum_rate * moment_new)
    average_new = average_rate * average + (1.0 - average_rate) * weight_new
    return (weight_new, moment_new, average_new, weight_new.astype(bf16))


def update_kernel(
    rate,
    rows,
    span_ref,
    ids_ref,
    recv_ref,
    extra_ref,
    w_ref,
    m_ref,
    a_ref,
    w_out_ref,
    m_out_ref,
    a_out_ref,
    copy_out_ref,
    w_held,
    m_held,
    a_held,
    copy_held,
    tiles_ref,
    grad_ref,
    in_sems,
    out_sems,
    extra_sem,
):
    count = w_ref.shape[0]
    devices, cap, unused = recv_ref.shape
    tiles = cap // 16
    edges = list(range(0, count, rows)) + [count]
    parts = [(k, edges[k], edges[k + 1] - edges[k]) for k in range(len(edges) - 1)]

    def copy_in(k, begin, size, j):
        source, target = ((w_ref, w_held), (m_ref, m_held), (a_ref, a_held))[j]
        part = pl.ds(begin, size)
        return pltpu.make_async_copy(source.at[part], target.at[part], in_sems.at[j, k])

    def copy_out(k, begin, size, j):
        pairs = (
            (w_held, w_out_ref),
            (m_held, m_out_ref),
            (a_held, a_out_ref),
            (copy_held, copy_out_ref),
        )
        source, target = pairs[j]
        part = pl.ds(begin, size)
        return pltpu.make_async_copy(source.at[part], target.at[part], out_sems.at[j, k])

    for part in parts:
        for j in range(3):
            copy_in(*part, j).start()
    for j in range(tiles):
        for n in range(devices):
            tiles_ref[j, 16 * n : 16 * (n + 1), :] = recv_ref[n, 16 * j : 16 * (j + 1), :]

    for k, begin, size in parts:
        here = pl.ds(0, size)
        grad_ref[here, :] = jnp.zeros((size, D), f32)

        @pl.when(span_ref[0] > 1)
        def start_from_extra():
            copy = pltpu.make_async_copy(
                extra_ref.at[pl.ds(begin, size)], grad_ref.at[here], extra_sem
            )
            copy.start()
            copy.wait()

        for j in range(tiles):

            @pl.when((span_ref[1 + 2 * j] < begin + size) & (span_ref[2 + 2 * j] >= begin))
            def add():
                spread = hot(ids_ref[j : j + 1, :] - begin == iota((size, ids_ref.shape[1]), 0))
                grad_ref[here, :] += dot(spread, tiles_ref[j])

        for j in range(3):
            copy_in(k, begin, size, j).wait()
        part = pl.ds(begin, size)
        new = advance(w_held[part, :], m_held[part, :], a_held[part, :], grad_ref[here, :], rate)
        w_held[part, :], m_held[part, :], a_held[part, :], copy_held[part, :] = new
        for j in range(4):
            copy_out(k, begin, size, j).start()
    for part in parts:
        for j in range(4):
            copy_out(*part, j).wait()


def update_table(span, ids, recv, extra, table_w, table_m, table_a, rate):
    count = table_w.shape[0]
    rows = min(784, count)
    blocks = math.ceil(count / rows)
    devices, cap, unused = recv.shape
    anywhere = pl.BlockSpec(memory_space=pl.ANY)
    inside = pl.BlockSpec(memory_space=pltpu.VMEM)
    tables = [pltpu.with_memory_space_constraint(x, pltpu.HBM) for x in (table_w, table_m, table_a)]
    return tuple(
        pl.pallas_call(
            functools.partial(update_kernel, rate, rows),
            in_specs=[pl.BlockSpec(memory_space=pltpu.SMEM), inside, inside] + [anywhere] * 4,
            out_specs=[anywhere] * 4,
            scratch_shapes=[pltpu.VMEM((count, D), f32)] * 3
            + [
                pltpu.VMEM((count, D), bf16),
                pltpu.VMEM((cap // 16, 16 * devices, D), bf16),
                pltpu.VMEM((rows, D), f32),
                pltpu.SemaphoreType.DMA((3, blocks)),
                pltpu.SemaphoreType.DMA((4, blocks)),
                pltpu.SemaphoreType.DMA(()),
            ],
            out_shape=[jax.ShapeDtypeStruct((count, D), f32)] * 3
            + [jax.ShapeDtypeStruct((count, D), bf16)],
            compiler_params=pltpu.CompilerParams(vmem_limit_bytes=56 << 20),
            cost_estimate=pl.CostEstimate(
                flops=count * devices * cap * D, bytes_accessed=26 * count * D, transcendentals=0
            ),
        )(span, ids, recv, extra, *tables)
    )


def blank_kernel(seed_ref, out_ref):
    del seed_ref, out_ref


def blank_of(shape, dtype, seed):
    return pl.pallas_call(
        blank_kernel,
        out_shape=jax.ShapeDtypeStruct(shape, dtype),
        in_specs=[pl.BlockSpec(memory_space=pl.ANY)],
        out_specs=pl.BlockSpec(memory_space=pl.ANY),
    )(seed)


def everyone(values):
    return lax.all_to_all(values, ("grp", "row"), split_axis=0, concat_axis=0, tiled=True)


def swap(values, axis, bit):
    pairs = [(i, i ^ bit) for i in range(lax.axis_size(axis))]
    return lax.ppermute(values, axis, pairs)


def bits_of(size):
    return [1 << k for k in range(size.bit_length() - 1)]


def after(values, *others):
    return lax.optimization_barrier((values,) + others)[0]


def spread_row(values, bit):
    got = swap(values, "row", bit)
    mine = (lax.axis_index("row") // bit) % 2 == 0
    return jnp.stack([jnp.where(mine, values, got), jnp.where(mine, got, values)], axis=-3)


def sum_row(values, owners):
    for bit in bits_of(owners):
        grps, count, rows, width = values.shape
        pairs = values.reshape(grps, count // 2, 2, rows, width)
        mine = (lax.axis_index("row") // bit) % 2
        keep = lax.dynamic_index_in_dim(pairs, mine, 2, keepdims=False)
        give = lax.dynamic_index_in_dim(pairs, 1 - mine, 2, keepdims=False)
        values = (keep.astype(f32) + swap(give, "row", bit).astype(f32)).astype(bf16)
    return values.reshape(grps, rows, width)


def local(
    item_owner,
    item_row,
    seg,
    query_slot,
    tgt_owner,
    tgt_row,
    freq_idx,
    valid,
    logfreq,
    table_w,
    table_m,
    table_a,
    attn_w,
    attn_m,
    attn_a,
    ffn_w,
    ffn_m,
    ffn_a,
    pos_w,
    pos_m,
    pos_a,
    small_w,
    small_m,
    small_a,
):
    owners = lax.axis_size("row")
    grps = lax.axis_size("grp")
    devices = grps * owners
    local_rows = table_w.shape[0]
    slots = seg.shape[1]
    queries = query_slot.shape[1]
    asks = slots + queries
    total_q = queries * devices
    mean = 2 * asks // devices
    cap = 16 * math.ceil((mean + 3.5 * math.sqrt(mean)) / 16)
    width = 128 * math.ceil((cap + 3) / 128)
    maxlen = pos_w.shape[1]
    own_rows = attn_w.shape[0]
    my_grp, my_row = lax.axis_index("grp"), lax.axis_index("row")

    wanted, place, place_col, rank, dest, local_row = run(
        functools.partial(route_kernel, cap, local_rows, grps),
        [((devices, width), i32), ((1, asks), i32), ((asks, 1), i32)] + [((1, asks), i32)] * 3,
        [
            item_owner.reshape(1, slots),
            item_row,
            tgt_owner.reshape(1, queries),
            tgt_row,
            valid,
        ],
        flops=2 * devices * asks * asks,
    )
    asked = everyone(wanted)
    (dense,) = run(
        low_kernel,
        [((grps, own_rows, TABLES + maxlen + SMALL), bf16)],
        [attn_w, ffn_w, pos_w, after(small_w, wanted)],
        moved=1 << 20,
    )
    low_table, token = lower_table(after(table_w, wanted))
    dense, asked, token = lax.optimization_barrier((dense, asked, token))
    dense = lax.all_to_all(
        dense, "grp", split_axis=0, concat_axis=0, tiled=True
    )
    most = jnp.max(asked[:, cap + 1])
    rounds = (most + cap - 1) // cap
    valid_total = jnp.maximum(jnp.sum(asked[:, cap + 2]).astype(f32), 1.0).reshape(1, 1)
    (rows_found,) = run(
        functools.partial(lookup_kernel, cap, local_rows),
        [((devices, cap, D), bf16)],
        [asked, token, low_table],
        scratch=[pltpu.VMEM((16 * devices, 128), f32), pltpu.VMEM((16 * devices, D), f32)],
        moved=8 * local_rows * D,
        vmem=24,
    )
    dense, rows_found = lax.optimization_barrier((dense, rows_found))
    for bit in reversed(bits_of(owners)):
        dense = spread_row(dense, bit)
    dense = dense.reshape(D, -1)
    found = everyone(rows_found).reshape(devices * cap, D)
    seg_col = seg.reshape(slots, 1)
    slot_col = query_slot.reshape(queries, 1)
    pos_part, pos_hot_t, pos_q, bias, choose, corr = run(
        prepare_kernel,
        [
            ((slots, D), f32),
            ((maxlen, slots), bf16),
            ((queries, D), f32),
            ((slots, queries), f32),
            ((queries, slots), bf16),
            ((META, queries), bf16),
        ],
        [seg_col, query_slot, slot_col, dense, freq_idx, logfreq.reshape(1, -1)],
        flops=1 << 30,
    )
    found = after(found, pos_part)
    (target_emb,) = run(
        extract_targets_kernel,
        [((grps, queries + META, D), bf16)],
        [found, place_col, corr],
        flops=2 * devices * cap * queries * D,
    )
    def wanted_of(k):
        here = rank[0] // cap == k
        spot = jnp.where(here, dest[0] * cap + rank[0] - k * cap, devices * cap)
        ids = jnp.full((devices * cap,), -1, i32).at[spot].set(local_row[0], mode="drop")
        return here, spot, everyone(ids.reshape(devices, cap)).reshape(devices * cap)

    def more_rows(carry):
        k, items, targets = carry
        here, spot, ids = wanted_of(k)
        rows = jnp.where((ids >= 0)[:, None], table_w[jnp.maximum(ids, 0)], 0.0).astype(bf16)
        got = everyone(rows.reshape(devices, cap, D)).reshape(devices * cap, D)
        got = got[jnp.minimum(spot, devices * cap - 1)]
        items = jnp.where(here[:slots, None], got[:slots], items)
        top = jnp.where(here[None, slots:, None], got[None, slots:], targets[:, :queries])
        return (k + 1, items, targets.at[:, :queries].set(top))

    unused, patch, target_emb = lax.while_loop(
        lambda carry: carry[0] < rounds,
        more_rows,
        (jnp.int32(1), blank_of((slots, D), bf16, wanted), target_emb),
    )
    (item_emb,) = run(
        extract_items_kernel,
        [((slots, D), bf16)],
        [after(found, target_emb), place_col, patch],
        flops=2 * devices * cap * slots * D,
    )
    targets = lax.all_to_all(target_emb, "grp", split_axis=0, concat_axis=0, tiled=True)
    query_own, first, normed, kv, q_own, mixed_o, lse, second, normed_b, active, third = run(
        forward_kernel,
        [
            ((queries, D), bf16),
            ((slots, D), f32),
            ((slots, D), bf16),
            ((slots, 2 * D), bf16),
            ((queries, D), bf16),
            ((queries, D), bf16),
            ((HEADS, queries), f32),
            ((queries, D), f32),
            ((queries, D), bf16),
            ((queries, FF), bf16),
            ((queries, D), f32),
        ],
        [item_emb, pos_part, pos_q, bias, choose, dense],
        scratch=[
            pltpu.VMEM((D, slots), bf16),
            pltpu.VMEM((D, queries), f32),
        ],
        flops=6 << 30,
    )
    query_all = lax.all_gather(query_own, "row", axis=0, tiled=True)
    tall = 16 * math.ceil((6 * owners + 6) / 16)
    (mixed,) = run(
        totals_kernel,
        [((owners, D + tall, queries), bf16)],
        [query_all, targets, query_own, target_emb[0], valid],
        scratch=[
            pltpu.VMEM((D, grps * queries), bf16),
            pltpu.VMEM((queries, 128), f32),
        ],
        flops=4 * owners * grps * queries * queries * D,
    )
    mixed = lax.all_to_all(mixed, "row", split_axis=0, concat_axis=0, tiled=True)
    normed_t, key_t = run(turn_kernel, [((D, slots), bf16)] * 2, [normed, kv], moved=4 << 20)
    mixed = after(mixed, normed_t, key_t)
    target_parts, sums = run(
        functools.partial(target_grad_kernel, owners),
        [((grps, queries + META, D), bf16), ((2 * owners, queries), f32)],
        [
            jnp.stack([my_grp, my_row]).astype(i32).reshape(1, 2),
            valid_total,
            query_all,
            targets,
            mixed,
        ],
        smem=(0, 1),
        scratch=[pltpu.VMEM((queries, 128), f32)],
        flops=4 * owners * grps * queries * queries * D,
    )
    target_parts = lax.all_to_all(target_parts, "grp", split_axis=0, concat_axis=0, tiled=True)
    grads_ffn, grads_proj, grad_second, grad_o, columns = run(
        backward_dense_kernel,
        [
            ((D, 2 * FF), bf16),
            ((D, D), bf16),
            ((queries, D), f32),
            ((queries, D), bf16),
            ((META, D), f32),
        ],
        [mixed, sums, target_emb, valid, valid_total, dense, mixed_o, second, normed_b]
        + [active, third],
        smem=(4,),
        flops=1 << 30,
    )
    grads_ffn = sum_row(grads_ffn.reshape(grps, owners, own_rows, -1), owners)
    grad_first, grads = run(
        backward_kernel,
        [((slots, D), bf16), ((D, ATTN + maxlen + SMALL), bf16)],
        [grads_proj, grad_second, grad_o, columns, query_slot, dense, bias, pos_hot_t, first]
        + [normed_t, key_t, kv, q_own, lse],
        scratch=[
            pltpu.VMEM((D, queries), f32),
            pltpu.VMEM((slots, HEADS * queries), bf16),
            pltpu.VMEM((slots, HEADS * queries), bf16),
            pltpu.VMEM((2, HEADS * queries, D), bf16),
            pltpu.VMEM((slots, queries), f32),
            pltpu.VMEM((slots, queries), f32),
            pltpu.VMEM((slots, QKV), bf16),
            pltpu.VMEM((slots, D), f32),
            pltpu.VMEM((slots, D), f32),
            pltpu.VMEM((slots, 2 * D), bf16),
        ],
        flops=10 << 30,
    )

    sent, both, loss = run(
        send_kernel,
        [((devices * cap, D), bf16), ((asks, D), bf16), ((1, 1), f32)],
        [grad_first, target_parts, place],
        flops=2 * devices * cap * asks * D,
    )
    received = everyone(sent.reshape(devices, cap, D))
    grads = sum_row(grads.reshape(grps, owners, own_rows, -1), owners)
    grad_own = jnp.concatenate([grads_ffn, grads], axis=-1)
    grad_own, received = lax.optimization_barrier((grad_own, received))
    grad_own = lax.all_to_all(grad_own, "grp", split_axis=0, concat_axis=0, tiled=True)
    grad_own = jnp.sum(grad_own.astype(f32), axis=0)

    rate_table = 4.0 * total_q
    rate_dense = 0.25 * math.sqrt(total_q)
    rate_place = 2.0 * math.sqrt(total_q)
    ids = asked[:, :cap].reshape(devices, cap // 16, 16).transpose(1, 0, 2)
    ids = ids.reshape(cap // 16, 16 * devices)
    low_end = jnp.min(jnp.where(ids >= 0, ids, local_rows), axis=1)
    span = jnp.stack([low_end, jnp.max(ids, axis=1)], axis=1).reshape(-1)
    span = jnp.concatenate([rounds.reshape(1), span])

    blank = blank_of((local_rows, D), f32, wanted)

    def more_grads(carry):
        k, total = carry
        here, spot, more_ids = wanted_of(k)
        rows = jnp.zeros((devices * cap, D), bf16).at[spot].set(both, mode="drop")
        rows = everyone(rows.reshape(devices, cap, D)).reshape(devices * cap, D)
        spot = jnp.where(more_ids >= 0, more_ids, local_rows)
        total = jnp.where(k > 1, total, 0.0)
        return (k + 1, total.at[spot].add(rows.astype(f32), mode="drop"))

    unused, extra = lax.while_loop(
        lambda carry: carry[0] < rounds,
        more_grads,
        (jnp.int32(1), blank),
    )
    table_out = update_table(span, ids, received, extra, table_w, table_m, table_a, rate_table)
    attn_at, place_at = 2 * FF, 2 * FF + ATTN
    small_at = place_at + maxlen
    return (
        (loss.reshape(()),)
        + table_out
        + advance(attn_w, attn_m, attn_a, grad_own[:, attn_at:place_at], rate_dense)
        + advance(ffn_w, ffn_m, ffn_a, grad_own[:, :attn_at], rate_dense)
        + advance(pos_w, pos_m, pos_a, grad_own[:, place_at:small_at], rate_place)
        + advance(small_w, small_m, small_a, grad_own[:, small_at : small_at + NSMALL], rate_dense)
    )


def solution(mesh):
    rows = P(("grp", "row"), None)
    table = P(("row", "grp"), None)
    ids = P(("grp", "row"), None, None)
    in_specs = (ids, rows, rows, rows, ids, rows, rows, rows, P()) + (table,) * 3 + (rows,) * 12
    out_specs = (P(),) + (table,) * 4 + (rows,) * 16
    return jax.shard_map(local, mesh=mesh, in_specs=in_specs, out_specs=out_specs, check_vma=False)
```

```python
import functools
import math

import jax
import jax.numpy as jnp
from jax import lax
from jax.experimental import pallas as pl
from jax.experimental.pallas import tpu as pltpu
from jax.sharding import PartitionSpec as P

D = 256
HEADS = 8
HEAD = 32
FF = 1024
QKV = 3 * D
ATTN = 4 * D
DOWN = ATTN + FF
TABLES = ATTN + 2 * FF
NSMALL = 11
SMALL = 128
META = 16
CHUNK = 512

norm_eps = 1e-05
score_scale = 0.125
logit_scale = 0.125
momentum_rate = 0.5
average_rate = 0.5
negative = -1e30
bf16 = jnp.bfloat16
f32 = jnp.float32
i32 = jnp.int32


def iota(shape, dim, dtype=i32):
    return lax.broadcasted_iota(i32, shape, dim).astype(dtype)


def hot(condition):
    return jnp.where(condition, 1.0, 0.0).astype(bf16)


def dot(left, right):
    return lax.dot_general(left, right, (((1,), (0,)), ((), ())), preferred_element_type=f32)


def dot_cols(left, right):
    return lax.dot_general(left, right, (((1,), (1,)), ((), ())), preferred_element_type=f32)


def split(value):
    high = value.astype(bf16)
    rest = value - high.astype(f32)
    middle = rest.astype(bf16)
    low = (rest - middle.astype(f32)).astype(bf16)
    return (high, middle, low)


def run(body, outs, args, smem=(), scratch=(), flops=0, moved=0, vmem=56, outside=()):
    return pl.pallas_call(
        body,
        out_shape=[jax.ShapeDtypeStruct(shape, dtype) for shape, dtype in outs],
        in_specs=[
            pl.BlockSpec(
                memory_space=pltpu.SMEM if i in smem else pl.ANY if i in outside else pltpu.VMEM
            )
            for i in range(len(args))
        ],
        out_specs=[pl.BlockSpec(memory_space=pltpu.VMEM) for unused in outs],
        scratch_shapes=list(scratch),
        compiler_params=pltpu.CompilerParams(vmem_limit_bytes=vmem << 20),
        cost_estimate=pl.CostEstimate(flops=flops, bytes_accessed=moved, transcendentals=0),
    )(*args)


def block_of(total, limit):
    return max(b for b in range(16, limit + 1, 16) if total % b == 0)


def by_rows(total, block, body, init=0):
    def step(i, carry):
        return body(pl.ds(pl.multiple_of(i * block, block), block), carry)

    return lax.fori_loop(0, total // block, step, init)


def fold(values, combine):
    parts = values.reshape(values.shape[0] // 8, 8, values.shape[1])
    return functools.reduce(combine, [parts[k] for k in range(parts.shape[0])])


def column_of(row):
    return jnp.broadcast_to(row, (128, row.shape[1])).T[:, :1]


def route_kernel(
    cap,
    local_rows,
    grps,
    item_owner_ref,
    item_row_ref,
    tgt_owner_ref,
    tgt_row_ref,
    valid_ref,
    wanted_ref,
    place_ref,
    column_ref,
    rank_ref,
    dest_ref,
    local_ref,
):
    devices, width = wanted_ref.shape
    asks = dest_ref.shape[1]
    owner = jnp.concatenate([item_owner_ref[...], tgt_owner_ref[...]], axis=1).astype(f32)
    row = jnp.concatenate([item_row_ref[...], tgt_row_ref[...]], axis=1).astype(f32)
    part = jnp.zeros((1, asks), f32)
    for g in range(1, grps):
        part = part + jnp.where(row >= g * local_rows, 1.0, 0.0)
    dest = part * (devices // grps) + owner
    local = row - part * local_rows
    dest_ref[...] = dest.astype(i32)
    local_ref[...] = local.astype(i32)
    named = jnp.where(iota((devices, asks), 0, f32) == dest, 1.0, 0.0)
    count = jnp.sum(named, axis=1, keepdims=True)
    count_row = jnp.broadcast_to(count, (devices, 128)).T[:1, :]
    below = jnp.where(iota((devices, devices), 1) < iota((devices, devices), 0), 1.0, 0.0)
    before = jnp.sum(below * count_row, axis=1, keepdims=True)
    room = jnp.sum(named * jnp.maximum(cap - count, 0.0), axis=0, keepdims=True)
    item = (dest * local_rows + local).astype(i32)
    key = item * 2048 + iota((1, asks), 1)
    key_col = column_of(dest * local_rows + local).astype(i32) * 2048 + iota((asks, 1), 0)
    rank = jnp.sum(jnp.where(key_col < key, 1.0, 0.0), axis=0, keepdims=True)
    rank = rank - jnp.sum(named * before, axis=0, keepdims=True)
    lead = jnp.floor(local * (cap / local_rows)) - rank + dest * 4096.0
    lead = jnp.where(key_col <= key, column_of(lead), 0.0)
    lead = jnp.max(lead, axis=0, keepdims=True) - dest * 4096.0
    slot = rank + jnp.minimum(lead, room)
    spot = iota((width, asks), 0, f32)
    at_spot = hot((spot == slot) & (rank < cap))
    high = jnp.floor((local + 1.0) * (1.0 / 64.0))
    low = local + 1.0 - high * 64.0
    ids = dot_cols((named * high).astype(bf16), at_spot) * 64.0 + dot_cols(
        (named * low).astype(bf16), at_spot
    )
    lane = iota((devices, width), 1, f32)
    most = jnp.max(count, axis=0, keepdims=True)
    flags = jnp.sum(valid_ref[...].astype(f32), axis=1, keepdims=True)
    ids = ids - 1.0
    ids = jnp.where(lane == cap, count, ids)
    ids = jnp.where(lane == cap + 1, most, ids)
    ids = jnp.where(lane == cap + 2, flags, ids)
    wanted_ref[...] = ids.astype(i32)
    place = jnp.where(rank < cap, dest * cap + slot, -1.0)
    place_ref[...] = place.astype(i32)
    rank_ref[...] = rank.astype(i32)
    column_ref[...] = column_of(place).astype(i32)


def low_kernel(attn_ref, ffn_ref, pos_ref, small_ref, out_ref):
    small_at = out_ref.shape[2] - SMALL
    rows = attn_ref.shape[0]
    tail = jnp.concatenate([small_ref[...], jnp.zeros((rows, SMALL - NSMALL), f32)], axis=1)
    for g in range(out_ref.shape[0]):
        out_ref[g, :, :ATTN] = attn_ref[...].astype(bf16)
        out_ref[g, :, ATTN:TABLES] = ffn_ref[...].astype(bf16)
        out_ref[g, :, TABLES:small_at] = pos_ref[...].astype(bf16)
        out_ref[g, :, small_at:] = tail.astype(bf16)


def lower_table_kernel(table_ref, low_ref, token_ref, held_ref, sems):
    count = table_ref.shape[0]
    edges = [count * k // 32 * 8 for k in range(4)] + [count]
    copies = []
    for k in range(4):
        part = pl.ds(edges[k], edges[k + 1] - edges[k])
        copies.append(pltpu.make_async_copy(table_ref.at[part], held_ref.at[part], sems.at[k]))
        copies[k].start()
    for k in range(4):
        copies[k].wait()
        part = slice(edges[k], edges[k + 1])
        low_ref[part, :] = held_ref[part, :].astype(bf16)
    spare = low_ref.shape[0] - count
    if spare:
        low_ref[count:, :] = jnp.zeros((spare, D), bf16)
    token_ref[...] = jnp.zeros(token_ref.shape, f32)


def lower_table(table):
    count = table.shape[0]
    return pl.pallas_call(
        lower_table_kernel,
        out_shape=[
            pltpu.VMEM((CHUNK * math.ceil(count / CHUNK), D), bf16),
            jax.ShapeDtypeStruct((8, 128), f32),
        ],
        in_specs=[pl.BlockSpec(memory_space=pl.ANY)],
        out_specs=[pl.BlockSpec(memory_space=pltpu.VMEM)] * 2,
        scratch_shapes=[pltpu.VMEM((count, D), f32), pltpu.SemaphoreType.DMA((4,))],
        compiler_params=pltpu.CompilerParams(vmem_limit_bytes=16 << 20),
        cost_estimate=pl.CostEstimate(flops=0, bytes_accessed=6 * count * D, transcendentals=0),
    )(pltpu.with_memory_space_constraint(table, pltpu.HBM))


def lookup_kernel(cap, local_rows, asked_ref, token_ref, low_ref, rows_ref, ids_ref, total_ref):
    del token_ref
    devices, width = asked_ref.shape
    chunk = CHUNK
    turned = asked_ref[...].astype(f32).T
    slot = iota((16, devices), 0)
    for j in range(cap // 16):
        part = turned[16 * j : 16 * (j + 1), :]
        for n in range(devices):
            ids_ref[16 * n : 16 * (n + 1), :] = jnp.broadcast_to(part[:, n : n + 1], (16, 128))
        first = jnp.min(jnp.where(part >= 0.0, part, float(local_rows))).astype(i32)
        last = jnp.max(part).astype(i32)
        total_ref[...] = jnp.zeros(total_ref.shape, f32)

        def one_chunk(c, carry):
            begin = pl.multiple_of(c * chunk, chunk)
            ids = ids_ref[...] - (c * chunk).astype(f32)
            near = jnp.concatenate(
                [hot(ids == iota((1, 128), 1, f32) + 128.0 * k) for k in range(chunk // 128)],
                axis=1,
            )
            total_ref[...] += dot(near, low_ref[pl.ds(begin, chunk), :])
            return carry

        lax.fori_loop(first // chunk, last // chunk + 1, one_chunk, 0)
        for n in range(devices):
            rows_ref[n, 16 * j : 16 * (j + 1), :] = total_ref[16 * n : 16 * (n + 1), :].astype(bf16)


def rows_of(found_ref, place):
    total = found_ref.shape[0]
    return dot(hot(place == iota((place.shape[0], total), 1)), found_ref[...])


def extract_targets_kernel(found_ref, column_ref, corr_ref, target_ref):
    queries = corr_ref.shape[1]
    rows = rows_of(found_ref, column_ref[column_ref.shape[0] - queries :, :])
    for g in range(target_ref.shape[0]):
        target_ref[g, :queries, :] = rows.astype(bf16)
        target_ref[g, queries:, :] = corr_ref[...]


def extract_items_kernel(found_ref, column_ref, patch_ref, item_ref):
    def items(part, carry):
        place = column_ref[part, :]
        rows = rows_of(found_ref, place)
        item_ref[part, :] = jnp.where(place < 0, patch_ref[part, :].astype(f32), rows).astype(bf16)
        return carry

    by_rows(item_ref.shape[0], 256, items)


def centred(values):
    centre = values - jnp.mean(values, axis=-1, keepdims=True)
    spread = jnp.mean(centre * centre, axis=-1, keepdims=True)
    scale = lax.rsqrt(spread + norm_eps)
    return (centre * scale, scale)


def norm_back(grad, unit, scale, gain):
    inner = grad * gain
    return scale * (
        inner
        - jnp.mean(inner, axis=-1, keepdims=True)
        - unit * jnp.mean(inner * unit, axis=-1, keepdims=True)
    )


def total_of(values):
    return jnp.sum(values, axis=0, keepdims=True)


def places_of(seg):
    slots = seg.shape[0]
    lane = iota((slots, 128), 1)
    below = jnp.sum(jnp.where(seg < lane, 1.0, 0.0), axis=0, keepdims=True)
    start = jnp.sum(jnp.where(seg == lane, below, 0.0), axis=1, keepdims=True)
    return iota((slots, 1), 0) - start.astype(i32)


def small_rows(dense_ref, begin):
    return dense_ref[:, begin:].astype(f32).T


def mask_bias(seg, slots_q):
    shape = (seg.shape[0], slots_q.shape[1])
    slot = iota(shape, 0)
    wide = seg.astype(f32)
    seg_q = jnp.sum(jnp.where(slot == slots_q, wide, 0.0), axis=0, keepdims=True)
    return jnp.where((wide == seg_q) & (slot <= slots_q), 0.0, negative)


def prepare_kernel(
    seg_ref,
    slot_row_ref,
    slot_col_ref,
    dense_ref,
    freq_ref,
    logfreq_ref,
    pos_ref,
    pos_hot_t_ref,
    pos_q_ref,
    bias_ref,
    choose_ref,
    corr_ref,
):
    slots = seg_ref.shape[0]
    queries = slot_row_ref.shape[1]
    maxlen = pos_hot_t_ref.shape[0]
    pos = dense_ref[:, TABLES : TABLES + maxlen]
    seg = seg_ref[...]
    places = places_of(seg)
    pos_hot = hot(places == iota((slots, maxlen), 1))
    places_row = jnp.broadcast_to(places.astype(f32), (slots, 128)).T[:1]
    pos_hot_t_ref[...] = hot(places_row == iota((maxlen, slots), 0, f32))
    pos_ref[...] = dot_cols(pos_hot, pos)
    choose = hot(slot_col_ref[...] == iota((queries, slots), 1))
    choose_ref[...] = choose
    pos_q_ref[...] = dot(choose, pos_ref[...].astype(bf16))
    bias_ref[...] = mask_bias(seg, slot_row_ref[...])
    entries = logfreq_ref.shape[1]
    corr = dot(logfreq_ref[...], hot(iota((entries, queries), 0) == freq_ref[...]))
    corr_ref[...] = jnp.broadcast_to(corr, (META, queries)).astype(bf16)


def forward_kernel(
    item_ref,
    pos_ref,
    pos_q_ref,
    bias_ref,
    choose_ref,
    dense_ref,
    query_ref,
    first_ref,
    normed_ref,
    kv_ref,
    q_ref,
    mixed_ref,
    lse_ref,
    second_ref,
    normed_b_ref,
    active_ref,
    third_ref,
    value_t_ref,
    mixed_t_ref,
):
    small_at = dense_ref.shape[1] - SMALL
    rows = small_rows(dense_ref, small_at)
    first = item_ref[...].astype(f32) + pos_ref[...]
    first_ref[...] = first
    unit, unused = centred(first)
    normed_ref[...] = (unit * rows[0:1] + rows[1:2]).astype(bf16)
    normed = normed_ref[...]
    kv_ref[...] = dot(normed, dense_ref[:, D:QKV]).astype(bf16)
    choose = choose_ref[...]
    normed_q = dot(choose, normed).astype(bf16)
    q_ref[...] = dot(normed_q, dense_ref[:, :D]).astype(bf16)
    first_q = dot(choose, item_ref[...]) + pos_q_ref[...]
    value_t_ref[...] = kv_ref[:, D:].T

    def one_head(h, carry):
        own = iota((1, D), 1) // HEAD == h
        q_own = jnp.where(own, q_ref[...].astype(f32) * score_scale, 0.0).astype(bf16)
        scores = dot_cols(kv_ref[:, :D], q_own) + bias_ref[...]
        top = jnp.max(scores, axis=0, keepdims=True)
        weight = jnp.exp(scores - top)
        total = jnp.sum(weight, axis=0, keepdims=True)
        lse_ref[pl.ds(h, 1), :] = top + jnp.log(total)
        part = pl.ds(pl.multiple_of(h * HEAD, HEAD), HEAD)
        mixed_t_ref[part, :] = dot(value_t_ref[part, :], (weight * (1.0 / total)).astype(bf16))
        return carry

    lax.fori_loop(0, HEADS, one_head, 0)
    mixed = mixed_t_ref[...].T.astype(bf16)
    mixed_ref[...] = mixed
    second = first_q + dot(mixed, dense_ref[:, QKV:ATTN])
    second_ref[...] = second
    unit, unused = centred(second)
    normed_b = (unit * rows[2:3] + rows[3:4]).astype(bf16)
    normed_b_ref[...] = normed_b
    up_bias = jnp.concatenate([rows[7 + k : 8 + k] for k in range(FF // D)], axis=1)
    hidden = dot(normed_b, dense_ref[:, ATTN:DOWN]) + up_bias
    active = jnp.maximum(hidden, 0.0).astype(bf16)
    active_ref[...] = active
    third = second + dot_cols(active, dense_ref[:, DOWN:TABLES]) + rows[6:7]
    third_ref[...] = third
    unit, unused = centred(third)
    query_ref[...] = (unit * rows[4:5] + rows[5:6]).astype(bf16)


def columns_of(target_ref, queries):
    grps = target_ref.shape[0]
    return jnp.concatenate(
        [target_ref[g, queries : queries + 1, :].astype(f32) for g in range(grps)]
        + [jnp.zeros((128 - grps, queries), f32)],
        axis=0,
    ).T


def block_at(index, size):
    return pl.ds(pl.multiple_of(index * size, size), size)


def totals_kernel(
    where_ref,
    query_ref,
    target_ref,
    own_ref,
    valid_ref,
    *refs,
):
    out_refs, (tail_ref, target_t_ref, corr_ref, hold_ref) = refs[:-4], refs[-4:]
    owners = len(out_refs)
    height = tail_ref.shape[0]
    own_g, me = where_ref[0, 0], where_ref[0, 1]
    queries = query_ref.shape[0] // owners
    grps = target_ref.shape[0]
    corr_ref[...] = columns_of(target_ref, queries)

    for g in range(grps):
        target_t_ref[:, g * queries : (g + 1) * queries] = target_ref[g, :queries, :].T

    def one_owner(r):
        query = query_ref[block_at(me ^ r, queries), :].astype(f32)
        query = (query * logit_scale).astype(bf16)
        logits = [
            dot_cols(target_ref[g, :queries, :], query) - corr_ref[:, g : g + 1]
            for g in range(grps)
        ]
        top = functools.reduce(jnp.maximum, [jnp.max(x, axis=0, keepdims=True) for x in logits])
        total = jnp.zeros((1, queries), f32)
        mixed = jnp.zeros((D, queries), f32)
        for g in range(grps):
            weight = jnp.exp(logits[g] - top)
            total = total + jnp.sum(weight, axis=0, keepdims=True)
            mixed = mixed + dot(
                target_t_ref[:, g * queries : (g + 1) * queries], weight.astype(bf16)
            )
        return (top, total, mixed)

    tops, totals = [], []
    if grps > 8:

        def hold(r, carry):
            top, total, mixed = one_owner(r)
            hold_ref[r, :D, :] = mixed
            hold_ref[r, D : D + 8, :] = jnp.broadcast_to(top, (8, queries))
            hold_ref[r, D + 8 :, :] = jnp.broadcast_to(total, (8, queries))
            return carry

        lax.fori_loop(0, owners, hold, 0)
        for r in range(owners):
            out_refs[r][...] = hold_ref[r, :D, :].astype(bf16)
            tops.append(hold_ref[r, D : D + 1, :])
            totals.append(hold_ref[r, D + 8 : D + 9, :])
    else:
        for r in range(owners):
            top, total, mixed = one_owner(r)
            out_refs[r][...] = mixed.astype(bf16)
            tops.append(top)
            totals.append(total)

    product = own_ref[...].astype(f32) * target_ref[own_g, :queries, :].astype(f32)
    own = jnp.sum(product.T, axis=0, keepdims=True) * logit_scale
    own = own - target_ref[own_g, queries : queries + 1, :].astype(f32)
    pieces = [p for x in tops + totals + [own, valid_ref[...].astype(f32)] for p in split(x)]
    fill = jnp.zeros((height - len(pieces), queries), f32)
    tail_ref[...] = jnp.concatenate([x.astype(f32) for x in pieces] + [fill], axis=0).astype(bf16)


def piece(tail, k):
    return tail[3 * k : 3 * k + 1] + tail[3 * k + 1 : 3 * k + 2] + tail[3 * k + 2 : 3 * k + 3]


def backward_dense_kernel(
    owners,
    sums_ref,
    target_ref,
    valid_ref,
    total_ref,
    dense_ref,
    mixed_ref,
    second_ref,
    normed_b_ref,
    active_ref,
    third_ref,
    *refs,
):
    parts_refs = refs[:owners]
    grads_ref, proj_ref, grad_second_ref, grad_o_ref, columns_ref = refs[owners:]
    queries = valid_ref.shape[1]
    small_at = dense_ref.shape[1] - SMALL
    rows = small_rows(dense_ref, small_at)
    sums = sums_ref[...]
    tops = [sums[2 * r : 2 * r + 1] for r in range(owners)]
    totals = [sums[2 * r + 1 : 2 * r + 2] for r in range(owners)]
    top = functools.reduce(jnp.maximum, tops)
    scales = [jnp.exp(x - top) for x in tops]
    total = sum(x * y for x, y in zip(scales, totals))
    weight = valid_ref[...].astype(f32) / total_ref[0, 0]
    mean_t = jnp.zeros((D, queries), f32)
    for r in range(owners):
        mean_t = mean_t + parts_refs[r][...].astype(f32) * (scales[r] / total)
    target = target_ref[0, :queries, :].astype(f32)
    grad_query = ((mean_t - target.T) * (weight * logit_scale)).T

    unit, scale = centred(third_ref[...])
    grad_third = norm_back(grad_query, unit, scale, rows[4:5])
    gain_f, shift_f = total_of(grad_query * unit), total_of(grad_query)
    grad_f = grad_third.astype(bf16)
    active = active_ref[...]
    grads_ref[:, FF:] = dot(grad_f.T, active).astype(bf16)
    down_bias = total_of(grad_f.astype(f32))
    grad_active = dot(grad_f, dense_ref[:, DOWN:TABLES])
    grad_hidden = jnp.where(active.astype(f32) > 0.0, grad_active, 0.0).astype(bf16)
    grads_ref[:, :FF] = dot(normed_b_ref[...].T, grad_hidden).astype(bf16)
    up_bias = total_of(grad_hidden.astype(f32))
    grad_b = dot_cols(grad_hidden, dense_ref[:, ATTN:DOWN])
    unit, scale = centred(second_ref[...])
    grad_second = grad_third + norm_back(grad_b, unit, scale, rows[2:3])
    gain_b, shift_b = total_of(grad_b * unit), total_of(grad_b)
    grad_second_ref[...] = grad_second
    grad_y = grad_second.astype(bf16)
    proj_ref[...] = dot(mixed_ref[...].T, grad_y).astype(bf16)
    grad_o_ref[...] = dot_cols(grad_y, dense_ref[:, QKV:ATTN]).astype(bf16)
    columns = [gain_b, shift_b, gain_f, shift_f, down_bias]
    columns += [up_bias[:, k * D : (k + 1) * D] for k in range(FF // D)]
    columns_ref[...] = jnp.concatenate(
        columns + [jnp.zeros((META - len(columns), D), f32)], axis=0
    )


def backward_kernel(
    proj_ref,
    grad_second_ref,
    grad_o_ref,
    columns_ref,
    slot_row_ref,
    dense_ref,
    bias_ref,
    pos_hot_t_ref,
    first_ref,
    normed_t_ref,
    key_t_ref,
    kv_ref,
    q_ref,
    lse_ref,
    grad_first_ref,
    grads_ref,
    grad_q_t_ref,
    probs_ref,
    grad_s_ref,
    stack_ref,
    p_ref,
    dp_ref,
    joined_ref,
    grad_a_ref,
    base_ref,
    halves_ref,
):
    slots, queries = bias_ref.shape
    maxlen = pos_hot_t_ref.shape[0]
    small_at = dense_ref.shape[1] - SMALL
    rows = small_rows(dense_ref, small_at)

    def one_head(h, carry):
        own = iota((1, D), 1) // HEAD == h
        q_own = jnp.where(own, q_ref[...].astype(f32), 0.0)
        stack_ref[0, pl.ds(pl.multiple_of(h * queries, queries), queries), :] = q_own.astype(bf16)
        o_own = jnp.where(own, grad_o_ref[...].astype(f32), 0.0).astype(bf16)
        stack_ref[1, pl.ds(pl.multiple_of(h * queries, queries), queries), :] = o_own
        columns = pl.ds(pl.multiple_of(h * queries, queries), queries)
        scores = dot_cols(kv_ref[:, :D], (q_own * score_scale).astype(bf16)) + bias_ref[...]
        probs = jnp.exp(scores - lse_ref[pl.ds(h, 1), :])
        p_ref[...] = probs
        probs_ref[:, columns] = probs.astype(bf16)
        grad_p = dot_cols(kv_ref[:, D:], o_own)
        dp_ref[...] = grad_p
        inner = jnp.sum(p_ref[...] * grad_p, axis=0, keepdims=True)
        grad_s_ref[:, columns] = (p_ref[...] * (dp_ref[...] - inner)).astype(bf16)
        part = pl.ds(pl.multiple_of(h * HEAD, HEAD), HEAD)
        grad_q_t_ref[part, :] = dot(key_t_ref[part, :], grad_s_ref[:, columns])
        return carry

    lax.fori_loop(0, HEADS, one_head, 0)
    grad_q = (grad_q_t_ref[...].T * score_scale).astype(bf16)
    spread = hot(iota((slots, queries), 0) == slot_row_ref[...])
    joined_ref[:, :D] = dot(spread, grad_q).astype(bf16)
    joined_ref[:, D : 2 * D] = (dot(grad_s_ref[...], stack_ref[0]) * score_scale).astype(bf16)
    joined_ref[:, 2 * D :] = dot(probs_ref[...], stack_ref[1]).astype(bf16)
    grads_ref[:, :QKV] = dot(normed_t_ref[...], joined_ref[...]).astype(bf16)
    grads_ref[:, QKV:ATTN] = proj_ref[...]
    grad_a_ref[...] = dot_cols(joined_ref[...], dense_ref[:, :QKV])
    high, middle, unused = split(grad_second_ref[...])
    base_ref[...] = dot(spread, high) + dot(spread, middle)

    grad_a = grad_a_ref[...]
    unit, scale = centred(first_ref[...])
    grad_first = base_ref[...] + norm_back(grad_a, unit, scale, rows[0:1])
    grad_first_ref[...] = grad_first.astype(bf16)
    high, middle, unused = split(grad_first)
    halves_ref[:, :D] = high
    halves_ref[:, D:] = middle
    gain_a, shift_a = total_of(grad_a * unit), total_of(grad_a)
    both = dot(pos_hot_t_ref[...], halves_ref[...])
    grads_ref[:, ATTN : ATTN + maxlen] = (both[:, :D] + both[:, D:]).T.astype(bf16)
    columns = jnp.concatenate(
        [gain_a, shift_a, columns_ref[: NSMALL - 2]]
        + [jnp.zeros((SMALL - NSMALL, D), f32)],
        axis=0,
    )
    grads_ref[:, ATTN + maxlen :] = columns.T.astype(bf16)


def target_grad_kernel(owners, where_ref, total_ref, query_ref, target_ref, early_ref, *refs):
    del early_ref
    tail_refs, (out_ref, sums_ref, corr_ref) = refs[:owners], refs[owners:]
    grps = target_ref.shape[0]
    queries = query_ref.shape[0] // owners
    corr_ref[...] = columns_of(target_ref, queries)
    same = jnp.where(iota((queries, queries), 0) == iota((queries, queries), 1), 1.0, 0.0)
    own_g, me = where_ref[0, 0], where_ref[0, 1]
    tails = [ref[...].astype(f32) for ref in tail_refs]
    log_totals, weights = [], []
    loss = jnp.zeros((1, queries), f32)
    for r in range(owners):
        tops = [piece(tails[k], k ^ r) for k in range(owners)]
        totals = [piece(tails[k], owners + (k ^ r)) for k in range(owners)]
        top = functools.reduce(jnp.maximum, tops)
        total = functools.reduce(
            jnp.add, [totals[k] * jnp.exp(tops[k] - top) for k in range(owners)]
        )
        log_totals.append(top + jnp.log(total))
        weights.append(piece(tails[r], 2 * owners + 1) / total_ref[0, 0])
        loss = loss + weights[r] * (log_totals[r] - piece(tails[r], 2 * owners))
        if r == 0:
            sums_ref[...] = jnp.concatenate(
                [x for pair in zip(tops, totals) for x in pair], axis=0
            )
    loss = jnp.sum(loss, axis=1, keepdims=True)
    pieces = split(jnp.broadcast_to(loss, (1, queries)))
    tail = jnp.concatenate(
        [x.astype(f32) for x in pieces] + [jnp.zeros((META - len(pieces), queries), f32)], axis=0
    ).astype(bf16)
    for g in range(grps):
        target = target_ref[g, :queries, :]
        grad = jnp.zeros((queries, D), f32)
        for r in range(owners):
            query = query_ref[block_at(me ^ r, queries), :]
            logits = dot_cols(target, query) * logit_scale - corr_ref[:, g : g + 1]
            probs = jnp.exp(logits - log_totals[r])
            if r == 0:
                probs = probs - jnp.where(own_g == g, 1.0, 0.0) * same
            coeff = weights[r] * probs
            grad = grad + dot(coeff.astype(bf16), query)
        out_ref[g, :queries, :] = grad.astype(bf16)
        out_ref[g, queries:, :] = tail


def turn_kernel(normed_ref, kv_ref, normed_t_ref, key_t_ref):
    normed_t_ref[...] = normed_ref[...].T
    key_t_ref[...] = kv_ref[:, :D].T


def send_kernel(
    grad_first_ref, parts_ref, place_ref, sent_ref, both_ref, loss_ref
):
    grps, height, unused = parts_ref.shape
    slots = grad_first_ref.shape[0]
    queries = height - META
    both_ref[:slots, :] = grad_first_ref[...]
    total = parts_ref[0, :queries, :].astype(f32)
    for g in range(1, grps):
        total = total + parts_ref[g, :queries, :].astype(f32)
    both_ref[slots:, :] = (total * logit_scale).astype(bf16)
    loss = parts_ref[0, queries : queries + 8, :].astype(f32)
    for g in range(1, grps):
        loss = loss + parts_ref[g, queries : queries + 8, :].astype(f32)
    loss_ref[...] = jnp.sum(loss[:, :1], axis=0, keepdims=True)
    asks = both_ref.shape[0]
    block = block_of(sent_ref.shape[0], 2048)

    def one_block(i, carry):
        begin = pl.multiple_of(i * block, block)
        spread = hot(place_ref[...] - begin == iota((block, asks), 0))
        sent_ref[pl.ds(begin, block), :] = dot(spread, both_ref[...]).astype(bf16)
        return carry

    lax.fori_loop(0, sent_ref.shape[0] // block, one_block, 0)


def advance(weight, moment, average, grad, rate):
    moment_new = momentum_rate * moment + grad
    weight_new = weight - rate * (grad + momentum_rate * moment_new)
    average_new = average_rate * average + (1.0 - average_rate) * weight_new
    return (weight_new, moment_new, average_new, weight_new.astype(bf16))


def update_kernel(
    rate,
    rows,
    span_ref,
    ids_ref,
    recv_ref,
    extra_ref,
    w_ref,
    m_ref,
    a_ref,
    w_out_ref,
    m_out_ref,
    a_out_ref,
    copy_out_ref,
    w_held,
    m_held,
    a_held,
    copy_held,
    tiles_ref,
    grad_ref,
    in_sems,
    out_sems,
    extra_sem,
):
    count = w_ref.shape[0]
    devices, cap, unused = recv_ref.shape
    tiles = cap // 16
    edges = list(range(0, count, rows)) + [count]
    parts = [(k, edges[k], edges[k + 1] - edges[k]) for k in range(len(edges) - 1)]

    def copy_in(k, begin, size, j):
        source, target = ((w_ref, w_held), (m_ref, m_held), (a_ref, a_held))[j]
        part = pl.ds(begin, size)
        return pltpu.make_async_copy(source.at[part], target.at[part], in_sems.at[j, k])

    def copy_out(k, begin, size, j):
        pairs = (
            (w_held, w_out_ref),
            (m_held, m_out_ref),
            (a_held, a_out_ref),
            (copy_held, copy_out_ref),
        )
        source, target = pairs[j]
        part = pl.ds(begin, size)
        return pltpu.make_async_copy(source.at[part], target.at[part], out_sems.at[j, k])

    for part in parts:
        for j in range(3):
            copy_in(*part, j).start()
    for j in range(tiles):
        for n in range(devices):
            tiles_ref[j, 16 * n : 16 * (n + 1), :] = recv_ref[n, 16 * j : 16 * (j + 1), :]

    for k, begin, size in parts:
        here = pl.ds(0, size)
        grad_ref[here, :] = jnp.zeros((size, D), f32)

        @pl.when(span_ref[0] > 1)
        def start_from_extra():
            copy = pltpu.make_async_copy(
                extra_ref.at[pl.ds(begin, size)], grad_ref.at[here], extra_sem
            )
            copy.start()
            copy.wait()

        for j in range(tiles):

            @pl.when((span_ref[1 + 2 * j] < begin + size) & (span_ref[2 + 2 * j] >= begin))
            def add():
                spread = hot(ids_ref[j : j + 1, :] - begin == iota((size, ids_ref.shape[1]), 0))
                grad_ref[here, :] += dot(spread, tiles_ref[j])

        for j in range(3):
            copy_in(k, begin, size, j).wait()
        part = pl.ds(begin, size)
        new = advance(w_held[part, :], m_held[part, :], a_held[part, :], grad_ref[here, :], rate)
        w_held[part, :], m_held[part, :], a_held[part, :], copy_held[part, :] = new
        for j in range(4):
            copy_out(k, begin, size, j).start()
    for part in parts:
        for j in range(4):
            copy_out(*part, j).wait()


def update_table(span, ids, recv, extra, table_w, table_m, table_a, rate):
    count = table_w.shape[0]
    rows = min(784, count)
    blocks = math.ceil(count / rows)
    devices, cap, unused = recv.shape
    anywhere = pl.BlockSpec(memory_space=pl.ANY)
    inside = pl.BlockSpec(memory_space=pltpu.VMEM)
    tables = [pltpu.with_memory_space_constraint(x, pltpu.HBM) for x in (table_w, table_m, table_a)]
    return tuple(
        pl.pallas_call(
            functools.partial(update_kernel, rate, rows),
            in_specs=[pl.BlockSpec(memory_space=pltpu.SMEM), inside, inside] + [anywhere] * 4,
            out_specs=[anywhere] * 4,
            scratch_shapes=[pltpu.VMEM((count, D), f32)] * 3
            + [
                pltpu.VMEM((count, D), bf16),
                pltpu.VMEM((cap // 16, 16 * devices, D), bf16),
                pltpu.VMEM((rows, D), f32),
                pltpu.SemaphoreType.DMA((3, blocks)),
                pltpu.SemaphoreType.DMA((4, blocks)),
                pltpu.SemaphoreType.DMA(()),
            ],
            out_shape=[jax.ShapeDtypeStruct((count, D), f32)] * 3
            + [jax.ShapeDtypeStruct((count, D), bf16)],
            compiler_params=pltpu.CompilerParams(vmem_limit_bytes=56 << 20),
            cost_estimate=pl.CostEstimate(
                flops=count * devices * cap * D, bytes_accessed=26 * count * D, transcendentals=0
            ),
        )(span, ids, recv, extra, *tables)
    )


def update_dense_kernel(rates, widths, parts_ref, *refs):
    ins, outs = refs[: 3 * len(widths)], refs[3 * len(widths) :]
    grad = parts_ref[0].astype(f32)
    for g in range(1, parts_ref.shape[0]):
        grad = grad + parts_ref[g].astype(f32)
    begin = 0
    for k, (rate, width) in enumerate(zip(rates, widths)):
        w_ref, m_ref, a_ref = ins[3 * k : 3 * k + 3]
        here = grad[:, begin : begin + width][:, : w_ref.shape[1]]
        new = advance(w_ref[...], m_ref[...], a_ref[...], here, rate)
        for j in range(4):
            outs[4 * k + j][...] = new[j]
        begin += width


def blank_kernel(seed_ref, out_ref):
    del seed_ref, out_ref


def blank_of(shape, dtype, seed):
    return pl.pallas_call(
        blank_kernel,
        out_shape=jax.ShapeDtypeStruct(shape, dtype),
        in_specs=[pl.BlockSpec(memory_space=pl.ANY)],
        out_specs=pl.BlockSpec(memory_space=pl.ANY),
    )(seed)


def everyone(values):
    return lax.all_to_all(values, ("grp", "row"), split_axis=0, concat_axis=0, tiled=True)


def swap(values, axis, bit):
    pairs = [(i, i ^ bit) for i in range(lax.axis_size(axis))]
    return lax.ppermute(values, axis, pairs)


def bits_of(size):
    return [1 << k for k in range(size.bit_length() - 1)]


def after(values, *others):
    return lax.optimization_barrier((values,) + others)[0]


def spread_row(values, bit):
    got = swap(values, "row", bit)
    mine = (lax.axis_index("row") // bit) % 2 == 0
    return jnp.stack([jnp.where(mine, values, got), jnp.where(mine, got, values)], axis=-3)


def sum_row(values, owners):
    for bit in bits_of(owners):
        grps, count, rows, width = values.shape
        pairs = values.reshape(grps, count // 2, 2, rows, width)
        mine = (lax.axis_index("row") // bit) % 2
        keep = lax.dynamic_index_in_dim(pairs, mine, 2, keepdims=False)
        give = lax.dynamic_index_in_dim(pairs, 1 - mine, 2, keepdims=False)
        values = (keep.astype(f32) + swap(give, "row", bit).astype(f32)).astype(bf16)
    return values.reshape(grps, rows, width)


def local(
    item_owner,
    item_row,
    seg,
    query_slot,
    tgt_owner,
    tgt_row,
    freq_idx,
    valid,
    logfreq,
    table_w,
    table_m,
    table_a,
    attn_w,
    attn_m,
    attn_a,
    ffn_w,
    ffn_m,
    ffn_a,
    pos_w,
    pos_m,
    pos_a,
    small_w,
    small_m,
    small_a,
):
    owners = lax.axis_size("row")
    grps = lax.axis_size("grp")
    devices = grps * owners
    local_rows = table_w.shape[0]
    slots = seg.shape[1]
    queries = query_slot.shape[1]
    asks = slots + queries
    total_q = queries * devices
    mean = 2 * asks // devices
    cap = 16 * math.ceil((mean + 3.5 * math.sqrt(mean)) / 16)
    width = 128 * math.ceil((cap + 3) / 128)
    maxlen = pos_w.shape[1]
    own_rows = attn_w.shape[0]
    my_grp, my_row = lax.axis_index("grp"), lax.axis_index("row")

    wanted, place, place_col, rank, dest, local_row = run(
        functools.partial(route_kernel, cap, local_rows, grps),
        [((devices, width), i32), ((1, asks), i32), ((asks, 1), i32)] + [((1, asks), i32)] * 3,
        [
            item_owner.reshape(1, slots),
            item_row,
            tgt_owner.reshape(1, queries),
            tgt_row,
            valid,
        ],
        flops=2 * devices * asks * asks,
    )
    asked = everyone(wanted)
    (dense,) = run(
        low_kernel,
        [((grps, own_rows, TABLES + maxlen + SMALL), bf16)],
        [attn_w, ffn_w, pos_w, after(small_w, wanted)],
        moved=1 << 20,
    )
    low_table, token = lower_table(after(table_w, wanted))
    dense, asked, token = lax.optimization_barrier((dense, asked, token))
    dense = lax.all_to_all(dense, "grp", split_axis=0, concat_axis=0, tiled=True)
    most = jnp.max(asked[:, cap + 1])
    rounds = (most + cap - 1) // cap
    valid_total = jnp.maximum(jnp.sum(asked[:, cap + 2]).astype(f32), 1.0).reshape(1, 1)
    (rows_found,) = run(
        functools.partial(lookup_kernel, cap, local_rows),
        [((devices, cap, D), bf16)],
        [asked, token, low_table],
        scratch=[pltpu.VMEM((16 * devices, 128), f32), pltpu.VMEM((16 * devices, D), f32)],
        moved=8 * local_rows * D,
        vmem=24,
    )
    dense, rows_found = lax.optimization_barrier((dense, rows_found))
    for bit in reversed(bits_of(owners)):
        dense = spread_row(dense, bit)
    dense = dense.reshape(D, -1)
    found = everyone(rows_found).reshape(devices * cap, D)
    ids = asked[:, :cap].reshape(devices, cap // 16, 16).transpose(1, 0, 2)
    ids = ids.reshape(cap // 16, 16 * devices)
    low_end = jnp.min(jnp.where(ids >= 0, ids, local_rows), axis=1)
    span = jnp.stack([low_end, jnp.max(ids, axis=1)], axis=1).reshape(-1)
    span = jnp.concatenate([rounds.reshape(1), span])

    found, ids, span = lax.optimization_barrier((found, ids, span))
    seg_col = seg.reshape(slots, 1)
    slot_col = query_slot.reshape(queries, 1)
    pos_part, pos_hot_t, pos_q, bias, choose, corr = run(
        prepare_kernel,
        [
            ((slots, D), f32),
            ((maxlen, slots), bf16),
            ((queries, D), f32),
            ((slots, queries), f32),
            ((queries, slots), bf16),
            ((META, queries), bf16),
        ],
        [seg_col, query_slot, slot_col, dense, freq_idx, logfreq.reshape(1, -1)],
        flops=1 << 30,
    )
    found = after(found, pos_part)
    (target_emb,) = run(
        extract_targets_kernel,
        [((grps, queries + META, D), bf16)],
        [found, place_col, corr],
        flops=2 * devices * cap * queries * D,
    )
    def wanted_of(k):
        here = rank[0] // cap == k
        spot = jnp.where(here, dest[0] * cap + rank[0] - k * cap, devices * cap)
        ids = jnp.full((devices * cap,), -1, i32).at[spot].set(local_row[0], mode="drop")
        return here, spot, everyone(ids.reshape(devices, cap)).reshape(devices * cap)

    def more_rows(carry):
        k, items, targets = carry
        here, spot, ids = wanted_of(k)
        rows = jnp.where((ids >= 0)[:, None], table_w[jnp.maximum(ids, 0)], 0.0).astype(bf16)
        got = everyone(rows.reshape(devices, cap, D)).reshape(devices * cap, D)
        got = got[jnp.minimum(spot, devices * cap - 1)]
        items = jnp.where(here[:slots, None], got[:slots], items)
        top = jnp.where(here[None, slots:, None], got[None, slots:], targets[:, :queries])
        return (k + 1, items, targets.at[:, :queries].set(top))

    unused, patch, target_emb = lax.while_loop(
        lambda carry: carry[0] < rounds,
        more_rows,
        (jnp.int32(1), blank_of((slots, D), bf16, wanted), target_emb),
    )
    (item_emb,) = run(
        extract_items_kernel,
        [((slots, D), bf16)],
        [after(found, target_emb), place_col, patch],
        flops=2 * devices * cap * slots * D,
    )
    targets = lax.all_to_all(target_emb, "grp", split_axis=0, concat_axis=0, tiled=True)
    query_own, first, normed, kv, q_own, mixed_o, lse, second, normed_b, active, third = run(
        forward_kernel,
        [
            ((queries, D), bf16),
            ((slots, D), f32),
            ((slots, D), bf16),
            ((slots, 2 * D), bf16),
            ((queries, D), bf16),
            ((queries, D), bf16),
            ((HEADS, queries), f32),
            ((queries, D), f32),
            ((queries, D), bf16),
            ((queries, FF), bf16),
            ((queries, D), f32),
        ],
        [item_emb, pos_part, pos_q, bias, choose, dense],
        scratch=[
            pltpu.VMEM((D, slots), bf16),
            pltpu.VMEM((D, queries), f32),
        ],
        flops=6 << 30,
    )
    query_all = lax.all_gather(query_own, "row", axis=0, tiled=True)
    where = jnp.stack([my_grp, my_row]).astype(i32).reshape(1, 2)
    tall = 16 * math.ceil((6 * owners + 6) / 16)
    *mixed, tail = run(
        totals_kernel,
        [((D, queries), bf16)] * owners + [((tall, queries), bf16)],
        [where, query_all, targets, query_own, valid],
        smem=(0,),
        scratch=[
            pltpu.VMEM((D, grps * queries), bf16),
            pltpu.VMEM((queries, 128), f32),
            pltpu.VMEM((owners if grps > 8 else 1, D + META, queries), f32),
        ],
        flops=4 * owners * grps * queries * queries * D,
    )
    tails = [tail] + [swap(tail, "row", k) for k in range(1, owners)]
    mixed = [mixed[0]] + [swap(mixed[k], "row", k) for k in range(1, owners)]
    normed_t, key_t = run(turn_kernel, [((D, slots), bf16)] * 2, [normed, kv], moved=4 << 20)
    target_parts, sums = run(
        functools.partial(target_grad_kernel, owners),
        [((grps, queries + META, D), bf16), ((2 * owners, queries), f32)],
        [
            where,
            valid_total,
            query_all,
            targets,
            normed_t,
        ]
        + tails,
        smem=(0, 1),
        outside=(4,),
        scratch=[pltpu.VMEM((queries, 128), f32)],
        flops=4 * owners * grps * queries * queries * D,
    )
    target_parts, *mixed = lax.optimization_barrier((target_parts, *mixed))
    target_parts = lax.all_to_all(target_parts, "grp", split_axis=0, concat_axis=0, tiled=True)
    grads_ffn, grads_proj, grad_second, grad_o, columns = run(
        functools.partial(backward_dense_kernel, owners),
        [
            ((D, 2 * FF), bf16),
            ((D, D), bf16),
            ((queries, D), f32),
            ((queries, D), bf16),
            ((META, D), f32),
        ],
        [sums, target_emb, valid, valid_total, dense, mixed_o, second, normed_b]
        + [active, third]
        + mixed,
        smem=(3,),
        flops=1 << 30,
    )
    grads_ffn = sum_row(grads_ffn.reshape(grps, owners, own_rows, -1), owners)
    grad_first, grads = run(
        backward_kernel,
        [((slots, D), bf16), ((D, ATTN + maxlen + SMALL), bf16)],
        [grads_proj, grad_second, grad_o, columns, query_slot, dense, bias, pos_hot_t, first]
        + [normed_t, key_t, kv, q_own, lse],
        scratch=[
            pltpu.VMEM((D, queries), f32),
            pltpu.VMEM((slots, HEADS * queries), bf16),
            pltpu.VMEM((slots, HEADS * queries), bf16),
            pltpu.VMEM((2, HEADS * queries, D), bf16),
            pltpu.VMEM((slots, queries), f32),
            pltpu.VMEM((slots, queries), f32),
            pltpu.VMEM((slots, QKV), bf16),
            pltpu.VMEM((slots, D), f32),
            pltpu.VMEM((slots, D), f32),
            pltpu.VMEM((slots, 2 * D), bf16),
        ],
        flops=17 << 30,
    )

    sent, both, loss = run(
        send_kernel,
        [((devices * cap, D), bf16), ((asks, D), bf16), ((1, 1), f32)],
        [grad_first, target_parts, place],
        flops=2 * devices * cap * asks * D,
    )
    received = everyone(sent.reshape(devices, cap, D))
    grads = sum_row(grads.reshape(grps, owners, own_rows, -1), owners)
    grad_own = jnp.concatenate([grads_ffn, grads], axis=-1)
    grad_own, received = lax.optimization_barrier((grad_own, received))
    grad_own = lax.all_to_all(grad_own, "grp", split_axis=0, concat_axis=0, tiled=True)

    rate_table = 4.0 * total_q
    rate_dense = 0.25 * math.sqrt(total_q)
    rate_place = 2.0 * math.sqrt(total_q)
    blank = blank_of((local_rows, D), f32, wanted)

    def more_grads(carry):
        k, total = carry
        here, spot, more_ids = wanted_of(k)
        rows = jnp.zeros((devices * cap, D), bf16).at[spot].set(both, mode="drop")
        rows = everyone(rows.reshape(devices, cap, D)).reshape(devices * cap, D)
        spot = jnp.where(more_ids >= 0, more_ids, local_rows)
        total = jnp.where(k > 1, total, 0.0)
        return (k + 1, total.at[spot].add(rows.astype(f32), mode="drop"))

    unused, extra = lax.while_loop(
        lambda carry: carry[0] < rounds,
        more_grads,
        (jnp.int32(1), blank),
    )
    table_out = update_table(span, ids, received, extra, table_w, table_m, table_a, rate_table)
    held = [
        [ffn_w, ffn_m, ffn_a],
        [attn_w, attn_m, attn_a],
        [pos_w, pos_m, pos_a],
        [small_w, small_m, small_a],
    ]
    dense_out = run(
        functools.partial(
            update_dense_kernel,
            [rate_dense, rate_dense, rate_place, rate_dense],
            [2 * FF, ATTN, maxlen, SMALL],
        ),
        [(x.shape, dtype) for three in held for x, dtype in zip(three + three[:1], [f32] * 3 + [bf16])],
        [grad_own] + [x for three in held for x in three],
    )
    ffn_out, attn_out, pos_out, small_out = [tuple(dense_out[4 * k : 4 * k + 4]) for k in range(4)]
    return (loss.reshape(()),) + table_out + attn_out + ffn_out + pos_out + small_out


def solution(mesh):
    rows = P(("grp", "row"), None)
    table = P(("row", "grp"), None)
    ids = P(("grp", "row"), None, None)
    in_specs = (ids, rows, rows, rows, ids, rows, rows, rows, P()) + (table,) * 3 + (rows,) * 12
    out_specs = (P(),) + (table,) * 4 + (rows,) * 16
    return jax.shard_map(local, mesh=mesh, in_specs=in_specs, out_specs=out_specs, check_vma=False)
```

```python
import functools
import math

import jax
import jax.numpy as jnp
from jax import lax
from jax.experimental import pallas as pl
from jax.experimental.pallas import tpu as pltpu
from jax.sharding import PartitionSpec as P

D = 256
HEADS = 8
HEAD = 32
FF = 1024
QKV = 3 * D
ATTN = 4 * D
DOWN = ATTN + FF
TABLES = ATTN + 2 * FF
NSMALL = 11
SMALL = 128
META = 16
CHUNK = 512

norm_eps = 1e-05
score_scale = 0.125
logit_scale = 0.125
momentum_rate = 0.5
average_rate = 0.5
negative = -1e30
bf16 = jnp.bfloat16
f32 = jnp.float32
i32 = jnp.int32


def iota(shape, dim, dtype=i32):
    return lax.broadcasted_iota(i32, shape, dim).astype(dtype)


def hot(condition):
    return jnp.where(condition, 1.0, 0.0).astype(bf16)


def dot(left, right):
    return lax.dot_general(left, right, (((1,), (0,)), ((), ())), preferred_element_type=f32)


def dot_cols(left, right):
    return lax.dot_general(left, right, (((1,), (1,)), ((), ())), preferred_element_type=f32)


def split(value):
    high = value.astype(bf16)
    rest = value - high.astype(f32)
    middle = rest.astype(bf16)
    low = (rest - middle.astype(f32)).astype(bf16)
    return (high, middle, low)


def run(body, outs, args, smem=(), scratch=(), flops=0, moved=0, vmem=56):
    return pl.pallas_call(
        body,
        out_shape=[jax.ShapeDtypeStruct(shape, dtype) for shape, dtype in outs],
        in_specs=[
            pl.BlockSpec(
                memory_space=pltpu.SMEM if i in smem else pltpu.VMEM
            )
            for i in range(len(args))
        ],
        out_specs=[pl.BlockSpec(memory_space=pltpu.VMEM) for unused in outs],
        scratch_shapes=list(scratch),
        compiler_params=pltpu.CompilerParams(vmem_limit_bytes=vmem << 20),
        cost_estimate=pl.CostEstimate(flops=flops, bytes_accessed=moved, transcendentals=0),
    )(*args)


def block_of(total, limit):
    return max(b for b in range(16, limit + 1, 16) if total % b == 0)


def by_rows(total, block, body, init=0):
    def step(i, carry):
        return body(pl.ds(pl.multiple_of(i * block, block), block), carry)

    return lax.fori_loop(0, total // block, step, init)


def fold(values, combine):
    parts = values.reshape(values.shape[0] // 8, 8, values.shape[1])
    return functools.reduce(combine, [parts[k] for k in range(parts.shape[0])])


def column_of(row):
    return jnp.broadcast_to(row, (128, row.shape[1])).T[:, :1]


def route_kernel(
    cap,
    local_rows,
    grps,
    item_owner_ref,
    item_row_ref,
    tgt_owner_ref,
    tgt_row_ref,
    valid_ref,
    wanted_ref,
    place_ref,
    column_ref,
    rank_ref,
    dest_ref,
    local_ref,
):
    devices, width = wanted_ref.shape
    asks = dest_ref.shape[1]
    owner = jnp.concatenate([item_owner_ref[...], tgt_owner_ref[...]], axis=1).astype(f32)
    row = jnp.concatenate([item_row_ref[...], tgt_row_ref[...]], axis=1).astype(f32)
    part = jnp.zeros((1, asks), f32)
    for g in range(1, grps):
        part = part + jnp.where(row >= g * local_rows, 1.0, 0.0)
    dest = part * (devices // grps) + owner
    local = row - part * local_rows
    dest_ref[...] = dest.astype(i32)
    local_ref[...] = local.astype(i32)
    named = jnp.where(iota((devices, asks), 0, f32) == dest, 1.0, 0.0)
    count = jnp.sum(named, axis=1, keepdims=True)
    count_row = jnp.broadcast_to(count, (devices, 128)).T[:1, :]
    below = jnp.where(iota((devices, devices), 1) < iota((devices, devices), 0), 1.0, 0.0)
    before = jnp.sum(below * count_row, axis=1, keepdims=True)
    room = jnp.sum(named * jnp.maximum(cap - count, 0.0), axis=0, keepdims=True)
    item = (dest * local_rows + local).astype(i32)
    key = item * 2048 + iota((1, asks), 1)
    key_col = column_of(dest * local_rows + local).astype(i32) * 2048 + iota((asks, 1), 0)
    rank = jnp.sum(jnp.where(key_col < key, 1.0, 0.0), axis=0, keepdims=True)
    rank = rank - jnp.sum(named * before, axis=0, keepdims=True)
    lead = jnp.floor(local * (cap / local_rows)) - rank + dest * 4096.0
    lead = jnp.where(key_col <= key, column_of(lead), 0.0)
    lead = jnp.max(lead, axis=0, keepdims=True) - dest * 4096.0
    slot = rank + jnp.minimum(lead, room)
    spot = iota((width, asks), 0, f32)
    at_spot = hot((spot == slot) & (rank < cap))
    high = jnp.floor((local + 1.0) * (1.0 / 64.0))
    low = local + 1.0 - high * 64.0
    ids = dot_cols((named * high).astype(bf16), at_spot) * 64.0 + dot_cols(
        (named * low).astype(bf16), at_spot
    )
    lane = iota((devices, width), 1, f32)
    most = jnp.max(count, axis=0, keepdims=True)
    flags = jnp.sum(valid_ref[...].astype(f32), axis=1, keepdims=True)
    ids = ids - 1.0
    ids = jnp.where(lane == cap, count, ids)
    ids = jnp.where(lane == cap + 1, most, ids)
    ids = jnp.where(lane == cap + 2, flags, ids)
    wanted_ref[...] = ids.astype(i32)
    place = jnp.where(rank < cap, dest * cap + slot, -1.0)
    place_ref[...] = place.astype(i32)
    rank_ref[...] = rank.astype(i32)
    column_ref[...] = column_of(place).astype(i32)


def low_kernel(attn_ref, ffn_ref, pos_ref, small_ref, out_ref):
    small_at = out_ref.shape[2] - SMALL
    rows = attn_ref.shape[0]
    tail = jnp.concatenate([small_ref[...], jnp.zeros((rows, SMALL - NSMALL), f32)], axis=1)
    for g in range(out_ref.shape[0]):
        out_ref[g, :, :ATTN] = attn_ref[...].astype(bf16)
        out_ref[g, :, ATTN:TABLES] = ffn_ref[...].astype(bf16)
        out_ref[g, :, TABLES:small_at] = pos_ref[...].astype(bf16)
        out_ref[g, :, small_at:] = tail.astype(bf16)


def lower_table_kernel(table_ref, low_ref, token_ref, held_ref, sems):
    count = table_ref.shape[0]
    edges = [count * k // 32 * 8 for k in range(4)] + [count]
    copies = []
    for k in range(4):
        part = pl.ds(edges[k], edges[k + 1] - edges[k])
        copies.append(pltpu.make_async_copy(table_ref.at[part], held_ref.at[part], sems.at[k]))
        copies[k].start()
    for k in range(4):
        copies[k].wait()
        part = slice(edges[k], edges[k + 1])
        low_ref[part, :] = held_ref[part, :].astype(bf16)
    spare = low_ref.shape[0] - count
    if spare:
        low_ref[count:, :] = jnp.zeros((spare, D), bf16)
    token_ref[...] = jnp.zeros(token_ref.shape, f32)


def lower_table(table):
    count = table.shape[0]
    return pl.pallas_call(
        lower_table_kernel,
        out_shape=[
            pltpu.VMEM((CHUNK * math.ceil(count / CHUNK), D), bf16),
            jax.ShapeDtypeStruct((8, 128), f32),
        ],
        in_specs=[pl.BlockSpec(memory_space=pl.ANY)],
        out_specs=[pl.BlockSpec(memory_space=pltpu.VMEM)] * 2,
        scratch_shapes=[pltpu.VMEM((count, D), f32), pltpu.SemaphoreType.DMA((4,))],
        compiler_params=pltpu.CompilerParams(vmem_limit_bytes=16 << 20),
        cost_estimate=pl.CostEstimate(flops=0, bytes_accessed=6 * count * D, transcendentals=0),
    )(pltpu.with_memory_space_constraint(table, pltpu.HBM))


def lookup_kernel(cap, local_rows, asked_ref, token_ref, low_ref, rows_ref, ids_ref, total_ref):
    del token_ref
    devices, width = asked_ref.shape
    chunk = CHUNK
    turned = asked_ref[...].astype(f32).T
    slot = iota((16, devices), 0)
    for j in range(cap // 16):
        part = turned[16 * j : 16 * (j + 1), :]
        for n in range(devices):
            ids_ref[16 * n : 16 * (n + 1), :] = jnp.broadcast_to(part[:, n : n + 1], (16, 128))
        first = jnp.min(jnp.where(part >= 0.0, part, float(local_rows))).astype(i32)
        last = jnp.max(part).astype(i32)
        total_ref[...] = jnp.zeros(total_ref.shape, f32)

        def one_chunk(c, carry):
            begin = pl.multiple_of(c * chunk, chunk)
            ids = ids_ref[...] - (c * chunk).astype(f32)
            near = jnp.concatenate(
                [hot(ids == iota((1, 128), 1, f32) + 128.0 * k) for k in range(chunk // 128)],
                axis=1,
            )
            total_ref[...] += dot(near, low_ref[pl.ds(begin, chunk), :])
            return carry

        lax.fori_loop(first // chunk, last // chunk + 1, one_chunk, 0)
        for n in range(devices):
            rows_ref[n, 16 * j : 16 * (j + 1), :] = total_ref[16 * n : 16 * (n + 1), :].astype(bf16)


def rows_of(found_ref, place):
    total = found_ref.shape[0]
    return dot(hot(place == iota((place.shape[0], total), 1)), found_ref[...])


def extract_targets_kernel(found_ref, column_ref, corr_ref, target_ref):
    queries = corr_ref.shape[1]
    rows = rows_of(found_ref, column_ref[column_ref.shape[0] - queries :, :])
    for g in range(target_ref.shape[0]):
        target_ref[g, :queries, :] = rows.astype(bf16)
        target_ref[g, queries:, :] = corr_ref[...]


def extract_items_kernel(found_ref, column_ref, patch_ref, item_ref):
    def items(part, carry):
        place = column_ref[part, :]
        rows = rows_of(found_ref, place)
        item_ref[part, :] = jnp.where(place < 0, patch_ref[part, :].astype(f32), rows).astype(bf16)
        return carry

    by_rows(item_ref.shape[0], 256, items)


def centred(values):
    centre = values - jnp.mean(values, axis=-1, keepdims=True)
    spread = jnp.mean(centre * centre, axis=-1, keepdims=True)
    scale = lax.rsqrt(spread + norm_eps)
    return (centre * scale, scale)


def norm_back(grad, unit, scale, gain):
    inner = grad * gain
    return scale * (
        inner
        - jnp.mean(inner, axis=-1, keepdims=True)
        - unit * jnp.mean(inner * unit, axis=-1, keepdims=True)
    )


def total_of(values):
    return jnp.sum(values, axis=0, keepdims=True)


def places_of(seg):
    slots = seg.shape[0]
    lane = iota((slots, 128), 1)
    below = jnp.sum(jnp.where(seg < lane, 1.0, 0.0), axis=0, keepdims=True)
    start = jnp.sum(jnp.where(seg == lane, below, 0.0), axis=1, keepdims=True)
    return iota((slots, 1), 0) - start.astype(i32)


def small_rows(dense_ref, begin):
    return dense_ref[:, begin:].astype(f32).T


def mask_bias(seg, slots_q):
    shape = (seg.shape[0], slots_q.shape[1])
    slot = iota(shape, 0)
    wide = seg.astype(f32)
    seg_q = jnp.sum(jnp.where(slot == slots_q, wide, 0.0), axis=0, keepdims=True)
    return jnp.where((wide == seg_q) & (slot <= slots_q), 0.0, negative)


def prepare_kernel(
    seg_ref,
    slot_row_ref,
    slot_col_ref,
    dense_ref,
    freq_ref,
    logfreq_ref,
    pos_ref,
    pos_hot_t_ref,
    pos_q_ref,
    bias_ref,
    choose_ref,
    corr_ref,
):
    slots = seg_ref.shape[0]
    queries = slot_row_ref.shape[1]
    maxlen = pos_hot_t_ref.shape[0]
    pos = dense_ref[:, TABLES : TABLES + maxlen]
    seg = seg_ref[...]
    places = places_of(seg)
    pos_hot = hot(places == iota((slots, maxlen), 1))
    places_row = jnp.broadcast_to(places.astype(f32), (slots, 128)).T[:1]
    pos_hot_t_ref[...] = hot(places_row == iota((maxlen, slots), 0, f32))
    pos_ref[...] = dot_cols(pos_hot, pos)
    choose = hot(slot_col_ref[...] == iota((queries, slots), 1))
    choose_ref[...] = choose
    pos_q_ref[...] = dot(choose, pos_ref[...].astype(bf16))
    bias_ref[...] = mask_bias(seg, slot_row_ref[...])
    entries = logfreq_ref.shape[1]
    corr = dot(logfreq_ref[...], hot(iota((entries, queries), 0) == freq_ref[...]))
    corr_ref[...] = jnp.broadcast_to(corr, (META, queries)).astype(bf16)


def forward_kernel(
    item_ref,
    pos_ref,
    pos_q_ref,
    bias_ref,
    choose_ref,
    dense_ref,
    query_ref,
    first_ref,
    normed_ref,
    kv_ref,
    q_ref,
    mixed_ref,
    lse_ref,
    second_ref,
    normed_b_ref,
    active_ref,
    third_ref,
    value_t_ref,
    mixed_t_ref,
):
    small_at = dense_ref.shape[1] - SMALL
    rows = small_rows(dense_ref, small_at)
    first = item_ref[...].astype(f32) + pos_ref[...]
    first_ref[...] = first
    unit, unused = centred(first)
    normed_ref[...] = (unit * rows[0:1] + rows[1:2]).astype(bf16)
    normed = normed_ref[...]
    kv_ref[...] = dot(normed, dense_ref[:, D:QKV]).astype(bf16)
    choose = choose_ref[...]
    normed_q = dot(choose, normed).astype(bf16)
    q_ref[...] = dot(normed_q, dense_ref[:, :D]).astype(bf16)
    first_q = dot(choose, item_ref[...]) + pos_q_ref[...]
    value_t_ref[...] = kv_ref[:, D:].T

    def one_head(h, carry):
        own = iota((1, D), 1) // HEAD == h
        q_own = jnp.where(own, q_ref[...].astype(f32) * score_scale, 0.0).astype(bf16)
        scores = dot_cols(kv_ref[:, :D], q_own) + bias_ref[...]
        top = jnp.max(scores, axis=0, keepdims=True)
        weight = jnp.exp(scores - top)
        total = jnp.sum(weight, axis=0, keepdims=True)
        lse_ref[pl.ds(h, 1), :] = top + jnp.log(total)
        part = pl.ds(pl.multiple_of(h * HEAD, HEAD), HEAD)
        mixed_t_ref[part, :] = dot(value_t_ref[part, :], (weight * (1.0 / total)).astype(bf16))
        return carry

    lax.fori_loop(0, HEADS, one_head, 0)
    mixed = mixed_t_ref[...].T.astype(bf16)
    mixed_ref[...] = mixed
    second = first_q + dot(mixed, dense_ref[:, QKV:ATTN])
    second_ref[...] = second
    unit, unused = centred(second)
    normed_b = (unit * rows[2:3] + rows[3:4]).astype(bf16)
    normed_b_ref[...] = normed_b
    up_bias = jnp.concatenate([rows[7 + k : 8 + k] for k in range(FF // D)], axis=1)
    hidden = dot(normed_b, dense_ref[:, ATTN:DOWN]) + up_bias
    active = jnp.maximum(hidden, 0.0).astype(bf16)
    active_ref[...] = active
    third = second + dot_cols(active, dense_ref[:, DOWN:TABLES]) + rows[6:7]
    third_ref[...] = third
    unit, unused = centred(third)
    query_ref[...] = (unit * rows[4:5] + rows[5:6]).astype(bf16)


def columns_of(target_ref, queries):
    grps = target_ref.shape[0]
    return jnp.concatenate(
        [target_ref[g, queries : queries + 1, :].astype(f32) for g in range(grps)]
        + [jnp.zeros((128 - grps, queries), f32)],
        axis=0,
    ).T


def block_at(index, size):
    return pl.ds(pl.multiple_of(index * size, size), size)


def totals_kernel(
    where_ref,
    query_ref,
    target_ref,
    own_ref,
    valid_ref,
    *refs,
):
    out_refs, (tail_ref, target_t_ref, corr_ref, hold_ref) = refs[:-4], refs[-4:]
    owners = len(out_refs)
    height = tail_ref.shape[0]
    own_g, me = where_ref[0, 0], where_ref[0, 1]
    queries = query_ref.shape[0] // owners
    grps = target_ref.shape[0]
    corr_ref[...] = columns_of(target_ref, queries)

    for g in range(grps):
        target_t_ref[:, g * queries : (g + 1) * queries] = target_ref[g, :queries, :].T

    def one_owner(r):
        query = query_ref[block_at(me ^ r, queries), :].astype(f32)
        query = (query * logit_scale).astype(bf16)
        logits = [
            dot_cols(target_ref[g, :queries, :], query) - corr_ref[:, g : g + 1]
            for g in range(grps)
        ]
        top = functools.reduce(jnp.maximum, [jnp.max(x, axis=0, keepdims=True) for x in logits])
        total = jnp.zeros((1, queries), f32)
        mixed = jnp.zeros((D, queries), f32)
        for g in range(grps):
            weight = jnp.exp(logits[g] - top)
            total = total + jnp.sum(weight, axis=0, keepdims=True)
            mixed = mixed + dot(
                target_t_ref[:, g * queries : (g + 1) * queries], weight.astype(bf16)
            )
        return (top, total, mixed)

    tops, totals = [], []
    if grps > 8:

        def hold(r, carry):
            top, total, mixed = one_owner(r)
            hold_ref[r, :D, :] = mixed
            hold_ref[r, D : D + 8, :] = jnp.broadcast_to(top, (8, queries))
            hold_ref[r, D + 8 :, :] = jnp.broadcast_to(total, (8, queries))
            return carry

        lax.fori_loop(0, owners, hold, 0)
        for r in range(owners):
            out_refs[r][...] = hold_ref[r, :D, :].astype(bf16)
            tops.append(hold_ref[r, D : D + 1, :])
            totals.append(hold_ref[r, D + 8 : D + 9, :])
    else:
        for r in range(owners):
            top, total, mixed = one_owner(r)
            out_refs[r][...] = mixed.astype(bf16)
            tops.append(top)
            totals.append(total)

    product = own_ref[...].astype(f32) * target_ref[own_g, :queries, :].astype(f32)
    own = jnp.sum(product.T, axis=0, keepdims=True) * logit_scale
    own = own - target_ref[own_g, queries : queries + 1, :].astype(f32)
    pieces = [p for x in tops + totals + [own, valid_ref[...].astype(f32)] for p in split(x)]
    fill = jnp.zeros((height - len(pieces), queries), f32)
    tail_ref[...] = jnp.concatenate([x.astype(f32) for x in pieces] + [fill], axis=0).astype(bf16)


def piece(tail, k):
    return tail[3 * k : 3 * k + 1] + tail[3 * k + 1 : 3 * k + 2] + tail[3 * k + 2 : 3 * k + 3]


def backward_dense_kernel(
    owners,
    sums_ref,
    target_ref,
    valid_ref,
    total_ref,
    dense_ref,
    mixed_ref,
    second_ref,
    normed_b_ref,
    active_ref,
    third_ref,
    *refs,
):
    parts_refs = refs[:owners]
    grads_ref, proj_ref, grad_second_ref, grad_o_ref, columns_ref = refs[owners:]
    queries = valid_ref.shape[1]
    small_at = dense_ref.shape[1] - SMALL
    rows = small_rows(dense_ref, small_at)
    sums = sums_ref[...]
    tops = [sums[2 * r : 2 * r + 1] for r in range(owners)]
    totals = [sums[2 * r + 1 : 2 * r + 2] for r in range(owners)]
    top = functools.reduce(jnp.maximum, tops)
    scales = [jnp.exp(x - top) for x in tops]
    total = sum(x * y for x, y in zip(scales, totals))
    weight = valid_ref[...].astype(f32) / total_ref[0, 0]
    mean_t = jnp.zeros((D, queries), f32)
    for r in range(owners):
        mean_t = mean_t + parts_refs[r][...].astype(f32) * (scales[r] / total)
    target = target_ref[0, :queries, :].astype(f32)
    grad_query = ((mean_t - target.T) * (weight * logit_scale)).T

    unit, scale = centred(third_ref[...])
    grad_third = norm_back(grad_query, unit, scale, rows[4:5])
    gain_f, shift_f = total_of(grad_query * unit), total_of(grad_query)
    grad_f = grad_third.astype(bf16)
    active = active_ref[...]
    grads_ref[:, FF:] = dot(grad_f.T, active).astype(bf16)
    down_bias = total_of(grad_f.astype(f32))
    grad_active = dot(grad_f, dense_ref[:, DOWN:TABLES])
    grad_hidden = jnp.where(active.astype(f32) > 0.0, grad_active, 0.0).astype(bf16)
    grads_ref[:, :FF] = dot(normed_b_ref[...].T, grad_hidden).astype(bf16)
    up_bias = total_of(grad_hidden.astype(f32))
    grad_b = dot_cols(grad_hidden, dense_ref[:, ATTN:DOWN])
    unit, scale = centred(second_ref[...])
    grad_second = grad_third + norm_back(grad_b, unit, scale, rows[2:3])
    gain_b, shift_b = total_of(grad_b * unit), total_of(grad_b)
    grad_second_ref[...] = grad_second
    grad_y = grad_second.astype(bf16)
    proj_ref[...] = dot(mixed_ref[...].T, grad_y).astype(bf16)
    grad_o_ref[...] = dot_cols(grad_y, dense_ref[:, QKV:ATTN]).astype(bf16)
    columns = [gain_b, shift_b, gain_f, shift_f, down_bias]
    columns += [up_bias[:, k * D : (k + 1) * D] for k in range(FF // D)]
    columns_ref[...] = jnp.concatenate(
        columns + [jnp.zeros((META - len(columns), D), f32)], axis=0
    )


def backward_kernel(
    proj_ref,
    grad_second_ref,
    grad_o_ref,
    columns_ref,
    slot_row_ref,
    dense_ref,
    bias_ref,
    pos_hot_t_ref,
    first_ref,
    normed_t_ref,
    key_t_ref,
    kv_ref,
    q_ref,
    lse_ref,
    grad_first_ref,
    grads_ref,
    grad_q_t_ref,
    probs_ref,
    grad_s_ref,
    stack_ref,
    p_ref,
    dp_ref,
    joined_ref,
    grad_a_ref,
    base_ref,
    halves_ref,
):
    slots, queries = bias_ref.shape
    maxlen = pos_hot_t_ref.shape[0]
    small_at = dense_ref.shape[1] - SMALL
    rows = small_rows(dense_ref, small_at)

    def one_head(h, carry):
        own = iota((1, D), 1) // HEAD == h
        q_own = jnp.where(own, q_ref[...].astype(f32), 0.0)
        stack_ref[0, pl.ds(pl.multiple_of(h * queries, queries), queries), :] = q_own.astype(bf16)
        o_own = jnp.where(own, grad_o_ref[...].astype(f32), 0.0).astype(bf16)
        stack_ref[1, pl.ds(pl.multiple_of(h * queries, queries), queries), :] = o_own
        columns = pl.ds(pl.multiple_of(h * queries, queries), queries)
        scores = dot_cols(kv_ref[:, :D], (q_own * score_scale).astype(bf16)) + bias_ref[...]
        probs = jnp.exp(scores - lse_ref[pl.ds(h, 1), :])
        p_ref[...] = probs
        probs_ref[:, columns] = probs.astype(bf16)
        grad_p = dot_cols(kv_ref[:, D:], o_own)
        dp_ref[...] = grad_p
        inner = jnp.sum(p_ref[...] * grad_p, axis=0, keepdims=True)
        grad_s_ref[:, columns] = (p_ref[...] * (dp_ref[...] - inner)).astype(bf16)
        part = pl.ds(pl.multiple_of(h * HEAD, HEAD), HEAD)
        grad_q_t_ref[part, :] = dot(key_t_ref[part, :], grad_s_ref[:, columns])
        return carry

    lax.fori_loop(0, HEADS, one_head, 0)
    grad_q = (grad_q_t_ref[...].T * score_scale).astype(bf16)
    spread = hot(iota((slots, queries), 0) == slot_row_ref[...])
    joined_ref[:, :D] = dot(spread, grad_q).astype(bf16)
    joined_ref[:, D : 2 * D] = (dot(grad_s_ref[...], stack_ref[0]) * score_scale).astype(bf16)
    joined_ref[:, 2 * D :] = dot(probs_ref[...], stack_ref[1]).astype(bf16)
    grads_ref[:, :QKV] = dot(normed_t_ref[...], joined_ref[...]).astype(bf16)
    grads_ref[:, QKV:ATTN] = proj_ref[...]
    grad_a_ref[...] = dot_cols(joined_ref[...], dense_ref[:, :QKV])
    high, middle, unused = split(grad_second_ref[...])
    base_ref[...] = dot(spread, high) + dot(spread, middle)

    grad_a = grad_a_ref[...]
    unit, scale = centred(first_ref[...])
    grad_first = base_ref[...] + norm_back(grad_a, unit, scale, rows[0:1])
    grad_first_ref[...] = grad_first.astype(bf16)
    high, middle, unused = split(grad_first)
    halves_ref[:, :D] = high
    halves_ref[:, D:] = middle
    gain_a, shift_a = total_of(grad_a * unit), total_of(grad_a)
    both = dot(pos_hot_t_ref[...], halves_ref[...])
    grads_ref[:, ATTN : ATTN + maxlen] = (both[:, :D] + both[:, D:]).T.astype(bf16)
    columns = jnp.concatenate(
        [gain_a, shift_a, columns_ref[: NSMALL - 2]]
        + [jnp.zeros((SMALL - NSMALL, D), f32)],
        axis=0,
    )
    grads_ref[:, ATTN + maxlen :] = columns.T.astype(bf16)


def target_grad_kernel(owners, where_ref, total_ref, query_ref, target_ref, *refs):
    tail_refs, (out_ref, sums_ref, corr_ref) = refs[:owners], refs[owners:]
    grps = target_ref.shape[0]
    queries = query_ref.shape[0] // owners
    corr_ref[...] = columns_of(target_ref, queries)
    same = jnp.where(iota((queries, queries), 0) == iota((queries, queries), 1), 1.0, 0.0)
    own_g, me = where_ref[0, 0], where_ref[0, 1]
    tails = [ref[...].astype(f32) for ref in tail_refs]
    log_totals, weights = [], []
    loss = jnp.zeros((1, queries), f32)
    for r in range(owners):
        tops = [piece(tails[k], k ^ r) for k in range(owners)]
        totals = [piece(tails[k], owners + (k ^ r)) for k in range(owners)]
        top = functools.reduce(jnp.maximum, tops)
        total = functools.reduce(
            jnp.add, [totals[k] * jnp.exp(tops[k] - top) for k in range(owners)]
        )
        log_totals.append(top + jnp.log(total))
        weights.append(piece(tails[r], 2 * owners + 1) / total_ref[0, 0])
        loss = loss + weights[r] * (log_totals[r] - piece(tails[r], 2 * owners))
        if r == 0:
            sums_ref[...] = jnp.concatenate(
                [x for pair in zip(tops, totals) for x in pair], axis=0
            )
    loss = jnp.sum(loss, axis=1, keepdims=True)
    pieces = split(jnp.broadcast_to(loss, (1, queries)))
    tail = jnp.concatenate(
        [x.astype(f32) for x in pieces] + [jnp.zeros((META - len(pieces), queries), f32)], axis=0
    ).astype(bf16)
    for g in range(grps):
        target = target_ref[g, :queries, :]
        grad = jnp.zeros((queries, D), f32)
        for r in range(owners):
            query = query_ref[block_at(me ^ r, queries), :]
            logits = dot_cols(target, query) * logit_scale - corr_ref[:, g : g + 1]
            probs = jnp.exp(logits - log_totals[r])
            if r == 0:
                probs = probs - jnp.where(own_g == g, 1.0, 0.0) * same
            coeff = weights[r] * probs
            grad = grad + dot(coeff.astype(bf16), query)
        out_ref[g, :queries, :] = grad.astype(bf16)
        out_ref[g, queries:, :] = tail


def turn_kernel(normed_ref, kv_ref, normed_t_ref, key_t_ref):
    normed_t_ref[...] = normed_ref[...].T
    key_t_ref[...] = kv_ref[:, :D].T


def send_kernel(
    grad_first_ref, parts_ref, place_ref, sent_ref, both_ref, loss_ref
):
    grps, height, unused = parts_ref.shape
    slots = grad_first_ref.shape[0]
    queries = height - META
    both_ref[:slots, :] = grad_first_ref[...]
    total = parts_ref[0, :queries, :].astype(f32)
    for g in range(1, grps):
        total = total + parts_ref[g, :queries, :].astype(f32)
    both_ref[slots:, :] = (total * logit_scale).astype(bf16)
    loss = parts_ref[0, queries : queries + 8, :].astype(f32)
    for g in range(1, grps):
        loss = loss + parts_ref[g, queries : queries + 8, :].astype(f32)
    loss_ref[...] = jnp.sum(loss[:, :1], axis=0, keepdims=True)
    asks = both_ref.shape[0]
    block = block_of(sent_ref.shape[0], 2048)

    def one_block(i, carry):
        begin = pl.multiple_of(i * block, block)
        spread = hot(place_ref[...] - begin == iota((block, asks), 0))
        sent_ref[pl.ds(begin, block), :] = dot(spread, both_ref[...]).astype(bf16)
        return carry

    lax.fori_loop(0, sent_ref.shape[0] // block, one_block, 0)


def advance(weight, moment, average, grad, rate):
    moment_new = momentum_rate * moment + grad
    weight_new = weight - rate * (grad + momentum_rate * moment_new)
    average_new = average_rate * average + (1.0 - average_rate) * weight_new
    return (weight_new, moment_new, average_new, weight_new.astype(bf16))


def update_kernel(
    rate,
    rows,
    span_ref,
    ids_ref,
    recv_ref,
    extra_ref,
    w_ref,
    m_ref,
    a_ref,
    w_out_ref,
    m_out_ref,
    a_out_ref,
    copy_out_ref,
    w_held,
    m_held,
    a_held,
    copy_held,
    tiles_ref,
    grad_ref,
    in_sems,
    out_sems,
    extra_sem,
):
    count = w_ref.shape[0]
    devices, cap, unused = recv_ref.shape
    tiles = cap // 16
    edges = list(range(0, count, rows)) + [count]
    parts = [(k, edges[k], edges[k + 1] - edges[k]) for k in range(len(edges) - 1)]

    def copy_in(k, begin, size, j):
        source, target = ((w_ref, w_held), (m_ref, m_held), (a_ref, a_held))[j]
        part = pl.ds(begin, size)
        return pltpu.make_async_copy(source.at[part], target.at[part], in_sems.at[j, k])

    def copy_out(k, begin, size, j):
        pairs = (
            (w_held, w_out_ref),
            (m_held, m_out_ref),
            (a_held, a_out_ref),
            (copy_held, copy_out_ref),
        )
        source, target = pairs[j]
        part = pl.ds(begin, size)
        return pltpu.make_async_copy(source.at[part], target.at[part], out_sems.at[j, k])

    for part in parts:
        for j in range(3):
            copy_in(*part, j).start()
    for j in range(tiles):
        for n in range(devices):
            tiles_ref[j, 16 * n : 16 * (n + 1), :] = recv_ref[n, 16 * j : 16 * (j + 1), :]

    for k, begin, size in parts:
        here = pl.ds(0, size)
        grad_ref[here, :] = jnp.zeros((size, D), f32)

        @pl.when(span_ref[0] > 1)
        def start_from_extra():
            copy = pltpu.make_async_copy(
                extra_ref.at[pl.ds(begin, size)], grad_ref.at[here], extra_sem
            )
            copy.start()
            copy.wait()

        for j in range(tiles):

            @pl.when((span_ref[1 + 2 * j] < begin + size) & (span_ref[2 + 2 * j] >= begin))
            def add():
                spread = hot(ids_ref[j : j + 1, :] - begin == iota((size, ids_ref.shape[1]), 0))
                grad_ref[here, :] += dot(spread, tiles_ref[j])

        for j in range(3):
            copy_in(k, begin, size, j).wait()
        part = pl.ds(begin, size)
        new = advance(w_held[part, :], m_held[part, :], a_held[part, :], grad_ref[here, :], rate)
        w_held[part, :], m_held[part, :], a_held[part, :], copy_held[part, :] = new
        for j in range(4):
            copy_out(k, begin, size, j).start()
    for part in parts:
        for j in range(4):
            copy_out(*part, j).wait()


def update_table(span, ids, recv, extra, table_w, table_m, table_a, rate):
    count = table_w.shape[0]
    rows = min(784, count)
    blocks = math.ceil(count / rows)
    devices, cap, unused = recv.shape
    anywhere = pl.BlockSpec(memory_space=pl.ANY)
    inside = pl.BlockSpec(memory_space=pltpu.VMEM)
    tables = [pltpu.with_memory_space_constraint(x, pltpu.HBM) for x in (table_w, table_m, table_a)]
    return tuple(
        pl.pallas_call(
            functools.partial(update_kernel, rate, rows),
            in_specs=[pl.BlockSpec(memory_space=pltpu.SMEM), inside, inside] + [anywhere] * 4,
            out_specs=[anywhere] * 4,
            scratch_shapes=[pltpu.VMEM((count, D), f32)] * 3
            + [
                pltpu.VMEM((count, D), bf16),
                pltpu.VMEM((cap // 16, 16 * devices, D), bf16),
                pltpu.VMEM((rows, D), f32),
                pltpu.SemaphoreType.DMA((3, blocks)),
                pltpu.SemaphoreType.DMA((4, blocks)),
                pltpu.SemaphoreType.DMA(()),
            ],
            out_shape=[jax.ShapeDtypeStruct((count, D), f32)] * 3
            + [jax.ShapeDtypeStruct((count, D), bf16)],
            compiler_params=pltpu.CompilerParams(vmem_limit_bytes=56 << 20),
            cost_estimate=pl.CostEstimate(
                flops=count * devices * cap * D, bytes_accessed=26 * count * D, transcendentals=0
            ),
        )(span, ids, recv, extra, *tables)
    )


def update_dense_kernel(rates, widths, parts_ref, *refs):
    ins, outs = refs[: 3 * len(widths)], refs[3 * len(widths) :]
    grad = parts_ref[0].astype(f32)
    for g in range(1, parts_ref.shape[0]):
        grad = grad + parts_ref[g].astype(f32)
    begin = 0
    for k, (rate, width) in enumerate(zip(rates, widths)):
        w_ref, m_ref, a_ref = ins[3 * k : 3 * k + 3]
        here = grad[:, begin : begin + width][:, : w_ref.shape[1]]
        new = advance(w_ref[...], m_ref[...], a_ref[...], here, rate)
        for j in range(4):
            outs[4 * k + j][...] = new[j]
        begin += width


def blank_kernel(seed_ref, out_ref):
    del seed_ref, out_ref


def blank_of(shape, dtype, seed):
    return pl.pallas_call(
        blank_kernel,
        out_shape=jax.ShapeDtypeStruct(shape, dtype),
        in_specs=[pl.BlockSpec(memory_space=pl.ANY)],
        out_specs=pl.BlockSpec(memory_space=pl.ANY),
    )(seed)


def everyone(values):
    return lax.all_to_all(values, ("grp", "row"), split_axis=0, concat_axis=0, tiled=True)


def swap(values, axis, bit):
    pairs = [(i, i ^ bit) for i in range(lax.axis_size(axis))]
    return lax.ppermute(values, axis, pairs)


def bits_of(size):
    return [1 << k for k in range(size.bit_length() - 1)]


def after(values, *others):
    return lax.optimization_barrier((values,) + others)[0]


def spread_row(values, bit):
    got = swap(values, "row", bit)
    mine = (lax.axis_index("row") // bit) % 2 == 0
    return jnp.stack([jnp.where(mine, values, got), jnp.where(mine, got, values)], axis=-3)


def sum_row(values, owners):
    for bit in bits_of(owners):
        grps, count, rows, width = values.shape
        pairs = values.reshape(grps, count // 2, 2, rows, width)
        mine = (lax.axis_index("row") // bit) % 2
        keep = lax.dynamic_index_in_dim(pairs, mine, 2, keepdims=False)
        give = lax.dynamic_index_in_dim(pairs, 1 - mine, 2, keepdims=False)
        values = (keep.astype(f32) + swap(give, "row", bit).astype(f32)).astype(bf16)
    return values.reshape(grps, rows, width)


def local(
    item_owner,
    item_row,
    seg,
    query_slot,
    tgt_owner,
    tgt_row,
    freq_idx,
    valid,
    logfreq,
    table_w,
    table_m,
    table_a,
    attn_w,
    attn_m,
    attn_a,
    ffn_w,
    ffn_m,
    ffn_a,
    pos_w,
    pos_m,
    pos_a,
    small_w,
    small_m,
    small_a,
):
    owners = lax.axis_size("row")
    grps = lax.axis_size("grp")
    devices = grps * owners
    local_rows = table_w.shape[0]
    slots = seg.shape[1]
    queries = query_slot.shape[1]
    asks = slots + queries
    total_q = queries * devices
    mean = 2 * asks // devices
    cap = 16 * math.ceil((mean + 3.5 * math.sqrt(mean)) / 16)
    width = 128 * math.ceil((cap + 3) / 128)
    maxlen = pos_w.shape[1]
    own_rows = attn_w.shape[0]
    my_grp, my_row = lax.axis_index("grp"), lax.axis_index("row")

    wanted, place, place_col, rank, dest, local_row = run(
        functools.partial(route_kernel, cap, local_rows, grps),
        [((devices, width), i32), ((1, asks), i32), ((asks, 1), i32)] + [((1, asks), i32)] * 3,
        [
            item_owner.reshape(1, slots),
            item_row,
            tgt_owner.reshape(1, queries),
            tgt_row,
            valid,
        ],
        flops=2 * devices * asks * asks,
    )
    asked = everyone(wanted)
    (dense,) = run(
        low_kernel,
        [((grps, own_rows, TABLES + maxlen + SMALL), bf16)],
        [attn_w, ffn_w, pos_w, after(small_w, wanted)],
        moved=1 << 20,
    )
    low_table, token = lower_table(after(table_w, wanted))
    dense, asked, token = lax.optimization_barrier((dense, asked, token))
    dense = lax.all_to_all(dense, "grp", split_axis=0, concat_axis=0, tiled=True)
    most = jnp.max(asked[:, cap + 1])
    rounds = (most + cap - 1) // cap
    valid_total = jnp.maximum(jnp.sum(asked[:, cap + 2]).astype(f32), 1.0).reshape(1, 1)
    (rows_found,) = run(
        functools.partial(lookup_kernel, cap, local_rows),
        [((devices, cap, D), bf16)],
        [asked, token, low_table],
        scratch=[pltpu.VMEM((16 * devices, 128), f32), pltpu.VMEM((16 * devices, D), f32)],
        moved=8 * local_rows * D,
        vmem=24,
    )
    dense, rows_found = lax.optimization_barrier((dense, rows_found))
    for bit in reversed(bits_of(owners)):
        dense = spread_row(dense, bit)
    dense = dense.reshape(D, -1)
    found = everyone(rows_found).reshape(devices * cap, D)
    ids = asked[:, :cap].reshape(devices, cap // 16, 16).transpose(1, 0, 2)
    ids = ids.reshape(cap // 16, 16 * devices)
    low_end = jnp.min(jnp.where(ids >= 0, ids, local_rows), axis=1)
    span = jnp.stack([low_end, jnp.max(ids, axis=1)], axis=1).reshape(-1)
    span = jnp.concatenate([rounds.reshape(1), span])

    found, ids, span = lax.optimization_barrier((found, ids, span))
    seg_col = seg.reshape(slots, 1)
    slot_col = query_slot.reshape(queries, 1)
    pos_part, pos_hot_t, pos_q, bias, choose, corr = run(
        prepare_kernel,
        [
            ((slots, D), f32),
            ((maxlen, slots), bf16),
            ((queries, D), f32),
            ((slots, queries), f32),
            ((queries, slots), bf16),
            ((META, queries), bf16),
        ],
        [seg_col, query_slot, slot_col, dense, freq_idx, logfreq.reshape(1, -1)],
        flops=1 << 30,
    )
    found = after(found, pos_part)
    (target_emb,) = run(
        extract_targets_kernel,
        [((grps, queries + META, D), bf16)],
        [found, place_col, corr],
        flops=2 * devices * cap * queries * D,
    )
    def wanted_of(k):
        here = rank[0] // cap == k
        spot = jnp.where(here, dest[0] * cap + rank[0] - k * cap, devices * cap)
        ids = jnp.full((devices * cap,), -1, i32).at[spot].set(local_row[0], mode="drop")
        return here, spot, everyone(ids.reshape(devices, cap)).reshape(devices * cap)

    def more_rows(carry):
        k, items, targets = carry
        here, spot, ids = wanted_of(k)
        rows = jnp.where((ids >= 0)[:, None], table_w[jnp.maximum(ids, 0)], 0.0).astype(bf16)
        got = everyone(rows.reshape(devices, cap, D)).reshape(devices * cap, D)
        got = got[jnp.minimum(spot, devices * cap - 1)]
        items = jnp.where(here[:slots, None], got[:slots], items)
        top = jnp.where(here[None, slots:, None], got[None, slots:], targets[:, :queries])
        return (k + 1, items, targets.at[:, :queries].set(top))

    unused, patch, target_emb = lax.while_loop(
        lambda carry: carry[0] < rounds,
        more_rows,
        (jnp.int32(1), blank_of((slots, D), bf16, wanted), target_emb),
    )
    (item_emb,) = run(
        extract_items_kernel,
        [((slots, D), bf16)],
        [after(found, target_emb), place_col, patch],
        flops=2 * devices * cap * slots * D,
    )
    targets = lax.all_to_all(target_emb, "grp", split_axis=0, concat_axis=0, tiled=True)
    query_own, first, normed, kv, q_own, mixed_o, lse, second, normed_b, active, third = run(
        forward_kernel,
        [
            ((queries, D), bf16),
            ((slots, D), f32),
            ((slots, D), bf16),
            ((slots, 2 * D), bf16),
            ((queries, D), bf16),
            ((queries, D), bf16),
            ((HEADS, queries), f32),
            ((queries, D), f32),
            ((queries, D), bf16),
            ((queries, FF), bf16),
            ((queries, D), f32),
        ],
        [item_emb, pos_part, pos_q, bias, choose, dense],
        scratch=[
            pltpu.VMEM((D, slots), bf16),
            pltpu.VMEM((D, queries), f32),
        ],
        flops=6 << 30,
    )
    query_all = lax.all_gather(query_own, "row", axis=0, tiled=True)
    where = jnp.stack([my_grp, my_row]).astype(i32).reshape(1, 2)
    tall = 16 * math.ceil((6 * owners + 6) / 16)
    *mixed, tail = run(
        totals_kernel,
        [((D, queries), bf16)] * owners + [((tall, queries), bf16)],
        [where, query_all, targets, query_own, valid],
        smem=(0,),
        scratch=[
            pltpu.VMEM((D, grps * queries), bf16),
            pltpu.VMEM((queries, 128), f32),
            pltpu.VMEM((owners if grps > 8 else 1, D + META, queries), f32),
        ],
        flops=4 * owners * grps * queries * queries * D,
    )
    tails = [tail] + [swap(tail, "row", k) for k in range(1, owners)]
    mixed = [mixed[0]] + [swap(mixed[k], "row", k) for k in range(1, owners)]
    normed_t, key_t = run(turn_kernel, [((D, slots), bf16)] * 2, [normed, kv], moved=4 << 20)
    target_parts, sums = run(
        functools.partial(target_grad_kernel, owners),
        [((grps, queries + META, D), bf16), ((2 * owners, queries), f32)],
        [
            where,
            valid_total,
            query_all,
            targets,
        ]
        + tails,
        smem=(0, 1),
        scratch=[pltpu.VMEM((queries, 128), f32)],
        flops=4 * owners * grps * queries * queries * D,
    )
    target_parts, *mixed = lax.optimization_barrier((target_parts, *mixed))
    target_parts = lax.all_to_all(target_parts, "grp", split_axis=0, concat_axis=0, tiled=True)
    grads_ffn, grads_proj, grad_second, grad_o, columns = run(
        functools.partial(backward_dense_kernel, owners),
        [
            ((D, 2 * FF), bf16),
            ((D, D), bf16),
            ((queries, D), f32),
            ((queries, D), bf16),
            ((META, D), f32),
        ],
        [sums, target_emb, valid, valid_total, dense, mixed_o, second, normed_b]
        + [active, third]
        + mixed,
        smem=(3,),
        flops=1 << 30,
    )
    grads_ffn = sum_row(grads_ffn.reshape(grps, owners, own_rows, -1), owners)
    grad_first, grads = run(
        backward_kernel,
        [((slots, D), bf16), ((D, ATTN + maxlen + SMALL), bf16)],
        [grads_proj, grad_second, grad_o, columns, query_slot, dense, bias, pos_hot_t, first]
        + [normed_t, key_t, kv, q_own, lse],
        scratch=[
            pltpu.VMEM((D, queries), f32),
            pltpu.VMEM((slots, HEADS * queries), bf16),
            pltpu.VMEM((slots, HEADS * queries), bf16),
            pltpu.VMEM((2, HEADS * queries, D), bf16),
            pltpu.VMEM((slots, queries), f32),
            pltpu.VMEM((slots, queries), f32),
            pltpu.VMEM((slots, QKV), bf16),
            pltpu.VMEM((slots, D), f32),
            pltpu.VMEM((slots, D), f32),
            pltpu.VMEM((slots, 2 * D), bf16),
        ],
        flops=17 << 30,
    )

    sent, both, loss = run(
        send_kernel,
        [((devices * cap, D), bf16), ((asks, D), bf16), ((1, 1), f32)],
        [grad_first, target_parts, place],
        flops=2 * devices * cap * asks * D,
    )
    received = everyone(sent.reshape(devices, cap, D))
    grads = sum_row(grads.reshape(grps, owners, own_rows, -1), owners)
    grad_own = jnp.concatenate([grads_ffn, grads], axis=-1)
    grad_own, received = lax.optimization_barrier((grad_own, received))
    grad_own = lax.all_to_all(grad_own, "grp", split_axis=0, concat_axis=0, tiled=True)

    rate_table = 4.0 * total_q
    rate_dense = 0.25 * math.sqrt(total_q)
    rate_place = 2.0 * math.sqrt(total_q)
    blank = blank_of((local_rows, D), f32, wanted)

    def more_grads(carry):
        k, total = carry
        here, spot, more_ids = wanted_of(k)
        rows = jnp.zeros((devices * cap, D), bf16).at[spot].set(both, mode="drop")
        rows = everyone(rows.reshape(devices, cap, D)).reshape(devices * cap, D)
        spot = jnp.where(more_ids >= 0, more_ids, local_rows)
        total = jnp.where(k > 1, total, 0.0)
        return (k + 1, total.at[spot].add(rows.astype(f32), mode="drop"))

    unused, extra = lax.while_loop(
        lambda carry: carry[0] < rounds,
        more_grads,
        (jnp.int32(1), blank),
    )
    table_out = update_table(span, ids, received, extra, table_w, table_m, table_a, rate_table)
    held = [
        [ffn_w, ffn_m, ffn_a],
        [attn_w, attn_m, attn_a],
        [pos_w, pos_m, pos_a],
        [small_w, small_m, small_a],
    ]
    dense_out = run(
        functools.partial(
            update_dense_kernel,
            [rate_dense, rate_dense, rate_place, rate_dense],
            [2 * FF, ATTN, maxlen, SMALL],
        ),
        [(x.shape, dtype) for three in held for x, dtype in zip(three + three[:1], [f32] * 3 + [bf16])],
        [grad_own] + [x for three in held for x in three],
    )
    ffn_out, attn_out, pos_out, small_out = [tuple(dense_out[4 * k : 4 * k + 4]) for k in range(4)]
    return (loss.reshape(()),) + table_out + attn_out + ffn_out + pos_out + small_out


def solution(mesh):
    rows = P(("grp", "row"), None)
    table = P(("row", "grp"), None)
    ids = P(("grp", "row"), None, None)
    in_specs = (ids, rows, rows, rows, ids, rows, rows, rows, P()) + (table,) * 3 + (rows,) * 12
    out_specs = (P(),) + (table,) * 4 + (rows,) * 16
    return jax.shard_map(local, mesh=mesh, in_specs=in_specs, out_specs=out_specs, check_vma=False)
```

```python
import functools
import math

import jax
import jax.numpy as jnp
from jax import lax
from jax.experimental import pallas as pl
from jax.experimental.pallas import tpu as pltpu
from jax.sharding import PartitionSpec as P

D = 256
HEADS = 8
HEAD = 32
FF = 1024
QKV = 3 * D
ATTN = 4 * D
DOWN = ATTN + FF
TABLES = ATTN + 2 * FF
NSMALL = 11
SMALL = 128
META = 16
CHUNK = 512

norm_eps = 1e-05
score_scale = 0.125
logit_scale = 0.125
momentum_rate = 0.5
average_rate = 0.5
negative = -1e30
bf16 = jnp.bfloat16
f32 = jnp.float32
i32 = jnp.int32


def iota(shape, dim, dtype=i32):
    return lax.broadcasted_iota(i32, shape, dim).astype(dtype)


def hot(condition):
    return jnp.where(condition, 1.0, 0.0).astype(bf16)


def dot(left, right):
    return lax.dot_general(left, right, (((1,), (0,)), ((), ())), preferred_element_type=f32)


def dot_cols(left, right):
    return lax.dot_general(left, right, (((1,), (1,)), ((), ())), preferred_element_type=f32)


def split(value):
    high = value.astype(bf16)
    rest = value - high.astype(f32)
    middle = rest.astype(bf16)
    low = (rest - middle.astype(f32)).astype(bf16)
    return (high, middle, low)


def run(body, outs, args, smem=(), scratch=(), flops=0, moved=0, vmem=56):
    return pl.pallas_call(
        body,
        out_shape=[jax.ShapeDtypeStruct(shape, dtype) for shape, dtype in outs],
        in_specs=[
            pl.BlockSpec(
                memory_space=pltpu.SMEM if i in smem else pltpu.VMEM
            )
            for i in range(len(args))
        ],
        out_specs=[pl.BlockSpec(memory_space=pltpu.VMEM) for unused in outs],
        scratch_shapes=list(scratch),
        compiler_params=pltpu.CompilerParams(vmem_limit_bytes=vmem << 20),
        cost_estimate=pl.CostEstimate(flops=flops, bytes_accessed=moved, transcendentals=0),
    )(*args)


def block_of(total, limit):
    return max(b for b in range(16, limit + 1, 16) if total % b == 0)


def by_rows(total, block, body, init=0):
    def step(i, carry):
        return body(pl.ds(pl.multiple_of(i * block, block), block), carry)

    return lax.fori_loop(0, total // block, step, init)


def fold(values, combine):
    parts = values.reshape(values.shape[0] // 8, 8, values.shape[1])
    return functools.reduce(combine, [parts[k] for k in range(parts.shape[0])])


def column_of(row):
    return jnp.broadcast_to(row, (128, row.shape[1])).T[:, :1]


def route_kernel(
    cap,
    local_rows,
    grps,
    item_owner_ref,
    item_row_ref,
    tgt_owner_ref,
    tgt_row_ref,
    valid_ref,
    wanted_ref,
    place_ref,
    column_ref,
    rank_ref,
    dest_ref,
    local_ref,
):
    devices, width = wanted_ref.shape
    asks = dest_ref.shape[1]
    owner = jnp.concatenate([item_owner_ref[...], tgt_owner_ref[...]], axis=1).astype(f32)
    row = jnp.concatenate([item_row_ref[...], tgt_row_ref[...]], axis=1).astype(f32)
    part = jnp.zeros((1, asks), f32)
    for g in range(1, grps):
        part = part + jnp.where(row >= g * local_rows, 1.0, 0.0)
    dest = part * (devices // grps) + owner
    local = row - part * local_rows
    dest_ref[...] = dest.astype(i32)
    local_ref[...] = local.astype(i32)
    named = jnp.where(iota((devices, asks), 0, f32) == dest, 1.0, 0.0)
    count = jnp.sum(named, axis=1, keepdims=True)
    count_row = jnp.broadcast_to(count, (devices, 128)).T[:1, :]
    below = jnp.where(iota((devices, devices), 1) < iota((devices, devices), 0), 1.0, 0.0)
    before = jnp.sum(below * count_row, axis=1, keepdims=True)
    room = jnp.sum(named * jnp.maximum(cap - count, 0.0), axis=0, keepdims=True)
    item = (dest * local_rows + local).astype(i32)
    key = item * 2048 + iota((1, asks), 1)
    key_col = column_of(dest * local_rows + local).astype(i32) * 2048 + iota((asks, 1), 0)
    rank = jnp.sum(jnp.where(key_col < key, 1.0, 0.0), axis=0, keepdims=True)
    rank = rank - jnp.sum(named * before, axis=0, keepdims=True)
    lead = jnp.floor(local * (cap / local_rows)) - rank + dest * 4096.0
    lead = jnp.where(key_col <= key, column_of(lead), 0.0)
    lead = jnp.max(lead, axis=0, keepdims=True) - dest * 4096.0
    slot = rank + jnp.minimum(lead, room)
    spot = iota((width, asks), 0, f32)
    at_spot = hot((spot == slot) & (rank < cap))
    high = jnp.floor((local + 1.0) * (1.0 / 64.0))
    low = local + 1.0 - high * 64.0
    ids = dot_cols((named * high).astype(bf16), at_spot) * 64.0 + dot_cols(
        (named * low).astype(bf16), at_spot
    )
    lane = iota((devices, width), 1, f32)
    most = jnp.max(count, axis=0, keepdims=True)
    flags = jnp.sum(valid_ref[...].astype(f32), axis=1, keepdims=True)
    ids = ids - 1.0
    ids = jnp.where(lane == cap, count, ids)
    ids = jnp.where(lane == cap + 1, most, ids)
    ids = jnp.where(lane == cap + 2, flags, ids)
    wanted_ref[...] = ids.astype(i32)
    place = jnp.where(rank < cap, dest * cap + slot, -1.0)
    place_ref[...] = place.astype(i32)
    rank_ref[...] = rank.astype(i32)
    column_ref[...] = column_of(place).astype(i32)


def low_kernel(attn_ref, ffn_ref, pos_ref, small_ref, out_ref):
    small_at = out_ref.shape[2] - SMALL
    rows = attn_ref.shape[0]
    tail = jnp.concatenate([small_ref[...], jnp.zeros((rows, SMALL - NSMALL), f32)], axis=1)
    for g in range(out_ref.shape[0]):
        out_ref[g, :, :ATTN] = attn_ref[...].astype(bf16)
        out_ref[g, :, ATTN:TABLES] = ffn_ref[...].astype(bf16)
        out_ref[g, :, TABLES:small_at] = pos_ref[...].astype(bf16)
        out_ref[g, :, small_at:] = tail.astype(bf16)


def lower_table_kernel(table_ref, low_ref, token_ref, held_ref, sems):
    count = table_ref.shape[0]
    edges = [count * k // 32 * 8 for k in range(4)] + [count]
    copies = []
    for k in range(4):
        part = pl.ds(edges[k], edges[k + 1] - edges[k])
        copies.append(pltpu.make_async_copy(table_ref.at[part], held_ref.at[part], sems.at[k]))
        copies[k].start()
    for k in range(4):
        copies[k].wait()
        part = slice(edges[k], edges[k + 1])
        low_ref[part, :] = held_ref[part, :].astype(bf16)
    spare = low_ref.shape[0] - count
    if spare:
        low_ref[count:, :] = jnp.zeros((spare, D), bf16)
    token_ref[...] = jnp.zeros(token_ref.shape, f32)


def lower_table(table):
    count = table.shape[0]
    return pl.pallas_call(
        lower_table_kernel,
        out_shape=[
            pltpu.VMEM((CHUNK * math.ceil(count / CHUNK), D), bf16),
            jax.ShapeDtypeStruct((8, 128), f32),
        ],
        in_specs=[pl.BlockSpec(memory_space=pl.ANY)],
        out_specs=[pl.BlockSpec(memory_space=pltpu.VMEM)] * 2,
        scratch_shapes=[pltpu.VMEM((count, D), f32), pltpu.SemaphoreType.DMA((4,))],
        compiler_params=pltpu.CompilerParams(vmem_limit_bytes=16 << 20),
        cost_estimate=pl.CostEstimate(flops=0, bytes_accessed=6 * count * D, transcendentals=0),
    )(pltpu.with_memory_space_constraint(table, pltpu.HBM))


def lookup_kernel(cap, local_rows, asked_ref, token_ref, low_ref, rows_ref, ids_ref, total_ref):
    del token_ref
    devices, width = asked_ref.shape
    chunk = CHUNK
    turned = asked_ref[...].astype(f32).T
    slot = iota((16, devices), 0)
    for j in range(cap // 16):
        part = turned[16 * j : 16 * (j + 1), :]
        for n in range(devices):
            ids_ref[16 * n : 16 * (n + 1), :] = jnp.broadcast_to(part[:, n : n + 1], (16, 128))
        first = jnp.min(jnp.where(part >= 0.0, part, float(local_rows))).astype(i32)
        last = jnp.max(part).astype(i32)
        total_ref[...] = jnp.zeros(total_ref.shape, f32)

        def one_chunk(c, carry):
            begin = pl.multiple_of(c * chunk, chunk)
            ids = ids_ref[...] - (c * chunk).astype(f32)
            near = jnp.concatenate(
                [hot(ids == iota((1, 128), 1, f32) + 128.0 * k) for k in range(chunk // 128)],
                axis=1,
            )
            total_ref[...] += dot(near, low_ref[pl.ds(begin, chunk), :])
            return carry

        lax.fori_loop(first // chunk, last // chunk + 1, one_chunk, 0)
        for n in range(devices):
            rows_ref[n, 16 * j : 16 * (j + 1), :] = total_ref[16 * n : 16 * (n + 1), :].astype(bf16)


def rows_of(found_ref, place):
    total = found_ref.shape[0]
    return dot(hot(place == iota((place.shape[0], total), 1)), found_ref[...])


def extract_targets_kernel(found_ref, column_ref, corr_ref, target_ref):
    queries = corr_ref.shape[1]
    rows = rows_of(found_ref, column_ref[column_ref.shape[0] - queries :, :])
    for g in range(target_ref.shape[0]):
        target_ref[g, :queries, :] = rows.astype(bf16)
        target_ref[g, queries:, :] = corr_ref[...]


def extract_items_kernel(found_ref, column_ref, patch_ref, item_ref):
    def items(part, carry):
        place = column_ref[part, :]
        rows = rows_of(found_ref, place)
        item_ref[part, :] = jnp.where(place < 0, patch_ref[part, :].astype(f32), rows).astype(bf16)
        return carry

    by_rows(item_ref.shape[0], 256, items)


def centred(values):
    centre = values - jnp.mean(values, axis=-1, keepdims=True)
    spread = jnp.mean(centre * centre, axis=-1, keepdims=True)
    scale = lax.rsqrt(spread + norm_eps)
    return (centre * scale, scale)


def norm_back(grad, unit, scale, gain):
    inner = grad * gain
    return scale * (
        inner
        - jnp.mean(inner, axis=-1, keepdims=True)
        - unit * jnp.mean(inner * unit, axis=-1, keepdims=True)
    )


def total_of(values):
    return jnp.sum(values, axis=0, keepdims=True)


def places_of(seg):
    slots = seg.shape[0]
    lane = iota((slots, 128), 1)
    below = jnp.sum(jnp.where(seg < lane, 1.0, 0.0), axis=0, keepdims=True)
    start = jnp.sum(jnp.where(seg == lane, below, 0.0), axis=1, keepdims=True)
    return iota((slots, 1), 0) - start.astype(i32)


def small_rows(dense_ref, begin):
    return dense_ref[:, begin:].astype(f32).T


def mask_bias(seg, slots_q):
    shape = (seg.shape[0], slots_q.shape[1])
    slot = iota(shape, 0)
    wide = seg.astype(f32)
    seg_q = jnp.sum(jnp.where(slot == slots_q, wide, 0.0), axis=0, keepdims=True)
    return jnp.where((wide == seg_q) & (slot <= slots_q), 0.0, negative)


def prepare_kernel(
    seg_ref,
    slot_row_ref,
    slot_col_ref,
    dense_ref,
    freq_ref,
    logfreq_ref,
    pos_ref,
    pos_hot_t_ref,
    pos_q_ref,
    bias_ref,
    choose_ref,
    corr_ref,
):
    slots = seg_ref.shape[0]
    queries = slot_row_ref.shape[1]
    maxlen = pos_hot_t_ref.shape[0]
    pos = dense_ref[:, TABLES : TABLES + maxlen]
    seg = seg_ref[...]
    places = places_of(seg)
    pos_hot = hot(places == iota((slots, maxlen), 1))
    places_row = jnp.broadcast_to(places.astype(f32), (slots, 128)).T[:1]
    pos_hot_t_ref[...] = hot(places_row == iota((maxlen, slots), 0, f32))
    pos_ref[...] = dot_cols(pos_hot, pos)
    choose = hot(slot_col_ref[...] == iota((queries, slots), 1))
    choose_ref[...] = choose
    pos_q_ref[...] = dot(choose, pos_ref[...].astype(bf16))
    bias_ref[...] = mask_bias(seg, slot_row_ref[...])
    entries = logfreq_ref.shape[1]
    corr = dot(logfreq_ref[...], hot(iota((entries, queries), 0) == freq_ref[...]))
    corr_ref[...] = jnp.broadcast_to(corr, (META, queries)).astype(bf16)


def forward_kernel(
    item_ref,
    pos_ref,
    pos_q_ref,
    bias_ref,
    choose_ref,
    dense_ref,
    query_ref,
    first_ref,
    normed_ref,
    kv_ref,
    q_ref,
    mixed_ref,
    lse_ref,
    second_ref,
    normed_b_ref,
    active_ref,
    third_ref,
    value_t_ref,
    mixed_t_ref,
):
    small_at = dense_ref.shape[1] - SMALL
    rows = small_rows(dense_ref, small_at)
    first = item_ref[...].astype(f32) + pos_ref[...]
    first_ref[...] = first
    unit, unused = centred(first)
    normed_ref[...] = (unit * rows[0:1] + rows[1:2]).astype(bf16)
    normed = normed_ref[...]
    kv_ref[...] = dot(normed, dense_ref[:, D:QKV]).astype(bf16)
    choose = choose_ref[...]
    normed_q = dot(choose, normed).astype(bf16)
    q_ref[...] = dot(normed_q, dense_ref[:, :D]).astype(bf16)
    first_q = dot(choose, item_ref[...]) + pos_q_ref[...]
    value_t_ref[...] = kv_ref[:, D:].T

    def one_head(h, carry):
        own = iota((1, D), 1) // HEAD == h
        q_own = jnp.where(own, q_ref[...].astype(f32) * score_scale, 0.0).astype(bf16)
        scores = dot_cols(kv_ref[:, :D], q_own) + bias_ref[...]
        top = jnp.max(scores, axis=0, keepdims=True)
        weight = jnp.exp(scores - top)
        total = jnp.sum(weight, axis=0, keepdims=True)
        lse_ref[pl.ds(h, 1), :] = top + jnp.log(total)
        part = pl.ds(pl.multiple_of(h * HEAD, HEAD), HEAD)
        mixed_t_ref[part, :] = dot(value_t_ref[part, :], (weight * (1.0 / total)).astype(bf16))
        return carry

    lax.fori_loop(0, HEADS, one_head, 0)
    mixed = mixed_t_ref[...].T.astype(bf16)
    mixed_ref[...] = mixed
    second = first_q + dot(mixed, dense_ref[:, QKV:ATTN])
    second_ref[...] = second
    unit, unused = centred(second)
    normed_b = (unit * rows[2:3] + rows[3:4]).astype(bf16)
    normed_b_ref[...] = normed_b
    up_bias = jnp.concatenate([rows[7 + k : 8 + k] for k in range(FF // D)], axis=1)
    hidden = dot(normed_b, dense_ref[:, ATTN:DOWN]) + up_bias
    active = jnp.maximum(hidden, 0.0).astype(bf16)
    active_ref[...] = active
    third = second + dot_cols(active, dense_ref[:, DOWN:TABLES]) + rows[6:7]
    third_ref[...] = third
    unit, unused = centred(third)
    query_ref[...] = (unit * rows[4:5] + rows[5:6]).astype(bf16)


def columns_of(target_ref, queries):
    grps = target_ref.shape[0]
    return jnp.concatenate(
        [target_ref[g, queries : queries + 1, :].astype(f32) for g in range(grps)]
        + [jnp.zeros((128 - grps, queries), f32)],
        axis=0,
    ).T


def block_at(index, size):
    return pl.ds(pl.multiple_of(index * size, size), size)


def totals_kernel(
    where_ref,
    query_ref,
    target_ref,
    own_ref,
    valid_ref,
    *refs,
):
    out_refs, (tail_ref, target_t_ref, corr_ref, hold_ref) = refs[:-4], refs[-4:]
    owners = len(out_refs)
    height = tail_ref.shape[0]
    own_g, me = where_ref[0, 0], where_ref[0, 1]
    queries = query_ref.shape[0] // owners
    grps = target_ref.shape[0]
    corr_ref[...] = columns_of(target_ref, queries)

    for g in range(grps):
        target_t_ref[:, g * queries : (g + 1) * queries] = target_ref[g, :queries, :].T

    def one_owner(r):
        query = query_ref[block_at(me ^ r, queries), :].astype(f32)
        query = (query * logit_scale).astype(bf16)
        logits = [
            dot_cols(target_ref[g, :queries, :], query) - corr_ref[:, g : g + 1]
            for g in range(grps)
        ]
        top = functools.reduce(jnp.maximum, [jnp.max(x, axis=0, keepdims=True) for x in logits])
        total = jnp.zeros((1, queries), f32)
        mixed = jnp.zeros((D, queries), f32)
        for g in range(grps):
            weight = jnp.exp(logits[g] - top)
            total = total + jnp.sum(weight, axis=0, keepdims=True)
            mixed = mixed + dot(
                target_t_ref[:, g * queries : (g + 1) * queries], weight.astype(bf16)
            )
        return (top, total, mixed)

    tops, totals = [], []
    if grps > 8:

        def hold(r, carry):
            top, total, mixed = one_owner(r)
            hold_ref[r, :D, :] = mixed
            hold_ref[r, D : D + 8, :] = jnp.broadcast_to(top, (8, queries))
            hold_ref[r, D + 8 :, :] = jnp.broadcast_to(total, (8, queries))
            return carry

        lax.fori_loop(0, owners, hold, 0)
        for r in range(owners):
            out_refs[r][...] = hold_ref[r, :D, :].astype(bf16)
            tops.append(hold_ref[r, D : D + 1, :])
            totals.append(hold_ref[r, D + 8 : D + 9, :])
    else:
        for r in range(owners):
            top, total, mixed = one_owner(r)
            out_refs[r][...] = mixed.astype(bf16)
            tops.append(top)
            totals.append(total)

    product = own_ref[...].astype(f32) * target_ref[own_g, :queries, :].astype(f32)
    own = jnp.sum(product.T, axis=0, keepdims=True) * logit_scale
    own = own - target_ref[own_g, queries : queries + 1, :].astype(f32)
    pieces = [p for x in tops + totals + [own, valid_ref[...].astype(f32)] for p in split(x)]
    fill = jnp.zeros((height - len(pieces), queries), f32)
    tail_ref[...] = jnp.concatenate([x.astype(f32) for x in pieces] + [fill], axis=0).astype(bf16)


def piece(tail, k):
    return tail[3 * k : 3 * k + 1] + tail[3 * k + 1 : 3 * k + 2] + tail[3 * k + 2 : 3 * k + 3]


def backward_dense_kernel(
    owners,
    sums_ref,
    target_ref,
    valid_ref,
    total_ref,
    dense_ref,
    mixed_ref,
    second_ref,
    normed_b_ref,
    active_ref,
    third_ref,
    *refs,
):
    parts_refs = refs[:owners]
    grads_ref, proj_ref, grad_second_ref, grad_o_ref, columns_ref = refs[owners:]
    queries = valid_ref.shape[1]
    small_at = dense_ref.shape[1] - SMALL
    rows = small_rows(dense_ref, small_at)
    sums = sums_ref[...]
    tops = [sums[2 * r : 2 * r + 1] for r in range(owners)]
    totals = [sums[2 * r + 1 : 2 * r + 2] for r in range(owners)]
    top = functools.reduce(jnp.maximum, tops)
    scales = [jnp.exp(x - top) for x in tops]
    total = sum(x * y for x, y in zip(scales, totals))
    weight = valid_ref[...].astype(f32) / total_ref[0, 0]
    mean_t = jnp.zeros((D, queries), f32)
    for r in range(owners):
        mean_t = mean_t + parts_refs[r][...].astype(f32) * (scales[r] / total)
    target = target_ref[0, :queries, :].astype(f32)
    grad_query = ((mean_t - target.T) * (weight * logit_scale)).T

    unit, scale = centred(third_ref[...])
    grad_third = norm_back(grad_query, unit, scale, rows[4:5])
    gain_f, shift_f = total_of(grad_query * unit), total_of(grad_query)
    grad_f = grad_third.astype(bf16)
    active = active_ref[...]
    grads_ref[:, FF:] = dot(grad_f.T, active).astype(bf16)
    down_bias = total_of(grad_f.astype(f32))
    grad_active = dot(grad_f, dense_ref[:, DOWN:TABLES])
    grad_hidden = jnp.where(active.astype(f32) > 0.0, grad_active, 0.0).astype(bf16)
    grads_ref[:, :FF] = dot(normed_b_ref[...].T, grad_hidden).astype(bf16)
    up_bias = total_of(grad_hidden.astype(f32))
    grad_b = dot_cols(grad_hidden, dense_ref[:, ATTN:DOWN])
    unit, scale = centred(second_ref[...])
    grad_second = grad_third + norm_back(grad_b, unit, scale, rows[2:3])
    gain_b, shift_b = total_of(grad_b * unit), total_of(grad_b)
    grad_second_ref[...] = grad_second
    grad_y = grad_second.astype(bf16)
    proj_ref[...] = dot(mixed_ref[...].T, grad_y).astype(bf16)
    grad_o_ref[...] = dot_cols(grad_y, dense_ref[:, QKV:ATTN]).astype(bf16)
    columns = [gain_b, shift_b, gain_f, shift_f, down_bias]
    columns += [up_bias[:, k * D : (k + 1) * D] for k in range(FF // D)]
    columns_ref[...] = jnp.concatenate(
        columns + [jnp.zeros((META - len(columns), D), f32)], axis=0
    )


def backward_kernel(
    proj_ref,
    grad_second_ref,
    grad_o_ref,
    columns_ref,
    slot_row_ref,
    dense_ref,
    bias_ref,
    pos_hot_t_ref,
    first_ref,
    normed_t_ref,
    key_t_ref,
    kv_ref,
    q_ref,
    lse_ref,
    grad_first_ref,
    grads_ref,
    grad_q_t_ref,
    probs_ref,
    grad_s_ref,
    stack_ref,
    p_ref,
    dp_ref,
    joined_ref,
    grad_a_ref,
    base_ref,
    halves_ref,
):
    slots, queries = bias_ref.shape
    maxlen = pos_hot_t_ref.shape[0]
    small_at = dense_ref.shape[1] - SMALL
    rows = small_rows(dense_ref, small_at)

    def one_head(h, carry):
        own = iota((1, D), 1) // HEAD == h
        q_own = jnp.where(own, q_ref[...].astype(f32), 0.0)
        stack_ref[0, pl.ds(pl.multiple_of(h * queries, queries), queries), :] = q_own.astype(bf16)
        o_own = jnp.where(own, grad_o_ref[...].astype(f32), 0.0).astype(bf16)
        stack_ref[1, pl.ds(pl.multiple_of(h * queries, queries), queries), :] = o_own
        columns = pl.ds(pl.multiple_of(h * queries, queries), queries)
        scores = dot_cols(kv_ref[:, :D], (q_own * score_scale).astype(bf16)) + bias_ref[...]
        probs = jnp.exp(scores - lse_ref[pl.ds(h, 1), :])
        p_ref[...] = probs
        probs_ref[:, columns] = probs.astype(bf16)
        grad_p = dot_cols(kv_ref[:, D:], o_own)
        dp_ref[...] = grad_p
        inner = jnp.sum(p_ref[...] * grad_p, axis=0, keepdims=True)
        grad_s_ref[:, columns] = (p_ref[...] * (dp_ref[...] - inner)).astype(bf16)
        part = pl.ds(pl.multiple_of(h * HEAD, HEAD), HEAD)
        grad_q_t_ref[part, :] = dot(key_t_ref[part, :], grad_s_ref[:, columns])
        return carry

    lax.fori_loop(0, HEADS, one_head, 0)
    grad_q = (grad_q_t_ref[...].T * score_scale).astype(bf16)
    spread = hot(iota((slots, queries), 0) == slot_row_ref[...])
    joined_ref[:, :D] = dot(spread, grad_q).astype(bf16)
    joined_ref[:, D : 2 * D] = (dot(grad_s_ref[...], stack_ref[0]) * score_scale).astype(bf16)
    joined_ref[:, 2 * D :] = dot(probs_ref[...], stack_ref[1]).astype(bf16)
    grads_ref[:, :QKV] = dot(normed_t_ref[...], joined_ref[...]).astype(bf16)
    grads_ref[:, QKV:ATTN] = proj_ref[...]
    grad_a_ref[...] = dot_cols(joined_ref[...], dense_ref[:, :QKV])
    high, middle, unused = split(grad_second_ref[...])
    base_ref[...] = dot(spread, high) + dot(spread, middle)

    grad_a = grad_a_ref[...]
    unit, scale = centred(first_ref[...])
    grad_first = base_ref[...] + norm_back(grad_a, unit, scale, rows[0:1])
    grad_first_ref[...] = grad_first.astype(bf16)
    high, middle, unused = split(grad_first)
    halves_ref[:, :D] = high
    halves_ref[:, D:] = middle
    gain_a, shift_a = total_of(grad_a * unit), total_of(grad_a)
    both = dot(pos_hot_t_ref[...], halves_ref[...])
    grads_ref[:, ATTN : ATTN + maxlen] = (both[:, :D] + both[:, D:]).T.astype(bf16)
    columns = jnp.concatenate(
        [gain_a, shift_a, columns_ref[: NSMALL - 2]]
        + [jnp.zeros((SMALL - NSMALL, D), f32)],
        axis=0,
    )
    grads_ref[:, ATTN + maxlen :] = columns.T.astype(bf16)


def target_grad_kernel(owners, where_ref, total_ref, query_ref, target_ref, *refs):
    tail_refs, (out_ref, sums_ref, corr_ref) = refs[:owners], refs[owners:]
    grps = target_ref.shape[0]
    queries = query_ref.shape[0] // owners
    corr_ref[...] = columns_of(target_ref, queries)
    same = jnp.where(iota((queries, queries), 0) == iota((queries, queries), 1), 1.0, 0.0)
    own_g, me = where_ref[0, 0], where_ref[0, 1]
    tails = [ref[...].astype(f32) for ref in tail_refs]
    log_totals, weights = [], []
    loss = jnp.zeros((1, queries), f32)
    for r in range(owners):
        tops = [piece(tails[k], k ^ r) for k in range(owners)]
        totals = [piece(tails[k], owners + (k ^ r)) for k in range(owners)]
        top = functools.reduce(jnp.maximum, tops)
        total = functools.reduce(
            jnp.add, [totals[k] * jnp.exp(tops[k] - top) for k in range(owners)]
        )
        log_totals.append(top + jnp.log(total))
        weights.append(piece(tails[r], 2 * owners + 1) / total_ref[0, 0])
        loss = loss + weights[r] * (log_totals[r] - piece(tails[r], 2 * owners))
        if r == 0:
            sums_ref[...] = jnp.concatenate(
                [x for pair in zip(tops, totals) for x in pair], axis=0
            )
    loss = jnp.sum(loss, axis=1, keepdims=True)
    pieces = split(jnp.broadcast_to(loss, (1, queries)))
    tail = jnp.concatenate(
        [x.astype(f32) for x in pieces] + [jnp.zeros((META - len(pieces), queries), f32)], axis=0
    ).astype(bf16)
    for g in range(grps):
        target = target_ref[g, :queries, :]
        grad = jnp.zeros((queries, D), f32)
        for r in range(owners):
            query = query_ref[block_at(me ^ r, queries), :]
            logits = dot_cols(target, query) * logit_scale - corr_ref[:, g : g + 1]
            probs = jnp.exp(logits - log_totals[r])
            if r == 0:
                probs = probs - jnp.where(own_g == g, 1.0, 0.0) * same
            coeff = weights[r] * probs
            grad = grad + dot(coeff.astype(bf16), query)
        out_ref[g, :queries, :] = grad.astype(bf16)
        out_ref[g, queries:, :] = tail


def turn_kernel(normed_ref, kv_ref, normed_t_ref, key_t_ref):
    normed_t_ref[...] = normed_ref[...].T
    key_t_ref[...] = kv_ref[:, :D].T


def send_kernel(
    grad_first_ref, parts_ref, place_ref, sent_ref, both_ref, loss_ref
):
    grps, height, unused = parts_ref.shape
    slots = grad_first_ref.shape[0]
    queries = height - META
    both_ref[:slots, :] = grad_first_ref[...]
    total = parts_ref[0, :queries, :].astype(f32)
    for g in range(1, grps):
        total = total + parts_ref[g, :queries, :].astype(f32)
    both_ref[slots:, :] = (total * logit_scale).astype(bf16)
    loss = parts_ref[0, queries : queries + 8, :].astype(f32)
    for g in range(1, grps):
        loss = loss + parts_ref[g, queries : queries + 8, :].astype(f32)
    loss_ref[...] = jnp.sum(loss[:, :1], axis=0, keepdims=True)
    asks = both_ref.shape[0]
    block = block_of(sent_ref.shape[0], 2048)

    def one_block(i, carry):
        begin = pl.multiple_of(i * block, block)
        spread = hot(place_ref[...] - begin == iota((block, asks), 0))
        sent_ref[pl.ds(begin, block), :] = dot(spread, both_ref[...]).astype(bf16)
        return carry

    lax.fori_loop(0, sent_ref.shape[0] // block, one_block, 0)


def advance(weight, moment, average, grad, rate):
    moment_new = momentum_rate * moment + grad
    weight_new = weight - rate * (grad + momentum_rate * moment_new)
    average_new = average_rate * average + (1.0 - average_rate) * weight_new
    return (weight_new, moment_new, average_new, weight_new.astype(bf16))


def update_kernel(
    rate,
    rows,
    span_ref,
    ids_ref,
    recv_ref,
    extra_ref,
    w_ref,
    m_ref,
    a_ref,
    w_out_ref,
    m_out_ref,
    a_out_ref,
    copy_out_ref,
    w_held,
    m_held,
    a_held,
    copy_held,
    tiles_ref,
    grad_ref,
    in_sems,
    out_sems,
    extra_sem,
):
    count = w_ref.shape[0]
    devices, cap, unused = recv_ref.shape
    tiles = cap // 16
    edges = list(range(0, count, rows)) + [count]
    parts = [(k, edges[k], edges[k + 1] - edges[k]) for k in range(len(edges) - 1)]

    def copy_in(k, begin, size, j):
        source, target = ((w_ref, w_held), (m_ref, m_held), (a_ref, a_held))[j]
        part = pl.ds(begin, size)
        return pltpu.make_async_copy(source.at[part], target.at[part], in_sems.at[j, k])

    def copy_out(k, begin, size, j):
        pairs = (
            (w_held, w_out_ref),
            (m_held, m_out_ref),
            (a_held, a_out_ref),
            (copy_held, copy_out_ref),
        )
        source, target = pairs[j]
        part = pl.ds(begin, size)
        return pltpu.make_async_copy(source.at[part], target.at[part], out_sems.at[j, k])

    for part in parts:
        for j in range(3):
            copy_in(*part, j).start()
    for j in range(tiles):
        for n in range(devices):
            tiles_ref[j, 16 * n : 16 * (n + 1), :] = recv_ref[n, 16 * j : 16 * (j + 1), :]

    for k, begin, size in parts:
        here = pl.ds(0, size)
        grad_ref[here, :] = jnp.zeros((size, D), f32)

        @pl.when(span_ref[0] > 1)
        def start_from_extra():
            copy = pltpu.make_async_copy(
                extra_ref.at[pl.ds(begin, size)], grad_ref.at[here], extra_sem
            )
            copy.start()
            copy.wait()

        for j in range(tiles):

            @pl.when((span_ref[1 + 2 * j] < begin + size) & (span_ref[2 + 2 * j] >= begin))
            def add():
                spread = hot(ids_ref[j : j + 1, :] - begin == iota((size, ids_ref.shape[1]), 0))
                grad_ref[here, :] += dot(spread, tiles_ref[j])

        for j in range(3):
            copy_in(k, begin, size, j).wait()
        part = pl.ds(begin, size)
        new = advance(w_held[part, :], m_held[part, :], a_held[part, :], grad_ref[here, :], rate)
        w_held[part, :], m_held[part, :], a_held[part, :], copy_held[part, :] = new
        for j in range(4):
            copy_out(k, begin, size, j).start()
    for part in parts:
        for j in range(4):
            copy_out(*part, j).wait()


def update_table(span, ids, recv, extra, table_w, table_m, table_a, rate):
    count = table_w.shape[0]
    rows = min(1568, count)
    blocks = math.ceil(count / rows)
    devices, cap, unused = recv.shape
    anywhere = pl.BlockSpec(memory_space=pl.ANY)
    inside = pl.BlockSpec(memory_space=pltpu.VMEM)
    tables = [pltpu.with_memory_space_constraint(x, pltpu.HBM) for x in (table_w, table_m, table_a)]
    return tuple(
        pl.pallas_call(
            functools.partial(update_kernel, rate, rows),
            in_specs=[pl.BlockSpec(memory_space=pltpu.SMEM), inside, inside] + [anywhere] * 4,
            out_specs=[anywhere] * 4,
            scratch_shapes=[pltpu.VMEM((count, D), f32)] * 3
            + [
                pltpu.VMEM((count, D), bf16),
                pltpu.VMEM((cap // 16, 16 * devices, D), bf16),
                pltpu.VMEM((rows, D), f32),
                pltpu.SemaphoreType.DMA((3, blocks)),
                pltpu.SemaphoreType.DMA((4, blocks)),
                pltpu.SemaphoreType.DMA(()),
            ],
            out_shape=[jax.ShapeDtypeStruct((count, D), f32)] * 3
            + [jax.ShapeDtypeStruct((count, D), bf16)],
            compiler_params=pltpu.CompilerParams(vmem_limit_bytes=56 << 20),
            cost_estimate=pl.CostEstimate(
                flops=count * devices * cap * D, bytes_accessed=26 * count * D, transcendentals=0
            ),
        )(span, ids, recv, extra, *tables)
    )


def update_dense_kernel(rates, widths, parts_ref, *refs):
    ins, outs = refs[: 3 * len(widths)], refs[3 * len(widths) :]
    grad = parts_ref[0].astype(f32)
    for g in range(1, parts_ref.shape[0]):
        grad = grad + parts_ref[g].astype(f32)
    begin = 0
    for k, (rate, width) in enumerate(zip(rates, widths)):
        w_ref, m_ref, a_ref = ins[3 * k : 3 * k + 3]
        here = grad[:, begin : begin + width][:, : w_ref.shape[1]]
        new = advance(w_ref[...], m_ref[...], a_ref[...], here, rate)
        for j in range(4):
            outs[4 * k + j][...] = new[j]
        begin += width


def blank_kernel(seed_ref, out_ref):
    del seed_ref, out_ref


def blank_of(shape, dtype, seed):
    return pl.pallas_call(
        blank_kernel,
        out_shape=jax.ShapeDtypeStruct(shape, dtype),
        in_specs=[pl.BlockSpec(memory_space=pl.ANY)],
        out_specs=pl.BlockSpec(memory_space=pl.ANY),
    )(seed)


def everyone(values):
    return lax.all_to_all(values, ("grp", "row"), split_axis=0, concat_axis=0, tiled=True)


def swap(values, axis, bit):
    pairs = [(i, i ^ bit) for i in range(lax.axis_size(axis))]
    return lax.ppermute(values, axis, pairs)


def bits_of(size):
    return [1 << k for k in range(size.bit_length() - 1)]


def after(values, *others):
    return lax.optimization_barrier((values,) + others)[0]


def spread_row(values, bit):
    got = swap(values, "row", bit)
    mine = (lax.axis_index("row") // bit) % 2 == 0
    return jnp.stack([jnp.where(mine, values, got), jnp.where(mine, got, values)], axis=-3)


def sum_row(values, owners):
    for bit in bits_of(owners):
        grps, count, rows, width = values.shape
        pairs = values.reshape(grps, count // 2, 2, rows, width)
        mine = (lax.axis_index("row") // bit) % 2
        keep = lax.dynamic_index_in_dim(pairs, mine, 2, keepdims=False)
        give = lax.dynamic_index_in_dim(pairs, 1 - mine, 2, keepdims=False)
        values = (keep.astype(f32) + swap(give, "row", bit).astype(f32)).astype(bf16)
    return values.reshape(grps, rows, width)


def local(
    item_owner,
    item_row,
    seg,
    query_slot,
    tgt_owner,
    tgt_row,
    freq_idx,
    valid,
    logfreq,
    table_w,
    table_m,
    table_a,
    attn_w,
    attn_m,
    attn_a,
    ffn_w,
    ffn_m,
    ffn_a,
    pos_w,
    pos_m,
    pos_a,
    small_w,
    small_m,
    small_a,
):
    owners = lax.axis_size("row")
    grps = lax.axis_size("grp")
    devices = grps * owners
    local_rows = table_w.shape[0]
    slots = seg.shape[1]
    queries = query_slot.shape[1]
    asks = slots + queries
    total_q = queries * devices
    mean = 2 * asks // devices
    cap = 16 * math.ceil((mean + 3.5 * math.sqrt(mean)) / 16)
    width = 128 * math.ceil((cap + 3) / 128)
    maxlen = pos_w.shape[1]
    own_rows = attn_w.shape[0]
    my_grp, my_row = lax.axis_index("grp"), lax.axis_index("row")

    wanted, place, place_col, rank, dest, local_row = run(
        functools.partial(route_kernel, cap, local_rows, grps),
        [((devices, width), i32), ((1, asks), i32), ((asks, 1), i32)] + [((1, asks), i32)] * 3,
        [
            item_owner.reshape(1, slots),
            item_row,
            tgt_owner.reshape(1, queries),
            tgt_row,
            valid,
        ],
        flops=2 * devices * asks * asks,
    )
    asked = everyone(wanted)
    (dense,) = run(
        low_kernel,
        [((grps, own_rows, TABLES + maxlen + SMALL), bf16)],
        [attn_w, ffn_w, pos_w, after(small_w, wanted)],
        moved=1 << 20,
    )
    low_table, token = lower_table(after(table_w, wanted))
    dense, asked, token = lax.optimization_barrier((dense, asked, token))
    dense = lax.all_to_all(dense, "grp", split_axis=0, concat_axis=0, tiled=True)
    most = jnp.max(asked[:, cap + 1])
    rounds = (most + cap - 1) // cap
    valid_total = jnp.maximum(jnp.sum(asked[:, cap + 2]).astype(f32), 1.0).reshape(1, 1)
    (rows_found,) = run(
        functools.partial(lookup_kernel, cap, local_rows),
        [((devices, cap, D), bf16)],
        [asked, token, low_table],
        scratch=[pltpu.VMEM((16 * devices, 128), f32), pltpu.VMEM((16 * devices, D), f32)],
        moved=8 * local_rows * D,
        vmem=24,
    )
    dense, rows_found = lax.optimization_barrier((dense, rows_found))
    for bit in reversed(bits_of(owners)):
        dense = spread_row(dense, bit)
    dense = dense.reshape(D, -1)
    found = everyone(rows_found).reshape(devices * cap, D)
    ids = asked[:, :cap].reshape(devices, cap // 16, 16).transpose(1, 0, 2)
    ids = ids.reshape(cap // 16, 16 * devices)
    low_end = jnp.min(jnp.where(ids >= 0, ids, local_rows), axis=1)
    span = jnp.stack([low_end, jnp.max(ids, axis=1)], axis=1).reshape(-1)
    span = jnp.concatenate([rounds.reshape(1), span])

    found, ids, span = lax.optimization_barrier((found, ids, span))
    seg_col = seg.reshape(slots, 1)
    slot_col = query_slot.reshape(queries, 1)
    pos_part, pos_hot_t, pos_q, bias, choose, corr = run(
        prepare_kernel,
        [
            ((slots, D), f32),
            ((maxlen, slots), bf16),
            ((queries, D), f32),
            ((slots, queries), f32),
            ((queries, slots), bf16),
            ((META, queries), bf16),
        ],
        [seg_col, query_slot, slot_col, dense, freq_idx, logfreq.reshape(1, -1)],
        flops=1 << 30,
    )
    found = after(found, pos_part)
    (target_emb,) = run(
        extract_targets_kernel,
        [((grps, queries + META, D), bf16)],
        [found, place_col, corr],
        flops=2 * devices * cap * queries * D,
    )
    def wanted_of(k):
        here = rank[0] // cap == k
        spot = jnp.where(here, dest[0] * cap + rank[0] - k * cap, devices * cap)
        ids = jnp.full((devices * cap,), -1, i32).at[spot].set(local_row[0], mode="drop")
        return here, spot, everyone(ids.reshape(devices, cap)).reshape(devices * cap)

    def more_rows(carry):
        k, items, targets = carry
        here, spot, ids = wanted_of(k)
        rows = jnp.where((ids >= 0)[:, None], table_w[jnp.maximum(ids, 0)], 0.0).astype(bf16)
        got = everyone(rows.reshape(devices, cap, D)).reshape(devices * cap, D)
        got = got[jnp.minimum(spot, devices * cap - 1)]
        items = jnp.where(here[:slots, None], got[:slots], items)
        top = jnp.where(here[None, slots:, None], got[None, slots:], targets[:, :queries])
        return (k + 1, items, targets.at[:, :queries].set(top))

    unused, patch, target_emb = lax.while_loop(
        lambda carry: carry[0] < rounds,
        more_rows,
        (jnp.int32(1), blank_of((slots, D), bf16, wanted), target_emb),
    )
    (item_emb,) = run(
        extract_items_kernel,
        [((slots, D), bf16)],
        [after(found, target_emb), place_col, patch],
        flops=2 * devices * cap * slots * D,
    )
    targets = lax.all_to_all(target_emb, "grp", split_axis=0, concat_axis=0, tiled=True)
    query_own, first, normed, kv, q_own, mixed_o, lse, second, normed_b, active, third = run(
        forward_kernel,
        [
            ((queries, D), bf16),
            ((slots, D), f32),
            ((slots, D), bf16),
            ((slots, 2 * D), bf16),
            ((queries, D), bf16),
            ((queries, D), bf16),
            ((HEADS, queries), f32),
            ((queries, D), f32),
            ((queries, D), bf16),
            ((queries, FF), bf16),
            ((queries, D), f32),
        ],
        [item_emb, pos_part, pos_q, bias, choose, dense],
        scratch=[
            pltpu.VMEM((D, slots), bf16),
            pltpu.VMEM((D, queries), f32),
        ],
        flops=6 << 30,
    )
    query_all = lax.all_gather(query_own, "row", axis=0, tiled=True)
    where = jnp.stack([my_grp, my_row]).astype(i32).reshape(1, 2)
    tall = 16 * math.ceil((6 * owners + 6) / 16)
    *mixed, tail = run(
        totals_kernel,
        [((D, queries), bf16)] * owners + [((tall, queries), bf16)],
        [where, query_all, targets, query_own, valid],
        smem=(0,),
        scratch=[
            pltpu.VMEM((D, grps * queries), bf16),
            pltpu.VMEM((queries, 128), f32),
            pltpu.VMEM((owners if grps > 8 else 1, D + META, queries), f32),
        ],
        flops=4 * owners * grps * queries * queries * D,
    )
    tails = [tail] + [swap(tail, "row", k) for k in range(1, owners)]
    mixed = [mixed[0]] + [swap(mixed[k], "row", k) for k in range(1, owners)]
    normed_t, key_t = run(turn_kernel, [((D, slots), bf16)] * 2, [normed, kv], moved=4 << 20)
    target_parts, sums = run(
        functools.partial(target_grad_kernel, owners),
        [((grps, queries + META, D), bf16), ((2 * owners, queries), f32)],
        [
            where,
            valid_total,
            query_all,
            targets,
        ]
        + tails,
        smem=(0, 1),
        scratch=[pltpu.VMEM((queries, 128), f32)],
        flops=4 * owners * grps * queries * queries * D,
    )
    target_parts, *mixed = lax.optimization_barrier((target_parts, *mixed))
    target_parts = lax.all_to_all(target_parts, "grp", split_axis=0, concat_axis=0, tiled=True)
    grads_ffn, grads_proj, grad_second, grad_o, columns = run(
        functools.partial(backward_dense_kernel, owners),
        [
            ((D, 2 * FF), bf16),
            ((D, D), bf16),
            ((queries, D), f32),
            ((queries, D), bf16),
            ((META, D), f32),
        ],
        [sums, target_emb, valid, valid_total, dense, mixed_o, second, normed_b]
        + [active, third]
        + mixed,
        smem=(3,),
        flops=1 << 30,
    )
    grads_ffn = sum_row(grads_ffn.reshape(grps, owners, own_rows, -1), owners)
    grad_first, grads = run(
        backward_kernel,
        [((slots, D), bf16), ((D, ATTN + maxlen + SMALL), bf16)],
        [grads_proj, grad_second, grad_o, columns, query_slot, dense, bias, pos_hot_t, first]
        + [normed_t, key_t, kv, q_own, lse],
        scratch=[
            pltpu.VMEM((D, queries), f32),
            pltpu.VMEM((slots, HEADS * queries), bf16),
            pltpu.VMEM((slots, HEADS * queries), bf16),
            pltpu.VMEM((2, HEADS * queries, D), bf16),
            pltpu.VMEM((slots, queries), f32),
            pltpu.VMEM((slots, queries), f32),
            pltpu.VMEM((slots, QKV), bf16),
            pltpu.VMEM((slots, D), f32),
            pltpu.VMEM((slots, D), f32),
            pltpu.VMEM((slots, 2 * D), bf16),
        ],
        flops=17 << 30,
    )

    sent, both, loss = run(
        send_kernel,
        [((devices * cap, D), bf16), ((asks, D), bf16), ((1, 1), f32)],
        [grad_first, target_parts, place],
        flops=2 * devices * cap * asks * D,
    )
    received = everyone(sent.reshape(devices, cap, D))
    grads = sum_row(grads.reshape(grps, owners, own_rows, -1), owners)
    grad_own = jnp.concatenate([grads_ffn, grads], axis=-1)
    grad_own, received = lax.optimization_barrier((grad_own, received))
    grad_own = lax.all_to_all(grad_own, "grp", split_axis=0, concat_axis=0, tiled=True)

    rate_table = 4.0 * total_q
    rate_dense = 0.25 * math.sqrt(total_q)
    rate_place = 2.0 * math.sqrt(total_q)
    blank = blank_of((local_rows, D), f32, wanted)

    def more_grads(carry):
        k, total = carry
        here, spot, more_ids = wanted_of(k)
        rows = jnp.zeros((devices * cap, D), bf16).at[spot].set(both, mode="drop")
        rows = everyone(rows.reshape(devices, cap, D)).reshape(devices * cap, D)
        spot = jnp.where(more_ids >= 0, more_ids, local_rows)
        total = jnp.where(k > 1, total, 0.0)
        return (k + 1, total.at[spot].add(rows.astype(f32), mode="drop"))

    unused, extra = lax.while_loop(
        lambda carry: carry[0] < rounds,
        more_grads,
        (jnp.int32(1), blank),
    )
    table_out = update_table(span, ids, received, extra, table_w, table_m, table_a, rate_table)
    held = [
        [ffn_w, ffn_m, ffn_a],
        [attn_w, attn_m, attn_a],
        [pos_w, pos_m, pos_a],
        [small_w, small_m, small_a],
    ]
    dense_out = run(
        functools.partial(
            update_dense_kernel,
            [rate_dense, rate_dense, rate_place, rate_dense],
            [2 * FF, ATTN, maxlen, SMALL],
        ),
        [(x.shape, dtype) for three in held for x, dtype in zip(three + three[:1], [f32] * 3 + [bf16])],
        [grad_own] + [x for three in held for x in three],
    )
    ffn_out, attn_out, pos_out, small_out = [tuple(dense_out[4 * k : 4 * k + 4]) for k in range(4)]
    return (loss.reshape(()),) + table_out + attn_out + ffn_out + pos_out + small_out


def solution(mesh):
    rows = P(("grp", "row"), None)
    table = P(("row", "grp"), None)
    ids = P(("grp", "row"), None, None)
    in_specs = (ids, rows, rows, rows, ids, rows, rows, rows, P()) + (table,) * 3 + (rows,) * 12
    out_specs = (P(),) + (table,) * 4 + (rows,) * 16
    return jax.shard_map(local, mesh=mesh, in_specs=in_specs, out_specs=out_specs, check_vma=False)
```
